32 devices in a mesh: dp: 8 (over z, x), mp: 4 (over y, core).
Axes of the slice: x: 2, y: 2, z: 4, core: 2. Of those that a mesh axis runs over, the one named last changes fastest.
Arguments:
- tokens: bfloat16 [16, 577, 1024], P('dp', None, 'mp'), may hold values from -32 to 32
- slot_flags: int32 [16], P('dp'), may hold values 0 or 1
- cotangent: bfloat16 [16, 577, 1024], P('dp', None, 'mp'), may hold values from -6 to 6
- attend_gain: bfloat16 [16, 64], P('mp', 'dp'), may hold values from 0.18 to 4.4
- attend_shift: bfloat16 [16, 64], P('mp', 'dp'), may hold values from -4 to 4
- input_weight: bfloat16 [1024, 3, 1024], P('dp', None, 'mp'), may hold values from -0.1875 to 0.1875
- input_bias: bfloat16 [2, 16, 64], P(None, 'mp', 'dp'), may hold values from -6 to 6
- output_weight: bfloat16 [1024, 1024], P('mp', 'dp'), may hold values from -0.5 to 0.5
- output_bias: bfloat16 [16, 64], P('mp', 'dp'), may hold values from -6 to 6
- dense_gain: bfloat16 [16, 64], P('mp', 'dp'), may hold values from 0.18 to 4.4
- dense_shift: bfloat16 [16, 64], P('mp', 'dp'), may hold values from -4 to 4
- up_weight: bfloat16 [1024, 4096], P('dp', 'mp'), may hold values from -0.1875 to 0.1875
- up_bias: bfloat16 [64, 64], P('mp', 'dp'), may hold values from -6 to 6
- down_weight: bfloat16 [4096, 1024], P('mp', 'dp'), may hold values from -0.09375 to 0.09375
- down_bias: bfloat16 [16, 64], P('mp', 'dp'), may hold values from -6 to 6
Outputs:
- layer_out: bfloat16 [16, 577, 1024], P('dp', None, 'mp')
- input_grad: float32 [16, 577, 1024], P('dp', None, 'mp')
- grad_attend_gain: float32 [16, 64], P('mp', 'dp')
- grad_attend_shift: float32 [16, 64], P('mp', 'dp')
- grad_input_weight: float32 [1024, 3, 1024], P('dp', None, 'mp')
- grad_input_bias: float32 [2, 16, 64], P(None, 'mp', 'dp')
- grad_output_weight: float32 [1024, 1024], P('mp', 'dp')
- grad_output_bias: float32 [16, 64], P('mp', 'dp')
- grad_dense_gain: float32 [16, 64], P('mp', 'dp')
- grad_dense_shift: float32 [16, 64], P('mp', 'dp')
- grad_up_weight: float32 [1024, 4096], P('dp', 'mp')
- grad_up_bias: float32 [64, 64], P('mp', 'dp')
- grad_down_weight: float32 [4096, 1024], P('mp', 'dp')
- grad_down_bias: float32 [16, 64], P('mp', 'dp')
The draws below stay inside these ranges and needn't reach their ends.
Inputs may be any that keep to these rules, and one draw needn't show every extreme that they name: `slot_flags`: 1 marks a filled image slot, 0 an empty one.
All inputs are finite; a program needn't handle non-finite values. No bound on the sum of `slot_flags` on one device may be relied on, other than what follows from the above.
Results may differ from the reference program's by a relative error of at most 0.022.
Values may be sent and summed in bfloat16 or wider, within the bound.
A program may use at most 128 MiB of HBM per device.

```python
import jax
import jax.numpy as jnp
from jax import lax

D = 1024
H = 16
HD = 64
FF = 4096
SEQ = 577
SLOTS = 16


def draw_tokens(key, part):
    key = jax.random.fold_in(key, 11)
    base_key, row_key, column_key, sign_key = jax.random.split(key, 4)
    base = jnp.clip(jax.random.normal(base_key, (SLOTS, SEQ, D), jnp.float32), -6.0, 6.0)
    offsets = jax.random.randint(row_key, (SLOTS, 1), 0, 32)
    marked_rows = jnp.arange(SEQ)[None, :] % 32 == offsets
    chosen = jax.random.permutation(column_key, D)[:4]
    marked_columns = jnp.any(jnp.arange(D)[:, None] == chosen[None, :], axis=1)
    signs = (jax.random.randint(sign_key, (D,), 0, 2) * 2 - 1).astype(jnp.float32)
    marked = marked_rows[:, :, None] & marked_columns[None, None, :]
    large_values = signs[None, None, :] * float(D // 32)
    return jnp.where(marked, large_values, base).astype(jnp.bfloat16)


def rising_gain(key, start_value, end_value, jitter):
    position = jnp.arange(D, dtype=jnp.float32) / float(D - 1)
    ramp = jnp.exp(jnp.log(start_value) + (jnp.log(end_value) - jnp.log(start_value)) * position)
    noise = jax.random.uniform(key, (D,), jnp.float32, 1.0 - jitter, 1.0 + jitter)
    return (ramp * noise).reshape(D // HD, HD)


def draw_attend_gain(key, part):
    key = jax.random.fold_in(key, 23)
    return rising_gain(key, 0.3, 3.0, 0.1).astype(jnp.bfloat16)


def draw_dense_gain(key, part):
    key = jax.random.fold_in(key, 37)
    return rising_gain(key, 0.3, 3.0, 0.1).astype(jnp.bfloat16)


def place_ends(drawn, key, least, high):
    longest = drawn.shape.index(max(drawn.shape))
    spots = []
    for shift in (0, 1):
        where = [jax.random.randint(jax.random.fold_in(key, axis), (), 0, length) for axis, length in enumerate(drawn.shape)]
        where[longest] = (where[longest] + shift) % drawn.shape[longest]
        spots.append(tuple(where))
    return drawn.at[spots[0]].set(least).at[spots[1]].set(high)


def steps_of(stream_key, extent, shards, low, top_value):
    gain, own = 1.0, jax.random.fold_in(stream_key, 6)
    for dim, shards_of in shards:
        draws = jnp.exp(jax.random.uniform(jax.random.fold_in(own, dim), (shards_of,), jnp.float32, low / len(shards), top_value / len(shards)))
        gain = gain * jnp.repeat(draws, extent[dim] // shards_of).reshape([-1 if axis == dim else 1 for axis in range(len(extent))])
    return gain


def gaussian(key, dims, width, reach, shards=(), kind=jnp.bfloat16):
    entries = width * jax.random.normal(key, dims, jnp.float32)
    if shards:
        entries = entries * steps_of(key, dims, shards, -0.22, 0.18)
    return jnp.clip(entries, -reach, reach).astype(kind)


def setup_inputs(seed: int = 0) -> dict:
    splits = jax.random.split(jax.random.key(seed), 16)
    tokens = draw_tokens(jax.random.fold_in(splits[15], 71), 0)
    slot_flags = place_ends((jax.random.randint(splits[1], (SLOTS,), 0, 8) < 7).astype(jnp.int32), jax.random.fold_in(splits[1], 1), 0, 1)
    cotangent = gaussian(splits[2], (SLOTS, SEQ, D), 1.0, 6.0, ((0, 8), (2, 4)))
    attend_gain = draw_attend_gain(jax.random.fold_in(splits[15], 71), 0)
    attend_shift = gaussian(splits[4], (D // HD, HD), 0.3, 4.0, ((0, 4), (1, 8)))
    input_weight = gaussian(splits[5], (D, 3, H * HD), D ** -0.5, 0.1875, ((0, 8), (2, 4)))
    input_bias = gaussian(splits[6], (2, H, HD), 0.5, 6.0, ((1, 4), (2, 8)))
    output_weight = gaussian(splits[7], (H * HD, D), (D // 8) ** -0.5, 0.5, ((0, 4), (1, 8)))
    output_bias = gaussian(splits[8], (D // HD, HD), 0.5, 6.0, ((0, 4), (1, 8)))
    dense_gain = draw_dense_gain(jax.random.fold_in(splits[15], 71), 0)
    dense_shift = gaussian(splits[10], (D // HD, HD), 0.3, 4.0, ((0, 4), (1, 8)))
    up_weight = gaussian(splits[11], (D, FF), D ** -0.5, 0.1875, ((0, 8), (1, 4)))
    up_bias = gaussian(splits[12], (FF // HD, HD), 0.5, 6.0, ((0, 4), (1, 8)))
    down_weight = gaussian(splits[13], (FF, D), FF ** -0.5, 0.09375, ((0, 4), (1, 8)))
    down_bias = gaussian(splits[14], (D // HD, HD), 0.5, 6.0, ((0, 4), (1, 8)))
    return {"tokens": tokens, "slot_flags": slot_flags, "cotangent": cotangent, "attend_gain": attend_gain, "attend_shift": attend_shift, "input_weight": input_weight, "input_bias": input_bias, "output_weight": output_weight, "output_bias": output_bias, "dense_gain": dense_gain, "dense_shift": dense_shift, "up_weight": up_weight, "up_bias": up_bias, "down_weight": down_weight, "down_bias": down_bias}


EPS = 1e-06

@jax.custom_vjp
def low(v):
    return lax.optimization_barrier(v.astype(jnp.bfloat16)).astype(jnp.float32)

@jax.custom_vjp
def low_back(v):
    return v

def low_keep(v):
    return (low(v), None)

def low_pass(kept, grad):
    return (grad,)

def back_keep(v):
    return (v, None)

def back_low(kept, grad):
    return (low(grad),)
low.defvjp(low_keep, low_pass)
low_back.defvjp(back_keep, back_low)

def highest(pattern, left_side, right_side):
    return jnp.einsum(pattern, left_side, right_side, precision=lax.Precision.HIGHEST)

def layer_norm(values, norm_gain, norm_shift):
    center = lax.optimization_barrier(jnp.mean(values, axis=-1, keepdims=True))
    square = lax.optimization_barrier(jnp.mean(values * values, axis=-1, keepdims=True))
    inverse = lax.rsqrt(square - center * center + EPS)
    return (values - center) * inverse * norm_gain + norm_shift

def one_slot(tokens, filled, params):
    attend_gain, attend_shift, input_weight, input_bias, output_weight, output_bias, dense_gain, dense_shift, up_weight, up_bias, down_weight, down_bias = params
    normed_one = low(layer_norm(tokens, attend_gain.reshape(D), attend_shift.reshape(D)))
    joint_rows = highest('sd,dtf->stf', normed_one, input_weight)
    bias_pair = input_bias.reshape(2, H * HD)
    bias_full = jnp.stack([bias_pair[0], jnp.zeros_like(bias_pair[0]), bias_pair[1]])
    joint_rows = low_back(low(joint_rows + bias_full)).reshape(SEQ, 3, H, HD)
    queries = joint_rows[:, 0]
    key_rows = joint_rows[:, 1]
    values = joint_rows[:, 2]
    scores = low_back(highest('qhd,khd->hqk', queries, key_rows) * HD ** (-0.5))
    largest = lax.optimization_barrier(jnp.max(scores, axis=-1, keepdims=True))
    exponent = jnp.exp(scores - largest)
    soft_weights = low(exponent / lax.optimization_barrier(jnp.sum(exponent, axis=-1, keepdims=True)))
    attended = highest('hqk,khd->qhd', soft_weights, values).reshape(SEQ, H * HD)
    attended = low_back(low(attended))
    branch = low_back(highest('sf,fd->sd', attended, output_weight) + output_bias.reshape(D))
    hidden = tokens + branch
    normed_two = low(layer_norm(hidden, dense_gain.reshape(D), dense_shift.reshape(D)))
    pre_active = low_back(highest('sd,df->sf', normed_two, up_weight) + up_bias.reshape(FF))
    active = low(jax.nn.gelu(pre_active, approximate=False))
    feed_out = low_back(highest('sf,fd->sd', active, down_weight) + down_bias.reshape(D))
    return filled * (hidden + feed_out)

def reference(tokens, slot_flags, cotangent, attend_gain, attend_shift, input_weight, input_bias, output_weight, output_bias, dense_gain, dense_shift, up_weight, up_bias, down_weight, down_bias):
    params = (attend_gain.astype(jnp.float32), attend_shift.astype(jnp.float32), input_weight.astype(jnp.float32), input_bias.astype(jnp.float32), output_weight.astype(jnp.float32), output_bias.astype(jnp.float32), dense_gain.astype(jnp.float32), dense_shift.astype(jnp.float32), up_weight.astype(jnp.float32), up_bias.astype(jnp.float32), down_weight.astype(jnp.float32), down_bias.astype(jnp.float32))
    token_rows = tokens.astype(jnp.float32)
    slot_fill = slot_flags.astype(jnp.float32)

    def forward(inputs, weights):

        def run_slot(record):
            return jax.checkpoint(one_slot)(record[0], record[1], weights)
        return lax.map(run_slot, (inputs, slot_fill))
    outputs, pullback = jax.vjp(forward, token_rows, params)
    input_grad, gradients = pullback(cotangent.astype(jnp.float32))
    return (outputs.astype(jnp.bfloat16), input_grad, gradients[0], gradients[1], gradients[2], gradients[3], gradients[4], gradients[5], gradients[6], gradients[7], gradients[8], gradients[9], gradients[10], gradients[11])
```

```python
import functools

import jax
import jax.numpy as jnp
from jax import lax
from jax.experimental import pallas as pl
from jax.experimental.pallas import tpu as pltpu
from jax.sharding import PartitionSpec as P

HD = 64
EPS = 1e-06
MESH = pl.DeviceIdType.MESH
BF = jnp.bfloat16
F32 = jnp.float32


def dot(left, right):
    return jnp.dot(left, right, preferred_element_type=F32)


def dot_nt(left, right):
    return lax.dot_general(left, right, (((1,), (1,)), ((), ())), preferred_element_type=F32)


def dot_tn(left, right):
    return lax.dot_general(left, right, (((0,), (0,)), ((), ())), preferred_element_type=F32)


class Ids:
    def __init__(self):
        self.count = 0

    def take(self, number):
        first = self.count
        self.count += number
        return first


class Sizes:
    def __init__(self, mesh, tokens, input_weight, up_weight):
        dp, mp = mesh.shape["dp"], mesh.shape["mp"]
        self.dp, self.mp = dp, mp
        self.A = 4 if dp % 4 == 0 else dp
        self.B = dp // self.A
        self.Y = mp // 2
        self.NS, self.SEQ, self.Dm = tokens.shape
        self.R = -(-self.SEQ // 32) * 32
        self.HR = self.R // 2
        self.ROWS = self.NS * self.R
        self.D = self.Dm * mp
        self.Dy = 2 * self.Dm
        self.RB = input_weight.shape[0]
        self.HW = input_weight.shape[2]
        self.NP = self.HW // 128
        self.F = up_weight.shape[1]
        self.VW = max(self.D, self.F, 2 * self.HW)
        self.cols = (3 * self.HW, self.HW, self.F, self.F)
        ids = Ids()
        A, B, Y, NS = self.A, self.B, self.Y, self.NS
        self.ag_r = [ids.take(A) for _ in range(4)]
        self.ag_l = [ids.take(A) for _ in range(4)]
        self.ag_x = [ids.take((B - 1) * A) for _ in range(4)]
        self.rs_r = [ids.take(A) for _ in range(4)]
        self.rs_l = [ids.take(A) for _ in range(4)]
        self.rs_x = [ids.take((B - 1) * A) for _ in range(4)]
        self.rows_c = [ids.take(1) for _ in range(2)]
        self.rows_y = [ids.take(Y) for _ in range(2)]
        self.rows_f = [ids.take(Y) for _ in range(2)]
        self.vec_ids = [[ids.take(n) for n in (A, B, 1, Y)] for _ in range(2)]
        self.slot_core = {
            name: [ids.take(1) for _ in range(NS)]
            for name in ("branch", "n2", "out", "lo", "gn2", "gb", "gn1", "ig")
        }
        self.slot_y = {
            name: [ids.take(Y) for _ in range(NS)] for name in ("branch", "out", "gn2", "gn1", "st")
        }
        self.local = ids.take(16)
        self.nsem = ids.count


SCRATCH = (
    "tokF", "feedF", "W0", "W1", "W2", "W3", "na", "q", "k", "v", "att", "csend", "cr1", "ysend", "yr1",
    "yrO", "hid", "n2", "gp", "cr2", "yr2", "gb", "gatt", "gj", "cr3", "yr3", "ebuf", "obuf", "stat", "statT",
    "statR", "ubuf", "lse", "G0", "G1", "G2", "G3", "RX0", "RX1", "RX2", "RX3", "ZL0", "ZL1", "ZL2", "ZL3",
    "ZR0", "ZR1", "ZR2", "ZR3", "vst", "vrA", "vrB", "vrC", "vrY", "acc", "gvl", "ss", "rs",
)
OPERANDS = (
    "tok", "feed", "w0", "w1", "w2", "w3", "vec", "lo", "ig", "o0", "o1", "o2", "o3", "gvec",
)


def scratch_shapes(z):
    A, B, Y, NS = z.A, z.B, z.Y, z.NS
    V = pltpu.VMEM
    half = (NS, z.HR, z.D)
    shapes = dict(
        tokF=V((z.ROWS, z.D), BF),
        feedF=V((z.ROWS, z.D), BF),
        na=V((z.ROWS, max(z.D, z.F)), BF),
        q=V((z.ROWS, z.HW), BF),
        k=V((z.ROWS, z.HW), BF),
        v=V((z.ROWS, z.HW), BF),
        att=V((z.ROWS, z.HW), BF),
        csend=V(half, BF),
        cr1=V(half, BF),
        ysend=V(half, BF),
        yr1=V((NS, Y - 1, z.HR, z.D), BF),
        yrO=V((NS, Y - 1, z.HR, z.Dy), BF),
        hid=V((NS * z.HR, z.D), F32),
        n2=V((z.ROWS, z.D), BF),
        gp=V((z.ROWS, z.F), BF),
        cr2=V(half, BF),
        yr2=V((NS, Y - 1, z.HR, z.D), BF),
        gb=V((z.ROWS, z.D), BF),
        gatt=V((z.R, z.HW), BF),
        gj=V((z.ROWS, 3 * z.HW), BF),
        cr3=V(half, BF),
        yr3=V((NS, Y - 1, z.HR, z.Dy), BF),
        ebuf=V((NS, z.HR, z.Dy), F32),
        obuf=V((NS, z.HR, z.Dy), BF),
        stat=V((z.HR, 128), F32),
        statT=V((NS, 8, z.HR), F32),
        statR=V((NS, Y - 1, 8, z.HR), F32),
        ubuf=V((z.R, min(512, z.F)), F32),
        lse=V((NS * 2 * z.NP, 1, z.R), F32),
        vst=V((2, 5, 8, z.VW), F32),
        vrA=V((2, A, 8, z.VW), F32),
        vrB=V((2, B, 8, z.VW), F32),
        vrC=V((2, 1, 8, z.VW), F32),
        vrY=V((2, Y, 8, z.VW), F32),
        acc=V((3, 8, z.D), F32),
        gvl=V((8, z.VW), F32),
        ss=pltpu.SemaphoreType.DMA((z.nsem,)),
        rs=pltpu.SemaphoreType.DMA((z.nsem,)),
    )
    for p, cols in enumerate(z.cols):
        shapes[f"W{p}"] = V((z.D, cols), BF)
        shapes[f"G{p}"] = V((z.D, cols), BF)
        shapes[f"RX{p}"] = V((max(B - 1, 1), A, z.RB, cols), BF)
        shapes[f"ZL{p}"] = V((A - 1, z.RB, cols), BF)
        shapes[f"ZR{p}"] = V((A - 1, z.RB, cols), BF)
    return [shapes[name] for name in SCRATCH]


def kernel(z, *refs):
    r = dict(zip(OPERANDS + SCRATCH, refs))
    A, B, Y, NS, R, HR, D, Dm, Dy, HW, F, RB = (
        z.A, z.B, z.Y, z.NS, z.R, z.HR, z.D, z.Dm, z.Dy, z.HW, z.F, z.RB,
    )
    ss, rs = r["ss"], r["rs"]
    dpi, mpi = lax.axis_index("dp"), lax.axis_index("mp")
    a, b = dpi // B, dpi % B
    y, c = mpi // 2, mpi % 2

    def dev(a=a, b=b, y=y, c=c):
        return (a * B + b, y * 2 + c)

    def rcopy(src, dst, i, device):
        return pltpu.make_async_remote_copy(
            src_ref=src, dst_ref=dst, send_sem=ss.at[i], recv_sem=rs.at[i],
            device_id=device, device_id_type=MESH,
        )

    def when(cond, f):
        if cond is True:
            f()
        elif cond is not False:
            pl.when(cond)(f)

    pending = []

    def send(copy, cond=True, late=True):
        when(cond, lambda: copy.start())
        if late:
            pending.append((cond, copy))
        return copy

    mate = dev(c=1 - c)

    def y_dev(dy):
        return dev(y=lax.rem(y + dy, Y))

    def b_dev(db):
        return dev(b=lax.rem(b + db, B))

    def a_dev(da):
        return dev(a=lax.rem(a + da, A))

    left, right = dev(a=jnp.maximum(a - 1, 0)), dev(a=jnp.minimum(a + 1, A - 1))

    def rows16(start, size):
        return pl.ds(pl.multiple_of(start, 16), size)

    def lanes(start, size):
        return pl.ds(pl.multiple_of(start, 128), size)

    def loop(n, f, unroll=1):
        def step(i, carry):
            f(i)
            return carry
        lax.fori_loop(0, n, step, 0, unroll=unroll)

    bar = pltpu.get_barrier_semaphore()
    friends = [mate] + [y_dev(i) for i in range(1, Y)] + [b_dev(i) for i in range(1, B)]
    friends += [a_dev(i) for i in range(1, A)]
    for friend in friends:
        pl.semaphore_signal(bar, inc=1, device_id=friend, device_id_type=MESH)
    pl.semaphore_wait(bar, len(friends))

    W = [r[f"W{p}"] for p in range(4)]
    wsh = [r[f"w{p}"] for p in range(4)]

    def wblock(p, blk):
        return W[p].at[rows16(blk * RB, RB)]

    def ag_out(p, src, blk_a, hop, go_right, go_left):
        blk = blk_a * B + b
        dst = wblock(p, blk)
        send(rcopy(src, dst, z.ag_r[p] + hop, right), go_right)
        send(rcopy(src, dst, z.ag_l[p] + hop, left), go_left)

    def ag_cross(p, src, blk_a, cond):
        dst = wblock(p, blk_a * B + b)
        for db in range(1, B):
            send(rcopy(src, dst, z.ag_x[p] + (db - 1) * A + blk_a, b_dev(db)), cond)

    def ag_start(p):
        own = wblock(p, dpi)
        local = pltpu.make_async_copy(wsh[p], own, ss.at[z.local + p])
        local.start()
        ag_out(p, wsh[p], a, 1, a < A - 1, a > 0)
        ag_cross(p, wsh[p], a, True)
        return local

    def ag_step(p, h):
        from_left = a >= h
        src_a = jnp.maximum(a - h, 0)
        src = wblock(p, src_a * B + b)

        def got_left():
            rcopy(src, src, z.ag_r[p] + h, right).wait_recv()
        when(from_left, got_left)
        if h < A - 1:
            send(rcopy(src, src, z.ag_r[p] + h + 1, right), from_left & (a < A - 1))
        ag_cross(p, src, src_a, from_left)
        from_right = a + h < A
        src_a2 = jnp.minimum(a + h, A - 1)
        src2 = wblock(p, src_a2 * B + b)

        def got_right():
            rcopy(src2, src2, z.ag_l[p] + h, left).wait_recv()
        when(from_right, got_right)
        if h < A - 1:
            send(rcopy(src2, src2, z.ag_l[p] + h + 1, left), from_right & (a > 0))
        ag_cross(p, src2, src_a2, from_right)

    def ag_done(p):
        for db in range(1, B):
            bs = lax.rem(b + B - db, B)
            for aa in range(A):
                blk = wblock(p, aa * B + bs)
                rcopy(blk, blk, z.ag_x[p] + (db - 1) * A + aa, mate).wait_recv()

    full = [r["tokF"], r["feedF"]]
    own_rows = [r["tok"], r["feed"]]

    def mblock(t, m):
        return full[t].at[:, lanes(m * Dm, Dm)]

    def rows_start(t):
        src = own_rows[t]
        local = pltpu.make_async_copy(src, mblock(t, mpi), ss.at[z.local + 4 + t])
        local.start()
        for dy in range(1, Y):
            send(rcopy(src, mblock(t, mpi), z.rows_y[t] + dy, y_dev(dy)))
        send(rcopy(src, mblock(t, mpi), z.rows_c[t], mate))
        return local

    def rows_relay(t):
        for dy in range(1, Y):
            blk = mblock(t, lax.rem(y + Y - dy, Y) * 2 + c)
            rcopy(blk, blk, z.rows_y[t] + dy, mate).wait_recv()
            send(rcopy(blk, blk, z.rows_f[t] + dy, mate))

    def rows_done(t):
        blk = mblock(t, y * 2 + 1 - c)
        rcopy(blk, blk, z.rows_c[t], mate).wait_recv()
        for dy in range(1, Y):
            blk = mblock(t, lax.rem(y + Y - dy, Y) * 2 + 1 - c)
            rcopy(blk, blk, z.rows_f[t] + dy, mate).wait_recv()

    vst = r["vst"]
    vr = (r["vrA"], r["vrB"], r["vrC"], r["vrY"])
    groups = (A, B, 2, Y)

    def vec_peer(stage, d):
        return (a_dev, b_dev, lambda _: mate, y_dev)[stage](d)

    def vec_send(use, stage):
        for d in range(1, groups[stage]):
            slot = d - 1
            send(rcopy(vst.at[use, stage], vr[stage].at[use, slot], z.vec_ids[use][stage] + slot, vec_peer(stage, d)))

    def vec_add(use, stage):
        total = vst[use, stage]
        for d in range(1, groups[stage]):
            slot = d - 1
            dst = vr[stage].at[use, slot]
            rcopy(dst, dst, z.vec_ids[use][stage] + slot, mate).wait_recv()
            got = vr[stage][use, slot]
            if stage >= 2:
                got = jnp.where(lax.broadcasted_iota(jnp.int32, got.shape, 0) < 6, got, 0.0)
            total = total + got
        vst[use, stage + 1] = total

    def vector(row, cols=slice(None)):
        return vst[0, 4, row:row + 1, cols]

    waits = [rows_start(0), ag_start(0), ag_start(1)]
    vst[0, 0] = r["vec"][...]
    vec_send(0, 0)
    vec_add(0, 0)
    vec_send(0, 1)
    ag_step(0, 1)
    vec_add(0, 1)
    vec_send(0, 2)
    vec_add(0, 2)
    vec_send(0, 3)
    if A > 2:
        ag_step(0, 2)
    vec_add(0, 3)
    waits.append(ag_start(2))
    rows_relay(0)
    waits.append(rows_start(1))
    rows_done(0)
    waits.append(ag_start(3))
    for h in range(3, A):
        ag_step(0, h)
    for w in waits:
        w.wait()

    tokF, feedF, na, n2 = r["tokF"], r["feedF"], r["na"], r["n2"]

    def stats(x):
        mu = jnp.sum(x, axis=1, keepdims=True) * (1.0 / D)
        sq = jnp.sum(x * x, axis=1, keepdims=True) * (1.0 / D)
        return mu, lax.rsqrt(sq - mu * mu + EPS)

    def norm_one():
        gain, shift = vector(0, slice(0, D)), vector(1, slice(0, D))

        def step(i):
            rr = rows16(i * 32, 32)
            x = tokF[rr, :].astype(F32)
            mu, inv = stats(x)
            na[rr, :D] = ((x - mu) * inv * gain + shift).astype(BF)
        loop(z.ROWS // 32, step)

    norm_one()
    ag_done(0)

    ticks = []
    for p in (1, 2, 3):
        for h in range(1, A):
            ticks.append(functools.partial(ag_step, p, h))
        ticks.append(functools.partial(ag_done, p))

    def tick(n=1):
        for _ in range(n):
            if ticks:
                ticks.pop(0)()

    q, k, v, att, lse = r["q"], r["k"], r["v"], r["att"], r["lse"]

    def project(s):
        rr = slice(s * R, s * R + R)
        x = na[rr, :D]
        for third, ref in enumerate((q, k, v)):
            for j in range(0, HW, 256):
                w = min(256, HW - j)
                col = third * HW + j
                out = dot(x, W[0][:, col:col + w])
                if third == 0:
                    out = out + vst[0, 4, 7:8, j:j + w]
                if third == 2:
                    out = out + vst[0, 4, 7:8, HW + j:HW + j + w]
                out = out.astype(BF)
                if third == 0:
                    out = out * BF(HD ** -0.5)
                ref[rr, j:j + w] = out

    chunks = [(i, min(256, R - i)) for i in range(0, R, 256)]
    top = z.SEQ // 16 * 16

    def half_mask(x, e):
        lane = lax.broadcasted_iota(jnp.int32, x.shape, 1)
        return jnp.where((lane < HD) if e == 0 else (lane >= HD), x, jnp.zeros_like(x))

    def mask_keys(scores):
        row = lax.broadcasted_iota(jnp.int32, scores.shape, 0)
        return jnp.where(row < z.SEQ, scores, -1e30)

    def attend(s, pr):
        cc = lanes(pr * 128, 128)
        rr = slice(s * R, s * R + R)
        kp = k[rr, cc]
        vt = v[rr, cc].T
        for (c0, cw) in chunks:
            qp = q[s * R + c0:s * R + c0 + cw, cc]
            parts = []
            for e in range(2):
                sc = mask_keys(dot_nt(kp, half_mask(qp, e)))
                mx = jnp.max(sc, axis=0, keepdims=True)
                ex = jnp.exp(sc - mx)
                tot = jnp.sum(ex, axis=0, keepdims=True)
                soft = (ex * (1.0 / tot)).astype(BF)
                parts.append(dot(vt[e * HD:(e + 1) * HD], soft))
                lse[(s * z.NP + pr) * 2 + e, :, c0:c0 + cw] = mx + jnp.log(tot)
            out = jnp.concatenate(parts, axis=0)
            att[s * R + c0:s * R + c0 + cw, cc] = out.T.astype(BF)

    csend, ysend = r["csend"], r["ysend"]
    busy = {}

    def free(key):
        for copy in busy.pop(key, []):
            copy.wait_send()

    def own(s):
        return rows16(s * R + c * HR, HR)

    def theirs(s):
        return rows16(s * R + (1 - c) * HR, HR)

    def core_part(s, name, x, w, dst):
        free(("c", s))
        rows_x = x[theirs(s), :]

        def step(j):
            cols = lanes(j * 256, 256)
            csend[s, :, cols] = dot_nt(rows_x, w[pl.ds(pl.multiple_of(j * 256, 256), 256), :]).astype(BF)
        loop(D // 256, step)
        copy = rcopy(csend.at[s], dst.at[s], z.slot_core[name][s], mate)
        busy[("c", s)] = [send(copy, late=False)]

    def core_wait(s, name, dst):
        rcopy(dst.at[s], dst.at[s], z.slot_core[name][s], mate).wait_recv()

    def chip_part(s, name, x, w, got, dst):
        core_wait(s, name, got)
        free(("y", s))
        rows_x = x[own(s), :]

        def step(j):
            cols = lanes(j * 256, 256)
            part = dot_nt(rows_x, w[pl.ds(pl.multiple_of(j * 256, 256), 256), :])
            ysend[s, :, cols] = (part + got[s, :, cols].astype(F32)).astype(BF)
        loop(D // 256, step)
        busy[("y", s)] = [
            send(rcopy(ysend.at[s], dst.at[s, dy - 1], z.slot_y[name][s] + dy - 1, y_dev(dy)), late=False)
            for dy in range(1, Y)
        ]

    def chip_share(s, name, x, w, got, dst):
        core_wait(s, name, got)
        free(("y", s))
        rows_x = x[own(s), :]
        copies = []
        for dy in range(1, Y):
            first = lax.rem(y + dy, Y) * Dy
            part = dot_nt(rows_x, w[rows16(first, Dy), :]) + got[s, :, lanes(first, Dy)].astype(F32)
            span = slice((dy - 1) * Dy, dy * Dy)
            ysend[s, :, span] = part.astype(BF)
            copies.append(send(rcopy(
                ysend.at[s, :, span], dst.at[s, dy - 1], z.slot_y[name][s] + dy - 1, y_dev(dy)
            ), late=False))
        busy[("y", s)] = copies

    def y_wait(s, name, dst):
        for dy in range(1, Y):
            got = dst.at[s, dy - 1]
            rcopy(got, got, z.slot_y[name][s] + dy - 1, mate).wait_recv()

    def own_share(s, x, w, got, dst):
        first = y * Dy
        total = dot_nt(x[own(s), :], w[rows16(first, Dy), :]) + got[s, :, lanes(first, Dy)].astype(F32)
        for dy in range(1, Y):
            total = total + dst[s, dy - 1].astype(F32)
        return total

    hid = r["hid"]
    cr1, cr2, cr3, yr1, yr2, yr3, yrO = (r[n] for n in ("cr1", "cr2", "cr3", "yr1", "yr2", "yr3", "yrO"))

    def norm_two(s):
        y_wait(s, "branch", yr1)
        gain, shift, bias = vector(3, slice(0, D)), vector(4, slice(0, D)), vector(2, slice(0, D))

        def step(i):
            lr = rows16(i * 16, 16)
            h = ysend[s, lr, :].astype(F32)
            for dy in range(Y - 1):
                h = h + yr1[s, dy, lr, :].astype(F32)
            gr = rows16(s * R + c * HR + i * 16, 16)
            h = tokF[gr, :].astype(F32) + (h + bias)
            hid[rows16(s * HR + i * 16, 16), :] = h
            mu, inv = stats(h)
            n2[gr, :] = ((h - mu) * inv * gain + shift).astype(BF)
        loop(HR // 16, step)
        part = n2.at[own(s)]
        send(rcopy(part, part, z.slot_core["n2"][s], mate))
        yc = lanes(y * Dy, Dy)
        ebuf[s] = hid[s * HR:s * HR + HR, yc] + vst[0, 4, 5:6, yc]

    ubuf, gp = r["ubuf"], r["gp"]
    UC = min(512, F)
    root = 0.5 ** 0.5
    dens = (2.0 * 3.141592653589793) ** -0.5

    def up(s):
        part = n2.at[theirs(s)]
        rcopy(part, part, z.slot_core["n2"][s], mate).wait_recv()
        x = n2[s * R:s * R + R, :]

        def column(j):
            cols = lanes(j * UC, UC)
            ubuf[...] = dot(x, W[2][:, cols]) + vst[0, 4, 6:7, cols]

            def step(i):
                lr = rows16(i * 32, 32)
                gr = rows16(s * R + i * 32, 32)
                u = ubuf[lr, :]
                phi = 0.5 * lax.erf(u * root) + 0.5
                na[gr, cols] = (u * phi).astype(BF)
                gp[gr, cols] = (phi + u * (jnp.exp(-0.5 * u * u) * dens)).astype(BF)
            loop(R // 32, step)
        loop(F // UC, column)

    def back_up(s):
        x = feedF[s * R:s * R + R, :]

        def column(j):
            cols = lanes(j * 256, 256)
            ga = dot(x, W[3][:, cols])
            gp[s * R:s * R + R, cols] = (ga * gp[s * R:s * R + R, cols].astype(F32)).astype(BF)
        loop(F // 256, column)

    obuf, ebuf, lo, ig = r["obuf"], r["ebuf"], r["lo"], r["ig"]

    def layer_out(s):
        y_wait(s, "out", yrO)
        total = own_share(s, na_act, W[3], cr1, yrO)
        obuf[s] = (total + ebuf[s]).astype(BF)
        give_out(s, obuf, lo, "lo")

    def give_out(s, buf, out, name):
        out[own(s), :] = buf[s, :, lanes(c * Dm, Dm)]
        send(rcopy(buf.at[s, :, lanes((1 - c) * Dm, Dm)], out.at[own(s)], z.slot_core[name][s], mate))

    def take_out(s, out, name):
        dst = out.at[theirs(s)]
        rcopy(dst, dst, z.slot_core[name][s], mate).wait_recv()

    na_act = na.at[:, 0:F]
    gb, gatt, gj, acc, gvl = r["gb"], r["gatt"], r["gj"], r["acc"], r["gvl"]

    def norm_two_back(s):
        y_wait(s, "gn2", yr2)
        gain = vector(3, slice(0, D))

        def step(i, sums):
            lr = rows16(i * 16, 16)
            e = ysend[s, lr, :].astype(F32)
            for dy in range(Y - 1):
                e = e + yr2[s, dy, lr, :].astype(F32)
            hr = rows16(s * HR + i * 16, 16)
            gr = rows16(s * R + c * HR + i * 16, 16)
            h = hid[hr, :]
            mu, inv = stats(h)
            xhat = (h - mu) * inv
            t = e * gain
            m1 = jnp.sum(t, axis=1, keepdims=True) * (1.0 / D)
            m2 = jnp.sum(t * xhat, axis=1, keepdims=True) * (1.0 / D)
            g = feedF[gr, :].astype(F32) + inv * (t - m1 - xhat * m2)
            hid[hr, :] = g
            g = g.astype(BF)
            gb[gr, :] = g
            g = g.astype(F32)
            ex = e * xhat
            fold = lambda m: m[0:8] + m[8:16]
            return (sums[0] + fold(ex), sums[1] + fold(e), sums[2] + fold(g))
        zero = jnp.zeros((8, D), F32)
        sums = lax.fori_loop(0, HR // 16, step, (zero, zero, zero))
        for i in range(3):
            acc[i] = sums[i] if s == 0 else acc[i] + sums[i]
        part = gb.at[own(s)]
        send(rcopy(part, part, z.slot_core["gb"][s], mate))

    def attend_back_start(s):
        part = gb.at[theirs(s)]
        rcopy(part, part, z.slot_core["gb"][s], mate).wait_recv()
        gatt[...] = dot(gb[s * R:s * R + R, :], W[1][...]).astype(BF)

    def attend_back(s, pr):
        cc = lanes(pr * 128, 128)
        rr = slice(s * R, s * R + R)
        kp = k[rr, cc]
        vp = v[rr, cc]
        kt = kp.T
        dk = jnp.zeros((R, 128), F32)
        dv = jnp.zeros((R, 128), F32)
        for (c0, cw) in chunks:
            qp = q[s * R + c0:s * R + c0 + cw, cc]
            go = gatt[c0:c0 + cw, cc]
            parts = []
            for e in range(2):
                qm, gm = half_mask(qp, e), half_mask(go, e)
                sc = mask_keys(dot_nt(kp, qm))
                soft = jnp.exp(sc - lse[(s * z.NP + pr) * 2 + e, :, c0:c0 + cw])
                dv = dv + dot(soft.astype(BF), gm)
                gs = dot_nt(vp, gm)
                delta = jnp.sum(gs * soft, axis=0, keepdims=True)
                ds = (soft * (gs - delta)).astype(BF)
                dk = dk + dot(ds, qm)
                parts.append(dot(kt[e * HD:(e + 1) * HD], ds))
            dq = jnp.concatenate(parts, axis=0) * (HD ** -0.5)
            gj[s * R + c0:s * R + c0 + cw, lanes(pr * 128, 128)] = dq.T.astype(BF)
        gj[rr, lanes(HW + pr * 128, 128)] = dk.astype(BF)
        gj[rr, lanes(2 * HW + pr * 128, 128)] = dv.astype(BF)

    stat, statT, statR = r["stat"], r["statT"], r["statR"]

    def norm_one_sums(s):
        y_wait(s, "gn1", yr3)
        ebuf[s] = own_share(s, gj, W[0], cr3, yr3)
        yc = lanes(y * Dy, Dy)
        gain = vector(0, yc)

        def step(i, sums):
            lr = rows16(i * 16, 16)
            gr = rows16(s * R + c * HR + i * 16, 16)
            mu, inv = stats(tokF[gr, :].astype(F32))
            xhat = (tokF[gr, yc].astype(F32) - mu) * inv
            e = ebuf[s, lr, :]
            t = e * gain
            s1 = jnp.sum(t, axis=1, keepdims=True)
            s2 = jnp.sum(t * xhat, axis=1, keepdims=True)
            lane = lax.broadcasted_iota(jnp.int32, (16, 128), 1)
            stat[lr, :] = jnp.where(lane == 0, s1, jnp.where(lane == 1, s2, 0.0))
            ex = e * xhat
            fold = lambda m: m[0:8] + m[8:16]
            return (sums[0] + fold(ex), sums[1] + fold(e))
        zero = jnp.zeros((8, Dy), F32)
        sums = lax.fori_loop(0, HR // 16, step, (zero, zero))
        for i in range(2):
            row = jnp.sum(sums[i], axis=0, keepdims=True)
            gvl[i:i + 1, yc] = row if s == 0 else gvl[i:i + 1, yc] + row
        statT[s] = stat[...].T[0:8]
        for dy in range(1, Y):
            send(rcopy(statT.at[s], statR.at[s, dy - 1], z.slot_y["st"][s] + dy - 1, y_dev(dy)))

    def norm_one_back(s):
        y_wait(s, "st", statR)
        total = statT[s]
        for dy in range(Y - 1):
            total = total + statR[s, dy]
        total = jnp.concatenate([total, jnp.zeros((120, HR), F32)], axis=0)
        stat[...] = total.T * (1.0 / D)
        yc = lanes(y * Dy, Dy)
        gain = vector(0, yc)

        def step(i):
            lr = rows16(i * 16, 16)
            gr = rows16(s * R + c * HR + i * 16, 16)
            mu, inv = stats(tokF[gr, :].astype(F32))
            xhat = (tokF[gr, yc].astype(F32) - mu) * inv
            t = ebuf[s, lr, :] * gain
            st = stat[lr, :]
            m1, m2 = st[:, 0:1], st[:, 1:2]
            g = hid[rows16(s * HR + i * 16, 16), yc]
            ebuf[s, lr, :] = g + inv * (t - m1 - xhat * m2)
        loop(HR // 16, step)
        give_out(s, ebuf, ig, "ig")

    G = [r[f"G{p}"] for p in range(4)]
    RX = [r[f"RX{p}"] for p in range(4)]
    ZL = [r[f"ZL{p}"] for p in range(4)]
    ZR = [r[f"ZR{p}"] for p in range(4)]
    outs = [r[f"o{p}"] for p in range(4)]

    def weight_grad(p, x, g):
        def step(i):
            rr = pl.ds(pl.multiple_of(i * 256, 256), 256)
            G[p][rr, :] = dot_tn(x[:, lanes(i * 256, 256)], g[...]).astype(BF)
        loop(D // 256, step)

    def gblock(p, blk):
        return rows16(blk * RB, RB)

    def rs_cross(p):
        for db in range(1, B):
            bd = lax.rem(b + db, B)
            for aa in range(A):
                send(rcopy(
                    G[p].at[gblock(p, aa * B + bd)], RX[p].at[db - 1, aa],
                    z.rs_x[p] + (db - 1) * A + aa, b_dev(db),
                ))

    def rs_add(p):
        for db in range(1, B):
            for aa in range(A):
                dst = RX[p].at[db - 1, aa]
                rcopy(dst, dst, z.rs_x[p] + (db - 1) * A + aa, mate).wait_recv()
        if B > 1:
            def step(aa):
                rr = gblock(p, aa * B + b)
                total = G[p][rr, :].astype(F32)
                for db in range(B - 1):
                    total = total + RX[p][db, aa].astype(F32)
                G[p][rr, :] = total.astype(BF)
            loop(A, step)

    def rs_line(p, n):
        def pass_on(dest, came, buf, sem, to, go):
            rr = gblock(p, dest * B + b)

            def add():
                dst = buf.at[n]
                rcopy(dst, dst, sem + n, mate).wait_recv()
                G[p][rr, :] = (G[p][rr, :].astype(F32) + buf[n].astype(F32)).astype(BF)
            when(go & came, add)
            send(rcopy(G[p].at[rr], buf.at[n], sem + n, to), go)
        dest = A - 1 - n
        pass_on(dest, a > 0, ZL[p], z.rs_r[p], right, a < dest)
        pass_on(n, a < A - 1, ZR[p], z.rs_l[p], left, a > n)

    def rs_done(p):
        outs[p][...] = G[p][gblock(p, dpi), :].astype(F32)

        def take(buf, sem, n):
            dst = buf.at[n]
            rcopy(dst, dst, sem + n, mate).wait_recv()
            outs[p][...] += buf[n].astype(F32)
        when(a > 0, lambda: take(ZL[p], z.rs_r[p], jnp.clip(A - 1 - a, 0, A - 2)))
        when(a < A - 1, lambda: take(ZR[p], z.rs_l[p], jnp.clip(a, 0, A - 2)))

    def rs_ticks(p):
        ticks.append(functools.partial(rs_add, p))
        for n in range(A - 1):
            ticks.append(functools.partial(rs_line, p, n))
        ticks.append(functools.partial(rs_done, p))

    for s in range(NS):
        project(s)
        tick(1)
        loop(z.NP, functools.partial(attend, s))
        tick(3 if s == 0 else 1)
        core_part(s, "branch", att, W[1], cr1)
        chip_part(s, "branch", att, W[1], cr1, yr1)
    rows_relay(1)
    rows_done(1)
    tick(1)
    while len(ticks) > A + 1:
        tick()
    tick(1)
    for s in range(NS):
        norm_two(s)
        tick(1)
        up(s)
    while ticks:
        tick()
    for s in range(NS):
        back_up(s)
        core_part(s, "gn2", gp, W[2], cr2)
    for s in range(NS):
        chip_part(s, "gn2", gp, W[2], cr2, yr2)
    weight_grad(3, feedF, na_act)
    rs_cross(3)
    weight_grad(2, n2, gp)
    rs_cross(2)
    rs_ticks(3)
    rs_ticks(2)
    gvl[...] = jnp.zeros_like(gvl)
    ones_row = jnp.ones((8, z.ROWS), BF)
    gvl[5:6, lanes(mpi * Dm, Dm)] = dot(ones_row, r["feed"][...])[0:1]
    gvl[6:7, 0:F] = dot(ones_row, gp[...])[0:1]
    for s in range(NS):
        core_part(s, "out", na_act, W[3], cr1)
    for s in range(NS):
        norm_two_back(s)
        chip_share(s, "out", na_act, W[3], cr1, yrO)
        tick(1)
        attend_back_start(s)
        tick(1)
        loop(z.NP, functools.partial(attend_back, s))
        tick(1)
        core_part(s, "gn1", gj, W[0], cr3)
        tick(1)
        chip_share(s, "gn1", gj, W[0], cr3, yr3)
    for s in range(NS):
        layer_out(s)
    norm_one()
    weight_grad(0, na.at[:, 0:D], gj)
    rs_cross(0)
    weight_grad(1, gb, att)
    rs_cross(1)
    rs_ticks(0)
    rs_ticks(1)
    gvl[7:8, 0:HW] = dot(ones_row, gj[:, 0:HW])[0:1]
    gvl[7:8, HW:2 * HW] = dot(ones_row, gj[:, 2 * HW:3 * HW])[0:1]
    yc = lanes(y * Dy, Dy)
    for row, i in ((3, 0), (4, 1), (2, 2)):
        gvl[row:row + 1, yc] = jnp.sum(acc[i, :, yc], axis=0, keepdims=True)
    for s in range(NS):
        norm_one_sums(s)
        tick(1)
    for s in range(NS):
        norm_one_back(s)
        tick(1)
    vst[1, 0] = gvl[...]
    vec_send(1, 0)
    tick(2)
    vec_add(1, 0)
    vec_send(1, 1)
    tick(1)
    vec_add(1, 1)
    vec_send(1, 2)
    tick(1)
    vec_add(1, 2)
    vec_send(1, 3)
    tick(1)
    vec_add(1, 3)
    r["gvec"][...] = vst[1, 4]
    while ticks:
        tick()
    for s in range(NS):
        take_out(s, lo, "lo")
        take_out(s, ig, "ig")
    for key in list(busy):
        free(key)
    for cond, copy in pending:
        when(cond, lambda copy=copy: copy.wait_send())


def body(mesh, tokens, slot_flags, cotangent, attend_gain, attend_shift, input_weight, input_bias,
         output_weight, output_bias, dense_gain, dense_shift, up_weight, up_bias, down_weight, down_bias):
    z = Sizes(mesh, tokens, input_weight, up_weight)
    dpi, mpi = lax.axis_index("dp"), lax.axis_index("mp")
    filled = slot_flags.astype(F32)[:, None, None]
    pad = ((0, 0), (0, z.R - z.SEQ), (0, 0))
    tok = jnp.pad(tokens, pad).reshape(z.ROWS, z.Dm)
    feed = jnp.pad((cotangent.astype(F32) * filled).astype(BF), pad).reshape(z.ROWS, z.Dm)
    hot_dp = (jnp.arange(z.dp) == dpi).astype(F32)
    hot_mp = (jnp.arange(z.mp) == mpi).astype(F32)
    wide = jnp.stack([attend_gain, attend_shift, output_bias, dense_gain, dense_shift, down_bias]).astype(F32)
    wide = wide[:, None, :, None, :] * hot_mp[:, None, None, None] * hot_dp[:, None]
    wide = wide.reshape(6, z.D)
    up_row = (up_bias.astype(F32)[:, None, :] * hot_dp[:, None]).reshape(1, z.F)
    in_row = (input_bias.astype(F32)[:, :, None, :] * hot_dp[:, None]).reshape(1, 2 * z.HW)
    rows = [jnp.pad(row, ((0, 0), (0, z.VW - row.shape[1]))) for row in (wide, up_row, in_row)]
    vec = jnp.concatenate(rows, axis=0)
    shapes = [
        jax.ShapeDtypeStruct((z.ROWS, z.Dm), BF),
        jax.ShapeDtypeStruct((z.ROWS, z.Dm), F32),
    ] + [jax.ShapeDtypeStruct((z.RB, n), F32) for n in z.cols] + [jax.ShapeDtypeStruct((8, z.VW), F32)]
    vmem = pl.BlockSpec(memory_space=pltpu.VMEM)
    lo, ig, g0, g1, g2, g3, gvec = pl.pallas_call(
        functools.partial(kernel, z),
        out_shape=shapes,
        in_specs=[vmem] * 7,
        out_specs=[vmem] * 7,
        scratch_shapes=scratch_shapes(z),
        compiler_params=pltpu.CompilerParams(
            collective_id=0, has_side_effects=True, vmem_limit_bytes=VMEM_LIMIT
        ),
        name="layer",
    )(
        tok, feed, input_weight.reshape(z.RB, 3 * z.HW), output_weight.T, up_weight, down_weight.T, vec
    )

    def own_part(row):
        part = row.reshape(z.mp, -1, z.dp, HD // z.dp)
        part = lax.dynamic_index_in_dim(part, mpi, 0, keepdims=False)
        return lax.dynamic_index_in_dim(part, dpi, 1, keepdims=False)

    def dp_part(row):
        part = row.reshape(-1, z.dp, HD // z.dp)
        return lax.dynamic_index_in_dim(part, dpi, 1, keepdims=False)

    layer_rows = (lo.reshape(z.NS, z.R, z.Dm)[:, :z.SEQ].astype(F32) * filled).astype(BF)
    input_grad = ig.reshape(z.NS, z.R, z.Dm)[:, :z.SEQ]
    d_rows = gvec[:6, :z.D]
    return (
        layer_rows,
        input_grad,
        own_part(d_rows[0]),
        own_part(d_rows[1]),
        g0.reshape(input_weight.shape),
        dp_part(gvec[7, :2 * z.HW]).reshape(input_bias.shape),
        g1.T,
        own_part(d_rows[2]),
        own_part(d_rows[3]),
        own_part(d_rows[4]),
        g2,
        dp_part(gvec[6, :z.F]),
        g3.T,
        own_part(d_rows[5]),
    )


VMEM_LIMIT = 63 * 2**20


def solution(mesh):
    rows = P("dp", None, "mp")
    vec = P("mp", "dp")
    pair = P(None, "mp", "dp")
    return jax.shard_map(
        functools.partial(body, mesh),
        mesh=mesh,
        in_specs=(rows, P("dp"), rows, vec, vec, rows, pair, vec, vec, vec, vec, P("dp", "mp"), vec, vec, vec),
        out_specs=(rows, rows, vec, vec, rows, pair, vec, vec, vec, vec, P("dp", "mp"), vec, vec, vec),
        check_vma=False,
    )
```

```python
import functools

import jax
import jax.numpy as jnp
from jax import lax
from jax.experimental import pallas as pl
from jax.experimental.pallas import tpu as pltpu
from jax.sharding import PartitionSpec as P

HD = 64
EPS = 1e-06
MESH = pl.DeviceIdType.MESH
BF = jnp.bfloat16
F32 = jnp.float32


def dot(left, right):
    return jnp.dot(left, right, preferred_element_type=F32)


def dot_nt(left, right):
    return lax.dot_general(left, right, (((1,), (1,)), ((), ())), preferred_element_type=F32)


def dot_tn(left, right):
    return lax.dot_general(left, right, (((0,), (0,)), ((), ())), preferred_element_type=F32)


class Ids:
    def __init__(self):
        self.count = 0

    def take(self, number):
        first = self.count
        self.count += number
        return first


class Sizes:
    def __init__(self, mesh, tokens, input_weight, up_weight):
        dp, mp = mesh.shape["dp"], mesh.shape["mp"]
        self.dp, self.mp = dp, mp
        self.A = 4 if dp % 4 == 0 else dp
        self.B = dp // self.A
        self.Y = mp // 2
        self.NS, self.SEQ, self.Dm = tokens.shape
        self.R = -(-self.SEQ // 32) * 32
        self.HR = self.R // 2
        self.ROWS = self.NS * self.R
        self.D = self.Dm * mp
        self.Dy = 2 * self.Dm
        self.RB = input_weight.shape[0]
        self.HW = input_weight.shape[2]
        self.NP = self.HW // 128
        self.F = up_weight.shape[1]
        self.VW = max(self.D, self.F, 2 * self.HW)
        self.cols = (3 * self.HW, self.HW, self.F, self.F)
        ids = Ids()
        A, B, Y, NS = self.A, self.B, self.Y, self.NS
        self.ag_r = [ids.take(A) for _ in range(4)]
        self.ag_l = [ids.take(A) for _ in range(4)]
        self.ag_x = [ids.take((B - 1) * A) for _ in range(4)]
        self.pieces = []
        for p, width in ((3, 512), (2, 512), (0, 256), (1, 256)):
            cols = self.cols[p]
            for first in range(0, cols, width):
                self.pieces.append((p, first, min(width, cols - first)))
        n = len(self.pieces)
        self.rs_r = [ids.take(A) for _ in range(n)]
        self.rs_l = [ids.take(A) for _ in range(n)]
        self.rs_x = [ids.take((B - 1) * A) for _ in range(n)]
        self.rows_c = [ids.take(1) for _ in range(2 * NS)]
        self.rows_y = [ids.take(Y) for _ in range(2 * NS)]
        self.rows_f = [ids.take(Y) for _ in range(2 * NS)]
        self.vec_ids = [[ids.take(n) for n in (A, B, 1, Y)] for _ in range(2)]
        self.slot_core = {
            name: [ids.take(1) for _ in range(NS)]
            for name in ("branch", "n2", "out", "lo", "gn2", "gb", "gn1", "ig")
        }
        self.slot_y = {
            name: [ids.take(Y) for _ in range(NS)] for name in ("branch", "out", "gn2", "gn1", "st")
        }
        self.local = ids.take(16)
        self.nsem = ids.count


SCRATCH = (
    "tokF", "feedF", "W0", "W1", "W2", "W3", "na", "q", "k", "v", "att", "csend", "cr1", "ysend", "yr1",
    "yrO", "hid", "n2", "gp", "cr2", "yr2", "gb", "gatt", "gj", "cr3", "yr3", "ebuf", "obuf", "stat", "statT",
    "statR", "ubuf", "lse", "G0", "G1", "G2", "G3", "RX0", "RX1", "RX2", "RX3", "ZL0", "ZL1", "ZL2", "ZL3",
    "ZR0", "ZR1", "ZR2", "ZR3", "vst", "vrA", "vrB", "vrC", "vrY", "acc", "gvl", "ss", "rs",
)
OPERANDS = (
    "tok", "feed", "w0", "w1", "w2", "w3", "vec", "lo", "ig", "o0", "o1", "o2", "o3", "gvec",
)


def scratch_shapes(z):
    A, B, Y, NS = z.A, z.B, z.Y, z.NS
    V = pltpu.VMEM
    half = (NS, z.HR, z.D)
    shapes = dict(
        tokF=V((z.ROWS, z.D), BF),
        feedF=V((z.ROWS, z.D), BF),
        na=V((z.ROWS, max(z.D, z.F)), BF),
        q=V((z.ROWS, z.HW), BF),
        k=V((z.ROWS, z.HW), BF),
        v=V((z.ROWS, z.HW), BF),
        att=V((z.ROWS, z.HW), BF),
        csend=V(half, BF),
        cr1=V(half, BF),
        ysend=V(half, BF),
        yr1=V((NS, Y - 1, z.HR, z.D), BF),
        yrO=V((NS, Y - 1, z.HR, z.Dy), BF),
        hid=V((NS * z.HR, z.D), F32),
        n2=V((z.ROWS, z.D), BF),
        gp=V((z.ROWS, z.F), BF),
        cr2=V(half, BF),
        yr2=V((NS, Y - 1, z.HR, z.D), BF),
        gb=V((z.ROWS, z.D), BF),
        gatt=V((z.R, z.HW), BF),
        gj=V((z.ROWS, 3 * z.HW), BF),
        cr3=V(half, BF),
        yr3=V((NS, Y - 1, z.HR, z.Dy), BF),
        ebuf=V((NS, z.HR, z.Dy), F32),
        obuf=V((NS, z.HR, z.Dy), BF),
        stat=V((z.HR, 128), F32),
        statT=V((NS, 8, z.HR), F32),
        statR=V((NS, Y - 1, 8, z.HR), F32),
        ubuf=V((z.R, min(512, z.F)), F32),
        lse=V((NS * 2 * z.NP, 1, z.R), F32),
        vst=V((2, 5, 8, z.VW), F32),
        vrA=V((2, A, 8, z.VW), F32),
        vrB=V((2, B, 8, z.VW), F32),
        vrC=V((2, 1, 8, z.VW), F32),
        vrY=V((2, Y, 8, z.VW), F32),
        acc=V((3, 8, z.D), F32),
        gvl=V((8, z.VW), F32),
        ss=pltpu.SemaphoreType.DMA((z.nsem,)),
        rs=pltpu.SemaphoreType.DMA((z.nsem,)),
    )
    for p, cols in enumerate(z.cols):
        shapes[f"W{p}"] = V((z.D, cols), BF)
        shapes[f"G{p}"] = V((z.D, cols), BF)
        shapes[f"RX{p}"] = V((max(B - 1, 1), A, z.RB, cols), BF)
        shapes[f"ZL{p}"] = V((A - 1, z.RB, cols), BF)
        shapes[f"ZR{p}"] = V((A - 1, z.RB, cols), BF)
    return [shapes[name] for name in SCRATCH]


def kernel(z, *refs):
    r = dict(zip(OPERANDS + SCRATCH, refs))
    A, B, Y, NS, R, HR, D, Dm, Dy, HW, F, RB = (
        z.A, z.B, z.Y, z.NS, z.R, z.HR, z.D, z.Dm, z.Dy, z.HW, z.F, z.RB,
    )
    ss, rs = r["ss"], r["rs"]
    dpi, mpi = lax.axis_index("dp"), lax.axis_index("mp")
    a, b = dpi // B, dpi % B
    y, c = mpi // 2, mpi % 2

    def dev(a=a, b=b, y=y, c=c):
        return (a * B + b, y * 2 + c)

    def rcopy(src, dst, i, device):
        return pltpu.make_async_remote_copy(
            src_ref=src, dst_ref=dst, send_sem=ss.at[i], recv_sem=rs.at[i],
            device_id=device, device_id_type=MESH,
        )

    def when(cond, f):
        if cond is True:
            f()
        elif cond is not False:
            pl.when(cond)(f)

    pending = []

    def send(copy, cond=True, late=True):
        when(cond, lambda: copy.start())
        if late:
            pending.append((cond, copy))
        return copy

    mate = dev(c=1 - c)

    def y_dev(dy):
        return dev(y=lax.rem(y + dy, Y))

    def b_dev(db):
        return dev(b=lax.rem(b + db, B))

    def a_dev(da):
        return dev(a=lax.rem(a + da, A))

    left, right = dev(a=jnp.maximum(a - 1, 0)), dev(a=jnp.minimum(a + 1, A - 1))

    def rows16(start, size):
        return pl.ds(pl.multiple_of(start, 16), size)

    def lanes(start, size):
        return pl.ds(pl.multiple_of(start, 128), size)

    def loop(n, f, unroll=1):
        def step(i, carry):
            f(i)
            return carry
        lax.fori_loop(0, n, step, 0, unroll=unroll)

    bar = pltpu.get_barrier_semaphore()
    friends = [mate] + [y_dev(i) for i in range(1, Y)] + [b_dev(i) for i in range(1, B)]
    friends += [a_dev(i) for i in range(1, A)]
    for friend in friends:
        pl.semaphore_signal(bar, inc=1, device_id=friend, device_id_type=MESH)
    pl.semaphore_wait(bar, len(friends))

    W = [r[f"W{p}"] for p in range(4)]
    wsh = [r[f"w{p}"] for p in range(4)]

    def wblock(p, blk):
        return W[p].at[rows16(blk * RB, RB)]

    def ag_out(p, src, blk_a, hop, go_right, go_left):
        blk = blk_a * B + b
        dst = wblock(p, blk)
        send(rcopy(src, dst, z.ag_r[p] + hop, right), go_right)
        send(rcopy(src, dst, z.ag_l[p] + hop, left), go_left)

    def ag_cross(p, src, blk_a, cond):
        dst = wblock(p, blk_a * B + b)
        for db in range(1, B):
            send(rcopy(src, dst, z.ag_x[p] + (db - 1) * A + blk_a, b_dev(db)), cond)

    def ag_start(p):
        own = wblock(p, dpi)
        local = pltpu.make_async_copy(wsh[p], own, ss.at[z.local + p])
        local.start()
        ag_out(p, wsh[p], a, 1, a < A - 1, a > 0)
        ag_cross(p, wsh[p], a, True)
        return local

    def ag_step(p, h):
        from_left = a >= h
        src_a = jnp.maximum(a - h, 0)
        src = wblock(p, src_a * B + b)

        def got_left():
            rcopy(src, src, z.ag_r[p] + h, right).wait_recv()
        when(from_left, got_left)
        if h < A - 1:
            send(rcopy(src, src, z.ag_r[p] + h + 1, right), from_left & (a < A - 1))
        ag_cross(p, src, src_a, from_left)
        from_right = a + h < A
        src_a2 = jnp.minimum(a + h, A - 1)
        src2 = wblock(p, src_a2 * B + b)

        def got_right():
            rcopy(src2, src2, z.ag_l[p] + h, left).wait_recv()
        when(from_right, got_right)
        if h < A - 1:
            send(rcopy(src2, src2, z.ag_l[p] + h + 1, left), from_right & (a > 0))
        ag_cross(p, src2, src_a2, from_right)

    def ag_done(p):
        for db in range(1, B):
            bs = lax.rem(b + B - db, B)
            for aa in range(A):
                blk = wblock(p, aa * B + bs)
                rcopy(blk, blk, z.ag_x[p] + (db - 1) * A + aa, mate).wait_recv()

    full = [r["tokF"], r["feedF"]]
    own_rows = [r["tok"], r["feed"]]

    rows_local = {}

    def mblock(t, m):
        return full[t // NS].at[pl.ds(t % NS * R, R), lanes(m * Dm, Dm)]

    def rows_start(t):
        src = own_rows[t // NS].at[pl.ds(t % NS * R, R)]
        rows_local[t] = pltpu.make_async_copy(src, mblock(t, mpi), ss.at[z.local + 4 + t])
        rows_local[t].start()
        for dy in range(1, Y):
            send(rcopy(src, mblock(t, mpi), z.rows_y[t] + dy, y_dev(dy)))
        send(rcopy(src, mblock(t, mpi), z.rows_c[t], mate))

    def rows_relay(t):
        for dy in range(1, Y):
            blk = mblock(t, lax.rem(y + Y - dy, Y) * 2 + c)
            rcopy(blk, blk, z.rows_y[t] + dy, mate).wait_recv()
            send(rcopy(blk, blk, z.rows_f[t] + dy, mate))

    def rows_done(t):
        rows_local[t].wait()
        blk = mblock(t, y * 2 + 1 - c)
        rcopy(blk, blk, z.rows_c[t], mate).wait_recv()
        for dy in range(1, Y):
            blk = mblock(t, lax.rem(y + Y - dy, Y) * 2 + 1 - c)
            rcopy(blk, blk, z.rows_f[t] + dy, mate).wait_recv()

    vst = r["vst"]
    vr = (r["vrA"], r["vrB"], r["vrC"], r["vrY"])
    groups = (A, B, 2, Y)

    def vec_peer(stage, d):
        return (a_dev, b_dev, lambda _: mate, y_dev)[stage](d)

    def vec_send(use, stage):
        for d in range(1, groups[stage]):
            slot = d - 1
            send(rcopy(vst.at[use, stage], vr[stage].at[use, slot], z.vec_ids[use][stage] + slot, vec_peer(stage, d)))

    def vec_add(use, stage):
        total = vst[use, stage]
        for d in range(1, groups[stage]):
            slot = d - 1
            dst = vr[stage].at[use, slot]
            rcopy(dst, dst, z.vec_ids[use][stage] + slot, mate).wait_recv()
            got = vr[stage][use, slot]
            if stage >= 2:
                got = jnp.where(lax.broadcasted_iota(jnp.int32, got.shape, 0) < 6, got, 0.0)
            total = total + got
        vst[use, stage + 1] = total

    def vector(row, cols=slice(None)):
        return vst[0, 4, row:row + 1, cols]

    tokF, feedF, na, n2 = r["tokF"], r["feedF"], r["na"], r["n2"]

    def stats(x):
        mu = jnp.sum(x, axis=1, keepdims=True) * (1.0 / D)
        sq = jnp.sum(x * x, axis=1, keepdims=True) * (1.0 / D)
        return mu, lax.rsqrt(sq - mu * mu + EPS)

    def norm_one(s, out):
        gain, shift = vector(0, slice(0, D)), vector(1, slice(0, D))

        def step(i):
            rr = rows16(s * R + i * 32, 32)
            x = tokF[rr, :].astype(F32)
            mu, inv = stats(x)
            out[rr, :D] = ((x - mu) * inv * gain + shift).astype(BF)
        loop(R // 32, step, True)

    ticks = []

    def tick(n=1):
        for _ in range(n):
            if ticks:
                for f in ticks.pop(0):
                    f()

    q, k, v, att, lse = r["q"], r["k"], r["v"], r["att"], r["lse"]

    def project(s):
        rr = slice(s * R, s * R + R)
        x = na[rr, :D]
        for third, ref in enumerate((q, k, v)):
            for j in range(0, HW, 256):
                w = min(256, HW - j)
                col = third * HW + j
                out = dot(x, W[0][:, col:col + w])
                if third == 0:
                    out = out + vst[0, 4, 7:8, j:j + w]
                if third == 2:
                    out = out + vst[0, 4, 7:8, HW + j:HW + j + w]
                out = out.astype(BF)
                if third == 0:
                    out = out * BF(HD ** -0.5)
                ref[rr, j:j + w] = out

    chunks = [(i, min(256, R - i)) for i in range(0, R, 256)]
    top = z.SEQ // 16 * 16

    def half_mask(x, e):
        lane = lax.broadcasted_iota(jnp.int32, x.shape, 1)
        return jnp.where((lane < HD) if e == 0 else (lane >= HD), x, jnp.zeros_like(x))

    def mask_keys(scores):
        row = lax.broadcasted_iota(jnp.int32, scores.shape, 0)
        return jnp.where(row < z.SEQ, scores, -1e30)

    def attend(s, pr):
        cc = lanes(pr * 128, 128)
        rr = slice(s * R, s * R + R)
        kp = k[rr, cc]
        vt = v[rr, cc].T
        for (c0, cw) in chunks:
            qp = q[s * R + c0:s * R + c0 + cw, cc]
            parts = []
            for e in range(2):
                sc = mask_keys(dot_nt(kp, half_mask(qp, e)))
                mx = jnp.max(sc, axis=0, keepdims=True)
                ex = jnp.exp(sc - mx)
                tot = jnp.sum(ex, axis=0, keepdims=True)
                soft = (ex * (1.0 / tot)).astype(BF)
                parts.append(dot(vt[e * HD:(e + 1) * HD], soft))
                lse[(s * z.NP + pr) * 2 + e, :, c0:c0 + cw] = mx + jnp.log(tot)
            out = jnp.concatenate(parts, axis=0)
            att[s * R + c0:s * R + c0 + cw, cc] = out.T.astype(BF)

    csend, ysend = r["csend"], r["ysend"]
    busy = {}

    def free(key):
        for copy in busy.pop(key, []):
            copy.wait_send()

    def own(s):
        return rows16(s * R + c * HR, HR)

    def theirs(s):
        return rows16(s * R + (1 - c) * HR, HR)

    def core_part(s, name, x, w, dst):
        free(("c", s))
        rows_x = x[theirs(s), :]

        def step(j):
            cols = lanes(j * 256, 256)
            csend[s, :, cols] = dot_nt(rows_x, w[pl.ds(pl.multiple_of(j * 256, 256), 256), :]).astype(BF)
        loop(D // 256, step)
        copy = rcopy(csend.at[s], dst.at[s], z.slot_core[name][s], mate)
        busy[("c", s)] = [send(copy, late=False)]

    def core_wait(s, name, dst):
        rcopy(dst.at[s], dst.at[s], z.slot_core[name][s], mate).wait_recv()

    def chip_part(s, name, x, w, got, dst):
        core_wait(s, name, got)
        free(("y", s))
        rows_x = x[own(s), :]

        def step(j):
            cols = lanes(j * 256, 256)
            part = dot_nt(rows_x, w[pl.ds(pl.multiple_of(j * 256, 256), 256), :])
            ysend[s, :, cols] = (part + got[s, :, cols].astype(F32)).astype(BF)
        loop(D // 256, step)
        busy[("y", s)] = [
            send(rcopy(ysend.at[s], dst.at[s, dy - 1], z.slot_y[name][s] + dy - 1, y_dev(dy)), late=False)
            for dy in range(1, Y)
        ]

    def chip_share(s, name, x, w, got, dst):
        core_wait(s, name, got)
        free(("y", s))
        rows_x = x[own(s), :]
        copies = []
        for dy in range(1, Y):
            first = lax.rem(y + dy, Y) * Dy
            part = dot_nt(rows_x, w[rows16(first, Dy), :]) + got[s, :, lanes(first, Dy)].astype(F32)
            span = slice((dy - 1) * Dy, dy * Dy)
            ysend[s, :, span] = part.astype(BF)
            copies.append(send(rcopy(
                ysend.at[s, :, span], dst.at[s, dy - 1], z.slot_y[name][s] + dy - 1, y_dev(dy)
            ), late=False))
        busy[("y", s)] = copies

    def y_wait(s, name, dst):
        for dy in range(1, Y):
            got = dst.at[s, dy - 1]
            rcopy(got, got, z.slot_y[name][s] + dy - 1, mate).wait_recv()

    def own_share(s, x, w, got, dst):
        first = y * Dy
        total = dot_nt(x[own(s), :], w[rows16(first, Dy), :]) + got[s, :, lanes(first, Dy)].astype(F32)
        for dy in range(1, Y):
            total = total + dst[s, dy - 1].astype(F32)
        return total

    hid = r["hid"]
    cr1, cr2, cr3, yr1, yr2, yr3, yrO = (r[n] for n in ("cr1", "cr2", "cr3", "yr1", "yr2", "yr3", "yrO"))

    def norm_two(s):
        y_wait(s, "branch", yr1)
        gain, shift, bias = vector(3, slice(0, D)), vector(4, slice(0, D)), vector(2, slice(0, D))

        def step(i):
            lr = rows16(i * 16, 16)
            h = ysend[s, lr, :].astype(F32)
            for dy in range(Y - 1):
                h = h + yr1[s, dy, lr, :].astype(F32)
            gr = rows16(s * R + c * HR + i * 16, 16)
            h = tokF[gr, :].astype(F32) + (h + bias)
            hid[rows16(s * HR + i * 16, 16), :] = h
            mu, inv = stats(h)
            n2[gr, :] = ((h - mu) * inv * gain + shift).astype(BF)
        loop(HR // 16, step, True)
        part = n2.at[own(s)]
        busy[("n", s)] = [send(rcopy(part, part, z.slot_core["n2"][s], mate), late=False)]
        yc = lanes(y * Dy, Dy)
        ebuf[s] = hid[s * HR:s * HR + HR, yc] + vst[0, 4, 5:6, yc]

    ubuf, gp = r["ubuf"], r["gp"]
    UC = min(512, F)
    root = 0.5 ** 0.5
    dens = (2.0 * 3.141592653589793) ** -0.5

    def up(s):
        part = n2.at[theirs(s)]
        rcopy(part, part, z.slot_core["n2"][s], mate).wait_recv()
        x = n2[s * R:s * R + R, :]

        def column(j):
            cols = lanes(j * UC, UC)
            ubuf[...] = dot(x, W[2][:, cols]) + vst[0, 4, 6:7, cols]

            def step(i):
                lr = rows16(i * 32, 32)
                gr = rows16(s * R + i * 32, 32)
                u = ubuf[lr, :]
                phi = 0.5 * lax.erf(u * root) + 0.5
                na[gr, cols] = (u * phi).astype(BF)
                gp[gr, cols] = (phi + u * (jnp.exp(-0.5 * u * u) * dens)).astype(BF)
            loop(R // 32, step)
        loop(F // UC, column)

    def back_up(s):
        x = feedF[s * R:s * R + R, :]

        def column(j):
            cols = lanes(j * 256, 256)
            ga = dot(x, W[3][:, cols])
            gp[s * R:s * R + R, cols] = (ga * gp[s * R:s * R + R, cols].astype(F32)).astype(BF)
        loop(F // 256, column)

    obuf, ebuf, lo, ig = r["obuf"], r["ebuf"], r["lo"], r["ig"]

    def layer_out(s):
        y_wait(s, "out", yrO)
        total = own_share(s, na_act, W[3], cr1, yrO)
        obuf[s] = (total + ebuf[s]).astype(BF)
        give_out(s, obuf, lo, "lo")

    def give_out(s, buf, out, name):
        out[own(s), :] = buf[s, :, lanes(c * Dm, Dm)]
        send(rcopy(buf.at[s, :, lanes((1 - c) * Dm, Dm)], out.at[own(s)], z.slot_core[name][s], mate))

    def take_out(s, out, name):
        dst = out.at[theirs(s)]
        rcopy(dst, dst, z.slot_core[name][s], mate).wait_recv()

    na_act = na.at[:, 0:F]
    gb, gatt, gj, acc, gvl = r["gb"], r["gatt"], r["gj"], r["acc"], r["gvl"]

    def norm_two_back(s):
        y_wait(s, "gn2", yr2)
        gain = vector(3, slice(0, D))

        def step(i, sums):
            lr = rows16(i * 16, 16)
            e = ysend[s, lr, :].astype(F32)
            for dy in range(Y - 1):
                e = e + yr2[s, dy, lr, :].astype(F32)
            hr = rows16(s * HR + i * 16, 16)
            gr = rows16(s * R + c * HR + i * 16, 16)
            h = hid[hr, :]
            mu, inv = stats(h)
            xhat = (h - mu) * inv
            t = e * gain
            m1 = jnp.sum(t, axis=1, keepdims=True) * (1.0 / D)
            m2 = jnp.sum(t * xhat, axis=1, keepdims=True) * (1.0 / D)
            g = feedF[gr, :].astype(F32) + inv * (t - m1 - xhat * m2)
            hid[hr, :] = g
            g = g.astype(BF)
            gb[gr, :] = g
            g = g.astype(F32)
            ex = e * xhat
            fold = lambda m: m[0:8] + m[8:16]
            return (sums[0] + fold(ex), sums[1] + fold(e), sums[2] + fold(g))
        zero = jnp.zeros((8, D), F32)
        sums = lax.fori_loop(0, HR // 16, step, (zero, zero, zero))
        for i in range(3):
            acc[i] = sums[i] if s == 0 else acc[i] + sums[i]
        part = gb.at[own(s)]
        send(rcopy(part, part, z.slot_core["gb"][s], mate))

    def attend_back_start(s):
        part = gb.at[theirs(s)]
        rcopy(part, part, z.slot_core["gb"][s], mate).wait_recv()
        gatt[...] = dot(gb[s * R:s * R + R, :], W[1][...]).astype(BF)

    def attend_back(s, pr):
        cc = lanes(pr * 128, 128)
        rr = slice(s * R, s * R + R)
        kp = k[rr, cc]
        vp = v[rr, cc]
        kt = kp.T
        dk = jnp.zeros((R, 128), F32)
        dv = jnp.zeros((R, 128), F32)
        for (c0, cw) in chunks:
            qp = q[s * R + c0:s * R + c0 + cw, cc]
            go = gatt[c0:c0 + cw, cc]
            parts = []
            for e in range(2):
                qm, gm = half_mask(qp, e), half_mask(go, e)
                sc = mask_keys(dot_nt(kp, qm))
                soft = jnp.exp(sc - lse[(s * z.NP + pr) * 2 + e, :, c0:c0 + cw])
                dv = dv + dot(soft.astype(BF), gm)
                gs = dot_nt(vp, gm)
                delta = jnp.sum(gs * soft, axis=0, keepdims=True)
                ds = (soft * (gs - delta)).astype(BF)
                dk = dk + dot(ds, qm)
                parts.append(dot(kt[e * HD:(e + 1) * HD], ds))
            dq = jnp.concatenate(parts, axis=0) * (HD ** -0.5)
            gj[s * R + c0:s * R + c0 + cw, lanes(pr * 128, 128)] = dq.T.astype(BF)
        gj[rr, lanes(HW + pr * 128, 128)] = dk.astype(BF)
        gj[rr, lanes(2 * HW + pr * 128, 128)] = dv.astype(BF)

    stat, statT, statR = r["stat"], r["statT"], r["statR"]

    def norm_one_sums(s):
        y_wait(s, "gn1", yr3)
        ebuf[s] = own_share(s, gj, W[0], cr3, yr3)
        yc = lanes(y * Dy, Dy)
        gain = vector(0, yc)

        def step(i, sums):
            lr = rows16(i * 16, 16)
            gr = rows16(s * R + c * HR + i * 16, 16)
            mu, inv = stats(tokF[gr, :].astype(F32))
            xhat = (tokF[gr, yc].astype(F32) - mu) * inv
            e = ebuf[s, lr, :]
            t = e * gain
            s1 = jnp.sum(t, axis=1, keepdims=True)
            s2 = jnp.sum(t * xhat, axis=1, keepdims=True)
            lane = lax.broadcasted_iota(jnp.int32, (16, 128), 1)
            stat[lr, :] = jnp.where(lane == 0, s1, jnp.where(lane == 1, s2, 0.0))
            ex = e * xhat
            fold = lambda m: m[0:8] + m[8:16]
            return (sums[0] + fold(ex), sums[1] + fold(e))
        zero = jnp.zeros((8, Dy), F32)
        sums = lax.fori_loop(0, HR // 16, step, (zero, zero))
        for i in range(2):
            row = jnp.sum(sums[i], axis=0, keepdims=True)
            gvl[i:i + 1, yc] = row if s == 0 else gvl[i:i + 1, yc] + row
        statT[s] = stat[...].T[0:8]
        for dy in range(1, Y):
            send(rcopy(statT.at[s], statR.at[s, dy - 1], z.slot_y["st"][s] + dy - 1, y_dev(dy)))

    def norm_one_back(s):
        y_wait(s, "st", statR)
        total = statT[s]
        for dy in range(Y - 1):
            total = total + statR[s, dy]
        total = jnp.concatenate([total, jnp.zeros((120, HR), F32)], axis=0)
        stat[...] = total.T * (1.0 / D)
        yc = lanes(y * Dy, Dy)
        gain = vector(0, yc)

        def step(i):
            lr = rows16(i * 16, 16)
            gr = rows16(s * R + c * HR + i * 16, 16)
            mu, inv = stats(tokF[gr, :].astype(F32))
            xhat = (tokF[gr, yc].astype(F32) - mu) * inv
            t = ebuf[s, lr, :] * gain
            st = stat[lr, :]
            m1, m2 = st[:, 0:1], st[:, 1:2]
            g = hid[rows16(s * HR + i * 16, 16), yc]
            ebuf[s, lr, :] = g + inv * (t - m1 - xhat * m2)
        loop(HR // 16, step, True)
        give_out(s, ebuf, ig, "ig")

    G = [r[f"G{p}"] for p in range(4)]
    RX = [r[f"RX{p}"] for p in range(4)]
    ZL = [r[f"ZL{p}"] for p in range(4)]
    ZR = [r[f"ZR{p}"] for p in range(4)]
    outs = [r[f"o{p}"] for p in range(4)]

    def weight_grad(p, x, g):
        def step(i):
            rr = pl.ds(pl.multiple_of(i * 256, 256), 256)
            G[p][rr, :] = dot_tn(x[:, lanes(i * 256, 256)], g[...]).astype(BF)
        loop(D // 256, step)

    def gblock(p, blk):
        return rows16(blk * RB, RB)

    def rs_cross(i):
        p, first, width = z.pieces[i]
        cols = pl.ds(first, width)
        for db in range(1, B):
            bd = lax.rem(b + db, B)
            for aa in range(A):
                send(rcopy(
                    G[p].at[gblock(p, aa * B + bd), cols], RX[p].at[db - 1, aa, :, cols],
                    z.rs_x[i] + (db - 1) * A + aa, b_dev(db),
                ))

    def rs_add(i):
        p, first, width = z.pieces[i]
        cols = pl.ds(first, width)
        for db in range(1, B):
            for aa in range(A):
                dst = RX[p].at[db - 1, aa, :, cols]
                rcopy(dst, dst, z.rs_x[i] + (db - 1) * A + aa, mate).wait_recv()
        if B > 1:
            def step(aa):
                rr = gblock(p, aa * B + b)
                total = G[p][rr, cols].astype(F32)
                for db in range(B - 1):
                    total = total + RX[p][db, aa, :, cols].astype(F32)
                G[p][rr, cols] = total.astype(BF)
            loop(A, step)

    def rs_line(i, t):
        p, first, width = z.pieces[i]
        cols = pl.ds(first, width)

        def pass_on(n, dest, came, buf, sem, to, go):
            n = jnp.clip(n, 0, A - 2)
            rr = gblock(p, jnp.clip(dest, 0, A - 1) * B + b)

            def add():
                dst = buf.at[n, :, cols]
                rcopy(dst, dst, sem + n, mate).wait_recv()
                G[p][rr, cols] = (G[p][rr, cols].astype(F32) + buf[n, :, cols].astype(F32)).astype(BF)
            when(go & came, add)
            send(rcopy(G[p].at[rr, cols], buf.at[n, :, cols], sem + n, to), go)
        n = t - a
        dest = A - 1 - n
        pass_on(n, dest, a > 0, ZL[p], z.rs_r[i], right, (n >= 0) & (a < dest))
        n = t - (A - 1 - a)
        pass_on(n, n, a < A - 1, ZR[p], z.rs_l[i], left, (n >= 0) & (a > n))

    def rs_done(i):
        p, first, width = z.pieces[i]
        cols = pl.ds(first, width)
        outs[p][:, cols] = G[p][gblock(p, dpi), cols].astype(F32)

        def take(buf, sem, n):
            dst = buf.at[n, :, cols]
            rcopy(dst, dst, sem + n, mate).wait_recv()
            outs[p][:, cols] += buf[n, :, cols].astype(F32)
        when(a > 0, lambda: take(ZL[p], z.rs_r[i], jnp.clip(A - 1 - a, 0, A - 2)))
        when(a < A - 1, lambda: take(ZR[p], z.rs_l[i], jnp.clip(a, 0, A - 2)))

    def rs_groups():
        groups = []
        count = len(z.pieces)
        for i in range(count + 2):
            first, second = [], []
            if 0 <= i - 1 < count:
                first.append(functools.partial(rs_line, i - 1, A - 2))
            if i < count:
                first.append(functools.partial(rs_add, i))
                for t in range(max(A - 2, 1) if A > 2 else A - 1):
                    (first if t == 0 else second).append(functools.partial(rs_line, i, t))
            if 0 <= i - 1 < count:
                second.append(functools.partial(rs_done, i - 1))
            groups += [first, second]
        return [g for g in groups if g]

    def cross_part(part):
        for i, piece in enumerate(z.pieces):
            if piece[0] == part:
                rs_cross(i)

    rows_start(0)
    waits = [ag_start(0), ag_start(1)]
    for t in range(1, NS):
        rows_start(t)
    vst[0, 0] = r["vec"][...]
    vec_send(0, 0)
    vec_add(0, 0)
    vec_send(0, 1)
    ag_step(0, 1)
    vec_add(0, 1)
    vec_send(0, 2)
    vec_add(0, 2)
    vec_send(0, 3)
    rows_relay(0)
    vec_add(0, 3)
    if A > 2:
        ag_step(0, 2)
    rows_done(0)
    norm_one(0, na)
    for t in range(1, NS):
        rows_relay(t)
    waits.append(ag_start(2))
    for t in range(NS, 2 * NS):
        rows_start(t)
    for h in range(3, A):
        ag_step(0, h)
    ag_step(1, 1)
    waits.append(ag_start(3))
    for t in range(1, NS):
        rows_done(t)
    norm_one(1, na)
    for h in range(2, A):
        ag_step(1, h)
    ag_done(0)
    for w in waits:
        w.wait()
    for h in range(1, A):
        if h == A - 1:
            ticks.append([functools.partial(ag_done, 1)])
        ticks.append([functools.partial(ag_step, 2, h)])
        ticks.append([functools.partial(ag_step, 3, h)])
    for s in range(NS):
        project(s)
        tick()
        for pr in range(z.NP):
            attend(s, pr)
            tick()
        if s == 0:
            while len(ticks) > 2:
                tick()
        core_part(s, "branch", att, W[1], cr1)
        chip_part(s, "branch", att, W[1], cr1, yr1)
    for t in range(NS, 2 * NS):
        rows_relay(t)
    while ticks:
        tick()
    for s in range(NS):
        norm_two(s)
        if s == 0:
            ag_done(2)
            for t in range(NS, 2 * NS):
                rows_done(t)
        up(s)
    weight_grad(3, feedF, na_act)
    cross_part(3)
    ag_done(3)
    for s in range(NS):
        back_up(s)
        core_part(s, "gn2", gp, W[2], cr2)
    for s in range(NS):
        chip_part(s, "gn2", gp, W[2], cr2, yr2)
    weight_grad(2, n2, gp)
    cross_part(2)
    ticks += rs_groups()
    gvl[...] = jnp.zeros_like(gvl)
    ones_row = jnp.ones((8, z.ROWS), BF)
    gvl[5:6, lanes(mpi * Dm, Dm)] = dot(ones_row, r["feed"][...])[0:1]
    gvl[6:7, 0:F] = dot(ones_row, gp[...])[0:1]
    for s in range(NS):
        core_part(s, "out", na_act, W[3], cr1)
    for s in range(NS):
        free(("n", s))
        norm_one(s, n2)
    tick()
    for s in range(NS):
        norm_two_back(s)
        tick()
        if s > 0:
            chip_share(s - 1, "gn1", gj, W[0], cr3, yr3)
        chip_share(s, "out", na_act, W[3], cr1, yrO)
        attend_back_start(s)
        if s == 0:
            tick()
        for pr in range(z.NP):
            attend_back(s, pr)
            if s == 0 or pr < z.NP - 1:
                tick()
        core_part(s, "gn1", gj, W[0], cr3)
    weight_grad(0, n2, gj)
    cross_part(0)
    chip_share(NS - 1, "gn1", gj, W[0], cr3, yr3)
    tick()
    weight_grad(1, gb, att)
    cross_part(1)
    for s in range(NS):
        layer_out(s)
    tick()
    gvl[7:8, 0:HW] = dot(ones_row, gj[:, 0:HW])[0:1]
    gvl[7:8, HW:2 * HW] = dot(ones_row, gj[:, 2 * HW:3 * HW])[0:1]
    yc = lanes(y * Dy, Dy)
    for row, i in ((3, 0), (4, 1), (2, 2)):
        gvl[row:row + 1, yc] = jnp.sum(acc[i, :, yc], axis=0, keepdims=True)
    for s in range(NS):
        norm_one_sums(s)
        tick()
    for s in range(NS):
        norm_one_back(s)
        tick()
    vst[1, 0] = gvl[...]
    for stage in range(4):
        vec_send(1, stage)
        tick()
        vec_add(1, stage)
    r["gvec"][...] = vst[1, 4]
    while ticks:
        tick()
    for s in range(NS):
        take_out(s, lo, "lo")
        take_out(s, ig, "ig")
    for key in list(busy):
        free(key)
    for cond, copy in pending:
        when(cond, lambda copy=copy: copy.wait_send())


def body(mesh, tokens, slot_flags, cotangent, attend_gain, attend_shift, input_weight, input_bias,
         output_weight, output_bias, dense_gain, dense_shift, up_weight, up_bias, down_weight, down_bias):
    z = Sizes(mesh, tokens, input_weight, up_weight)
    dpi, mpi = lax.axis_index("dp"), lax.axis_index("mp")
    filled = slot_flags.astype(F32)[:, None, None]
    pad = ((0, 0), (0, z.R - z.SEQ), (0, 0))
    tok = jnp.pad(tokens, pad).reshape(z.ROWS, z.Dm)
    feed = jnp.pad((cotangent.astype(F32) * filled).astype(BF), pad).reshape(z.ROWS, z.Dm)
    hot_dp = (jnp.arange(z.dp) == dpi).astype(F32)
    hot_mp = (jnp.arange(z.mp) == mpi).astype(F32)
    wide = jnp.stack([attend_gain, attend_shift, output_bias, dense_gain, dense_shift, down_bias]).astype(F32)
    wide = wide[:, None, :, None, :] * hot_mp[:, None, None, None] * hot_dp[:, None]
    wide = wide.reshape(6, z.D)
    up_row = (up_bias.astype(F32)[:, None, :] * hot_dp[:, None]).reshape(1, z.F)
    in_row = (input_bias.astype(F32)[:, :, None, :] * hot_dp[:, None]).reshape(1, 2 * z.HW)
    rows = [jnp.pad(row, ((0, 0), (0, z.VW - row.shape[1]))) for row in (wide, up_row, in_row)]
    vec = jnp.concatenate(rows, axis=0)
    shapes = [
        jax.ShapeDtypeStruct((z.ROWS, z.Dm), BF),
        jax.ShapeDtypeStruct((z.ROWS, z.Dm), F32),
    ] + [jax.ShapeDtypeStruct((z.RB, n), F32) for n in z.cols] + [jax.ShapeDtypeStruct((8, z.VW), F32)]
    vmem = pl.BlockSpec(memory_space=pltpu.VMEM)
    lo, ig, g0, g1, g2, g3, gvec = pl.pallas_call(
        functools.partial(kernel, z),
        out_shape=shapes,
        in_specs=[vmem] * 7,
        out_specs=[vmem] * 7,
        scratch_shapes=scratch_shapes(z),
        compiler_params=pltpu.CompilerParams(
            collective_id=0, has_side_effects=True, vmem_limit_bytes=VMEM_LIMIT
        ),
        name="layer",
    )(
        tok, feed, input_weight.reshape(z.RB, 3 * z.HW), output_weight.T, up_weight, down_weight.T, vec
    )

    def own_part(row):
        part = row.reshape(z.mp, -1, z.dp, HD // z.dp)
        part = lax.dynamic_index_in_dim(part, mpi, 0, keepdims=False)
        return lax.dynamic_index_in_dim(part, dpi, 1, keepdims=False)

    def dp_part(row):
        part = row.reshape(-1, z.dp, HD // z.dp)
        return lax.dynamic_index_in_dim(part, dpi, 1, keepdims=False)

    layer_rows = (lo.reshape(z.NS, z.R, z.Dm)[:, :z.SEQ].astype(F32) * filled).astype(BF)
    input_grad = ig.reshape(z.NS, z.R, z.Dm)[:, :z.SEQ]
    d_rows = gvec[:6, :z.D]
    return (
        layer_rows,
        input_grad,
        own_part(d_rows[0]),
        own_part(d_rows[1]),
        g0.reshape(input_weight.shape),
        dp_part(gvec[7, :2 * z.HW]).reshape(input_bias.shape),
        g1.T,
        own_part(d_rows[2]),
        own_part(d_rows[3]),
        own_part(d_rows[4]),
        g2,
        dp_part(gvec[6, :z.F]),
        g3.T,
        own_part(d_rows[5]),
    )


VMEM_LIMIT = 63 * 2**20


def solution(mesh):
    rows = P("dp", None, "mp")
    vec = P("mp", "dp")
    pair = P(None, "mp", "dp")
    return jax.shard_map(
        functools.partial(body, mesh),
        mesh=mesh,
        in_specs=(rows, P("dp"), rows, vec, vec, rows, pair, vec, vec, vec, vec, P("dp", "mp"), vec, vec, vec),
        out_specs=(rows, rows, vec, vec, rows, pair, vec, vec, vec, vec, P("dp", "mp"), vec, vec, vec),
        check_vma=False,
    )
```

```python
import functools

import jax
import jax.numpy as jnp
from jax import lax
from jax.experimental import pallas as pl
from jax.experimental.pallas import tpu as pltpu
from jax.sharding import PartitionSpec as P

HD = 64
EPS = 1e-06
MESH = pl.DeviceIdType.MESH
BF = jnp.bfloat16
F32 = jnp.float32


def dot(left, right):
    return jnp.dot(left, right, preferred_element_type=F32)


def dot_nt(left, right):
    return lax.dot_general(left, right, (((1,), (1,)), ((), ())), preferred_element_type=F32)


def dot_tn(left, right):
    return lax.dot_general(left, right, (((0,), (0,)), ((), ())), preferred_element_type=F32)


class Ids:
    def __init__(self):
        self.count = 0

    def take(self, number):
        first = self.count
        self.count += number
        return first


class Sizes:
    def __init__(self, mesh, tokens, input_weight, up_weight):
        dp, mp = mesh.shape["dp"], mesh.shape["mp"]
        self.dp, self.mp = dp, mp
        self.A = 4 if dp % 4 == 0 else dp
        self.B = dp // self.A
        self.Y = mp // 2
        self.NS, self.SEQ, self.Dm = tokens.shape
        self.R = -(-self.SEQ // 32) * 32
        self.HR = self.R // 2
        self.ROWS = self.NS * self.R
        self.D = self.Dm * mp
        self.Dy = 2 * self.Dm
        self.RB = input_weight.shape[0]
        self.HW = input_weight.shape[2]
        self.NP = self.HW // 128
        self.F = up_weight.shape[1]
        self.VW = max(self.D, self.F, 2 * self.HW)
        self.wide = HD // dp
        heads = self.D // mp // HD
        self.groups = [heads] * 6 + [self.F // HD, 2 * self.HW // HD]
        self.NR = sum(self.groups)
        self.cols = (3 * self.HW, self.HW, self.F, self.F)
        ids = Ids()
        A, B, Y, NS = self.A, self.B, self.Y, self.NS
        self.gathers = self.cut(((0, 256), (1, 256), (2, 512), (3, 512)))
        self.scatters = self.cut(((3, 512), (2, 512), (0, 256), (1, 256)))
        self.ag_z = [ids.take(6) for _ in self.gathers]
        self.ag_x = [ids.take((B - 1) * A) for _ in self.gathers]
        self.rs_z = [ids.take(A) for _ in self.scatters]
        self.rs_x = [ids.take((B - 1) * A) for _ in self.scatters]
        self.rows_c = [ids.take(1) for _ in range(2 * NS)]
        self.rows_y = [ids.take(Y) for _ in range(2 * NS)]
        self.rows_f = [ids.take(Y) for _ in range(2 * NS)]
        self.vec_ids = [[ids.take(n) for n in (A, B, 1, Y)] for _ in range(2)]
        self.slot_core = {
            name: [ids.take(1) for _ in range(NS)]
            for name in ("branch", "n2", "out", "lo", "gn2", "gb", "gn1", "ig")
        }
        self.slot_y = {
            name: [ids.take(Y) for _ in range(NS)] for name in ("branch", "out", "gn2", "gn1", "st")
        }
        self.nsem = ids.count

    def cut(self, widths):
        return [
            (p, first, min(width, self.cols[p] - first))
            for p, width in widths
            for first in range(0, self.cols[p], width)
        ]


SCRATCH = (
    "tokF", "feedF", "W0", "W1", "W2", "W3", "na", "q", "k", "v", "att", "csend", "cr1", "ysend", "ysO", "yr1",
    "yrO", "hid", "n2", "gp", "cr2", "yr2", "gb", "gatt", "gj", "cr3", "yr3", "ebuf", "obuf", "stat", "statT",
    "statR", "ubuf", "lse", "G0", "G1", "G2", "G3", "RX0", "RX1", "RX2", "RX3", "Z0", "Z1", "Z2", "Z3",
    "vst", "vrA", "vrB", "vrC", "vrY", "acc", "gvl", "prm", "big", "ss", "rs",
)
OPERANDS = (
    "tokens", "cot", "flags", "iw", "ow", "uw", "dw", "p0", "p1", "p2", "p3", "p4", "p5", "pu", "pi",
    "lo", "ig", "o0", "o1", "o2", "o3", "q0", "q1", "q2", "q3", "q4", "q5", "qu", "qi",
)


def scratch_shapes(z):
    A, B, Y, NS = z.A, z.B, z.Y, z.NS
    V = pltpu.VMEM
    half = (NS, z.HR, z.D)
    shapes = dict(
        tokF=V((z.ROWS, z.D), BF),
        feedF=V((z.ROWS, z.D), BF),
        na=V((z.ROWS, max(z.D, z.F)), BF),
        q=V((z.ROWS, z.HW), BF),
        k=V((z.ROWS, z.HW), BF),
        v=V((z.ROWS, z.HW), BF),
        att=V((z.ROWS, z.HW), BF),
        csend=V(half, BF),
        cr1=V(half, BF),
        ysend=V(half, BF),
        ysO=V((NS, z.HR, (Y - 1) * z.Dy), BF),
        yr1=V((NS, Y - 1, z.HR, z.D), BF),
        yrO=V((NS, Y - 1, z.HR, z.Dy), BF),
        hid=V((NS * z.HR, z.D), F32),
        n2=V((z.ROWS, z.D), BF),
        gp=V((z.ROWS, z.F), BF),
        cr2=V(half, BF),
        yr2=V((NS, Y - 1, z.HR, z.D), BF),
        gb=V((z.ROWS, z.D), BF),
        gatt=V((z.R, z.HW), BF),
        gj=V((z.ROWS, 3 * z.HW), BF),
        cr3=V(half, BF),
        yr3=V((NS, Y - 1, z.HR, z.Dy), BF),
        ebuf=V((NS, z.HR, z.Dy), F32),
        obuf=V((NS, z.HR, z.Dy), BF),
        stat=V((z.HR, 128), F32),
        statT=V((NS, 8, z.HR), F32),
        statR=V((NS, Y - 1, 8, z.HR), F32),
        ubuf=V((z.R, min(512, z.F)), F32),
        lse=V((NS * 2 * z.NP, 1, z.R), F32),
        vst=V((2, 5, 8, z.VW), F32),
        vrA=V((2, A, 8, z.VW), F32),
        vrB=V((2, B, 8, z.VW), F32),
        vrC=V((2, 1, 8, z.VW), F32),
        vrY=V((2, Y, 8, z.VW), F32),
        acc=V((3, 8, z.D), F32),
        gvl=V((8, z.VW), F32),
        prm=V((z.NR, 128), F32),
        big=V((z.NR, z.VW), F32),
        ss=pltpu.SemaphoreType.DMA((z.nsem,)),
        rs=pltpu.SemaphoreType.DMA((z.nsem,)),
    )
    for p, cols in enumerate(z.cols):
        shapes[f"W{p}"] = V((z.D, cols), BF)
        shapes[f"G{p}"] = V((z.D, cols), BF)
        shapes[f"RX{p}"] = V((max(B - 1, 1), A, z.RB, cols), BF)
        shapes[f"Z{p}"] = V((A - 1, z.RB, cols), BF)
    return [shapes[name] for name in SCRATCH]


def kernel(z, *refs):
    r = dict(zip(OPERANDS + SCRATCH, refs))
    A, B, Y, NS, R, HR, D, Dm, Dy, HW, F, RB = (
        z.A, z.B, z.Y, z.NS, z.R, z.HR, z.D, z.Dm, z.Dy, z.HW, z.F, z.RB,
    )
    ss, rs = r["ss"], r["rs"]
    dpi, mpi = lax.axis_index("dp"), lax.axis_index("mp")
    a, b = dpi // B, dpi % B
    y, c = mpi // 2, mpi % 2

    def dev(a=a, b=b, y=y, c=c):
        return (a * B + b, y * 2 + c)

    def rcopy(src, dst, i, device):
        return pltpu.make_async_remote_copy(
            src_ref=src, dst_ref=dst, send_sem=ss.at[i], recv_sem=rs.at[i],
            device_id=device, device_id_type=MESH,
        )

    def when(cond, f):
        if cond is True:
            f()
        elif cond is not False:
            pl.when(cond)(f)

    pending = []

    def send(copy, cond=True, late=True):
        when(cond, lambda: copy.start())
        if late:
            pending.append((cond, copy))
        return copy

    mate = dev(c=1 - c)

    def y_dev(dy):
        return dev(y=lax.rem(y + dy, Y))

    def b_dev(db):
        return dev(b=lax.rem(b + db, B))

    def a_dev(da):
        return dev(a=lax.rem(a + da, A))

    def rows16(start, size):
        return pl.ds(pl.multiple_of(start, 16), size)

    def lanes(start, size):
        return pl.ds(pl.multiple_of(start, 128), size)

    def loop(n, f, unroll=1):
        def step(i, carry):
            f(i)
            return carry
        lax.fori_loop(0, n, step, 0, unroll=unroll)

    bar = pltpu.get_barrier_semaphore()
    friends = [mate] + [y_dev(i) for i in range(1, Y)] + [b_dev(i) for i in range(1, B)]
    friends += [a_dev(i) for i in range(1, A)]
    for friend in friends:
        pl.semaphore_signal(bar, inc=1, device_id=friend, device_id_type=MESH)
    pl.semaphore_wait(bar, len(friends))

    W = [r[f"W{p}"] for p in range(4)]
    own_w = rows16(dpi * RB, RB)

    def place_weights(p):
        if p == 0:
            for t in range(3):
                W[0][own_w, t * HW:(t + 1) * HW] = r["iw"][t]
        elif p == 2:
            W[2][own_w, :] = r["uw"][...]
        else:
            W[p][own_w, :] = r["ow" if p == 1 else "dw"][...].T

    def wblock(p, blk, first, width):
        return W[p].at[rows16(blk * RB, RB), pl.ds(first, width)]

    def line_dev(step):
        return dev(a=jnp.clip(a + step, 0, A - 1))

    def ag_cross(i, src, blk_a, cond):
        p, first, width = z.gathers[i]
        dst = wblock(p, blk_a * B + b, first, width)
        for db in range(1, B):
            send(rcopy(src, dst, z.ag_x[i] + (db - 1) * A + blk_a, b_dev(db)), cond)

    def ag_start(i):
        p, first, width = z.gathers[i]
        own_block = src = wblock(p, dpi, first, width)
        ag_cross(i, src, a, True)
        send(rcopy(src, own_block, z.ag_z[i], line_dev(1)), a + 1 < A)
        send(rcopy(src, own_block, z.ag_z[i] + 1, line_dev(-1)), a >= 1)
        send(rcopy(src, own_block, z.ag_z[i] + 2, line_dev(2)), a + 2 < A)
        send(rcopy(src, own_block, z.ag_z[i] + 3, line_dev(-2)), a >= 2)

    def ag_take(i, kind, step, relay=None):
        p, first, width = z.gathers[i]
        there = (a + step >= 0) if step < 0 else (a + step < A)
        src_a = jnp.clip(a + step, 0, A - 1)
        blk = wblock(p, src_a * B + b, first, width)
        when(there, lambda: rcopy(blk, blk, z.ag_z[i] + kind, mate).wait_recv())
        if relay is not None:
            go = there & ((a + relay < A) if relay > 0 else (a + relay >= 0))
            send(rcopy(blk, blk, z.ag_z[i] + kind + 2, line_dev(relay)), go)
        ag_cross(i, blk, src_a, there)

    def ag_near(i):
        ag_take(i, 0, -1)
        ag_take(i, 1, 1)
        ag_take(i, 2, -2, 1)
        ag_take(i, 3, 2, -1)

    def ag_far(i):
        ag_take(i, 4, -3)
        ag_take(i, 5, 3)

    def ag_done(i):
        p, first, width = z.gathers[i]
        for db in range(1, B):
            bs = lax.rem(b + B - db, B)
            for aa in range(A):
                blk = wblock(p, aa * B + bs, first, width)
                rcopy(blk, blk, z.ag_x[i] + (db - 1) * A + aa, mate).wait_recv()

    def of_part(p):
        return [i for i, piece in enumerate(z.gathers) if piece[0] == p]

    full = [r["tokF"], r["feedF"]]

    def place_rows(t):
        s = t % NS
        src = r["tokens"] if t < NS else r["cot"]
        keep = 1.0 if t < NS else r["flags"][s].astype(F32)
        cols = lanes(mpi * Dm, Dm)
        head = z.SEQ // 16 * 16
        full[t // NS][s * R:s * R + head, cols] = (src[s, 0:head, :].astype(F32) * keep).astype(BF)
        last = jnp.broadcast_to(src[s, head:z.SEQ, :].astype(F32) * keep, (R - head, Dm))
        row = lax.broadcasted_iota(jnp.int32, (R - head, Dm), 0)
        full[t // NS][s * R + head:s * R + R, cols] = jnp.where(row < z.SEQ - head, last, 0.0).astype(BF)

    def mblock(t, m):
        return full[t // NS].at[pl.ds(t % NS * R, R), lanes(m * Dm, Dm)]

    def rows_start(t):
        src = mblock(t, mpi)
        for dy in range(1, Y):
            send(rcopy(src, src, z.rows_y[t] + dy, y_dev(dy)))
        send(rcopy(src, src, z.rows_c[t], mate))

    def rows_relay(t):
        for dy in range(1, Y):
            blk = mblock(t, lax.rem(y + Y - dy, Y) * 2 + c)
            rcopy(blk, blk, z.rows_y[t] + dy, mate).wait_recv()
            send(rcopy(blk, blk, z.rows_f[t] + dy, mate))

    def rows_done(t):
        blk = mblock(t, y * 2 + 1 - c)
        rcopy(blk, blk, z.rows_c[t], mate).wait_recv()
        for dy in range(1, Y):
            blk = mblock(t, lax.rem(y + Y - dy, Y) * 2 + 1 - c)
            rcopy(blk, blk, z.rows_f[t] + dy, mate).wait_recv()

    vst = r["vst"]
    vr = (r["vrA"], r["vrB"], r["vrC"], r["vrY"])
    groups = (A, B, 2, Y)

    def vec_peer(stage, d):
        return (a_dev, b_dev, lambda _: mate, y_dev)[stage](d)

    def vec_send(use, stage):
        for d in range(1, groups[stage]):
            slot = d - 1
            send(rcopy(vst.at[use, stage], vr[stage].at[use, slot], z.vec_ids[use][stage] + slot, vec_peer(stage, d)))

    def vec_add(use, stage):
        total = vst[use, stage]
        for d in range(1, groups[stage]):
            slot = d - 1
            dst = vr[stage].at[use, slot]
            rcopy(dst, dst, z.vec_ids[use][stage] + slot, mate).wait_recv()
            got = vr[stage][use, slot]
            if stage >= 2:
                got = jnp.where(lax.broadcasted_iota(jnp.int32, got.shape, 0) < 6, got, 0.0)
            total = total + got
        vst[use, stage + 1] = total

    def spread():
        lane = lax.broadcasted_iota(jnp.int32, (128, z.VW), 1)
        j = lax.broadcasted_iota(jnp.int32, (128, z.VW), 0)
        return ((lane & (HD - 1)) - dpi * z.wide == j) & (j < z.wide)

    def heads_mask():
        row = lax.broadcasted_iota(jnp.int32, (z.NR, z.VW), 0)
        lane = lax.broadcasted_iota(jnp.int32, (z.NR, z.VW), 1)
        first, head = 0, row
        for p, n in enumerate(z.groups):
            base = mpi * n if p < 6 else 0
            head = jnp.where(row >= first, row - first + base, head)
            first += n
        return (lane >> 6) == head

    def small_in():
        prm = r["prm"]
        prm[...] = jnp.zeros_like(prm)
        first = 0
        for p in range(6):
            prm[first:first + z.groups[p], 0:z.wide] = r[f"p{p}"][...].astype(F32)
            first += z.groups[p]
        prm[first:first + z.groups[6], 0:z.wide] = r["pu"][...].astype(F32).T
        first += z.groups[6]
        for t in range(2):
            half = z.groups[7] // 2
            prm[first + t * half:first + (t + 1) * half, 0:z.wide] = r["pi"][t].astype(F32)
        rows = dot(prm[...].astype(BF), jnp.where(spread(), 1.0, 0.0).astype(BF))
        rows = jnp.where(heads_mask(), rows, 0.0).astype(BF)
        p = lax.broadcasted_iota(jnp.int32, (8, z.NR), 0)
        row = lax.broadcasted_iota(jnp.int32, (8, z.NR), 1)
        first, group = 0, jnp.zeros_like(row)
        for i, n in enumerate(z.groups):
            group = jnp.where(row >= first, i, group)
            first += n
        vst[0, 0] = dot(jnp.where(group == p, 1.0, 0.0).astype(BF), rows)

    def small_out(sums):
        big = r["big"]
        first = 0
        for p, n in enumerate(z.groups):
            big[first:first + n, :] = jnp.broadcast_to(sums[p:p + 1, :], (n, z.VW))
            first += n
        rows = jnp.where(heads_mask(), big[...], 0.0)
        r["prm"][...] = lax.dot_general(
            rows, jnp.where(spread(), 1.0, 0.0), (((1,), (1,)), ((), ())),
            precision=lax.Precision.HIGHEST, preferred_element_type=F32,
        )
        prm = r["prm"]
        first = 0
        for p in range(6):
            r[f"q{p}"][...] = prm[first:first + z.groups[p], 0:z.wide]
            first += z.groups[p]
        r["qu"][...] = prm[first:first + z.groups[6], :].T[0:z.wide]
        first += z.groups[6]
        half = z.groups[7] // 2
        for t in range(2):
            r["qi"][t] = prm[first + t * half:first + (t + 1) * half, 0:z.wide]

    def vector(row, cols=slice(None)):
        return vst[0, 4, row:row + 1, cols]

    tokF, feedF, na, n2 = r["tokF"], r["feedF"], r["na"], r["n2"]

    def stats(x):
        mu = jnp.sum(x, axis=1, keepdims=True) * (1.0 / D)
        sq = jnp.sum(x * x, axis=1, keepdims=True) * (1.0 / D)
        return mu, lax.rsqrt(sq - mu * mu + EPS)

    def norm_one(s, out):
        gain, shift = vector(0, slice(0, D)), vector(1, slice(0, D))

        def step(i):
            rr = rows16(s * R + i * 32, 32)
            x = tokF[rr, :].astype(F32)
            mu, inv = stats(x)
            out[rr, :D] = ((x - mu) * inv * gain + shift).astype(BF)
        loop(R // 32, step, True)

    ticks, waiting, flying = [], [], []

    def tick():
        if ticks and (ticks[0][0] is None or ticks[0][0] in flying):
            for f in ticks.pop(0)[1]:
                f()

    q, k, v, att, lse = r["q"], r["k"], r["v"], r["att"], r["lse"]

    def project(s):
        rr = slice(s * R, s * R + R)
        x = na[rr, :D]
        for third, ref in enumerate((q, k, v)):
            for j in range(0, HW, 256):
                w = min(256, HW - j)
                col = third * HW + j
                out = dot(x, W[0][:, col:col + w])
                if third == 0:
                    out = out + vst[0, 4, 7:8, j:j + w]
                if third == 2:
                    out = out + vst[0, 4, 7:8, HW + j:HW + j + w]
                out = out.astype(BF)
                if third == 0:
                    out = out * BF(HD ** -0.5)
                ref[rr, j:j + w] = out

    chunks = [(i, min(256, R - i)) for i in range(0, R, 256)]
    top = z.SEQ // 16 * 16

    def half_mask(x, e):
        lane = lax.broadcasted_iota(jnp.int32, x.shape, 1)
        return jnp.where((lane < HD) if e == 0 else (lane >= HD), x, jnp.zeros_like(x))

    def mask_keys(scores):
        row = lax.broadcasted_iota(jnp.int32, scores.shape, 0)
        return jnp.where(row < z.SEQ, scores, -1e30)

    def attend(s, pr):
        cc = lanes(pr * 128, 128)
        rr = slice(s * R, s * R + R)
        kp = k[rr, cc]
        vt = v[rr, cc].T
        for (c0, cw) in chunks:
            qp = q[s * R + c0:s * R + c0 + cw, cc]
            parts = []
            for e in range(2):
                sc = mask_keys(dot_nt(kp, half_mask(qp, e)))
                mx = jnp.max(sc, axis=0, keepdims=True)
                ex = jnp.exp(sc - mx)
                tot = jnp.sum(ex, axis=0, keepdims=True)
                soft = (ex * (1.0 / tot)).astype(BF)
                parts.append(dot(vt[e * HD:(e + 1) * HD], soft))
                lse[(s * z.NP + pr) * 2 + e, :, c0:c0 + cw] = mx + jnp.log(tot)
            out = jnp.concatenate(parts, axis=0)
            att[s * R + c0:s * R + c0 + cw, cc] = out.T.astype(BF)

    csend, ysend = r["csend"], r["ysend"]
    busy = {}
    held = []

    def let_go():
        while held:
            held.pop(0)()

    def free(key):
        for copy in busy.pop(key, []):
            copy.wait_send()

    def own(s):
        return rows16(s * R + c * HR, HR)

    def theirs(s):
        return rows16(s * R + (1 - c) * HR, HR)

    def core_part(s, name, x, w, dst):
        free(("c", s))
        rows_x = x[theirs(s), :]

        def step(j):
            cols = lanes(j * 256, 256)
            csend[s, :, cols] = dot_nt(rows_x, w[pl.ds(pl.multiple_of(j * 256, 256), 256), :]).astype(BF)
        loop(D // 256, step)
        copy = rcopy(csend.at[s], dst.at[s], z.slot_core[name][s], mate)
        busy[("c", s)] = [send(copy, late=False)]

    def core_wait(s, name, dst):
        rcopy(dst.at[s], dst.at[s], z.slot_core[name][s], mate).wait_recv()

    def chip_part(s, name, x, w, got, dst, hold=False):
        core_wait(s, name, got)
        free(("y", s))
        rows_x = x[own(s), :]

        def step(j):
            cols = lanes(j * 256, 256)
            part = dot_nt(rows_x, w[pl.ds(pl.multiple_of(j * 256, 256), 256), :])
            ysend[s, :, cols] = (part + got[s, :, cols].astype(F32)).astype(BF)
        loop(D // 256, step)
        copies = [
            rcopy(ysend.at[s], dst.at[s, dy - 1], z.slot_y[name][s] + dy - 1, y_dev(dy)) for dy in range(1, Y)
        ]
        start_all(("y", s), copies, hold)

    def start_all(key, copies, hold):
        busy[key] = copies

        def go():
            for copy in copies:
                copy.start()
        if hold:
            held.append(go)
        else:
            go()

    def chip_share(s, name, x, w, got, dst, buf, key, hold=False):
        core_wait(s, name, got)
        free((key, s))
        rows_x = x[own(s), :]
        copies = []
        for dy in range(1, Y):
            first = lax.rem(y + dy, Y) * Dy
            part = dot_nt(rows_x, w[rows16(first, Dy), :]) + got[s, :, lanes(first, Dy)].astype(F32)
            span = slice((dy - 1) * Dy, dy * Dy)
            buf[s, :, span] = part.astype(BF)
            copies.append(rcopy(buf.at[s, :, span], dst.at[s, dy - 1], z.slot_y[name][s] + dy - 1, y_dev(dy)))
        start_all((key, s), copies, hold)

    def y_wait(s, name, dst):
        for dy in range(1, Y):
            got = dst.at[s, dy - 1]
            rcopy(got, got, z.slot_y[name][s] + dy - 1, mate).wait_recv()

    def own_share(s, x, w, got, dst):
        first = y * Dy
        total = dot_nt(x[own(s), :], w[rows16(first, Dy), :]) + got[s, :, lanes(first, Dy)].astype(F32)
        for dy in range(1, Y):
            total = total + dst[s, dy - 1].astype(F32)
        return total

    hid = r["hid"]
    cr1, cr2, cr3, yr1, yr2, yr3, yrO = (r[n] for n in ("cr1", "cr2", "cr3", "yr1", "yr2", "yr3", "yrO"))

    def norm_two(s):
        y_wait(s, "branch", yr1)
        gain, shift, bias = vector(3, slice(0, D)), vector(4, slice(0, D)), vector(2, slice(0, D))

        def step(i):
            lr = rows16(i * 16, 16)
            h = ysend[s, lr, :].astype(F32)
            for dy in range(Y - 1):
                h = h + yr1[s, dy, lr, :].astype(F32)
            gr = rows16(s * R + c * HR + i * 16, 16)
            h = tokF[gr, :].astype(F32) + (h + bias)
            hid[rows16(s * HR + i * 16, 16), :] = h
            mu, inv = stats(h)
            n2[gr, :] = ((h - mu) * inv * gain + shift).astype(BF)
        loop(HR // 16, step, True)
        part = n2.at[own(s)]
        busy[("n", s)] = [send(rcopy(part, part, z.slot_core["n2"][s], mate), late=False)]
        yc = lanes(y * Dy, Dy)
        ebuf[s] = hid[s * HR:s * HR + HR, yc] + vst[0, 4, 5:6, yc]

    ubuf, gp = r["ubuf"], r["gp"]
    UC = min(512, F)
    root = 0.5 ** 0.5
    dens = (2.0 * 3.141592653589793) ** -0.5

    def up(s):
        part = n2.at[theirs(s)]
        rcopy(part, part, z.slot_core["n2"][s], mate).wait_recv()
        x = n2[s * R:s * R + R, :]

        def column(j):
            cols = lanes(j * UC, UC)
            ubuf[...] = dot(x, W[2][:, cols]) + vst[0, 4, 6:7, cols]

            def step(i):
                lr = rows16(i * 32, 32)
                gr = rows16(s * R + i * 32, 32)
                u = ubuf[lr, :]
                phi = 0.5 * lax.erf(u * root) + 0.5
                na[gr, cols] = (u * phi).astype(BF)
                gp[gr, cols] = (phi + u * (jnp.exp(-0.5 * u * u) * dens)).astype(BF)
            loop(R // 32, step)
        loop(F // UC, column)

    def back_up(s):
        x = feedF[s * R:s * R + R, :]

        def column(j):
            cols = lanes(j * 256, 256)
            ga = dot(x, W[3][:, cols])
            gp[s * R:s * R + R, cols] = (ga * gp[s * R:s * R + R, cols].astype(F32)).astype(BF)
        loop(F // 256, column)

    obuf, ebuf, lo, ig = r["obuf"], r["ebuf"], r["lo"], r["ig"]

    def layer_out(s):
        y_wait(s, "out", yrO)
        total = own_share(s, na_act, W[3], cr1, yrO)
        obuf[s] = (total + ebuf[s]).astype(BF)
        give_out(s, obuf, lo, "lo")

    def give_out(s, buf, out, name):
        out[own(s), :] = buf[s, :, lanes(c * Dm, Dm)]
        send(rcopy(buf.at[s, :, lanes((1 - c) * Dm, Dm)], out.at[own(s)], z.slot_core[name][s], mate))

    def take_out(s, out, name):
        dst = out.at[theirs(s)]
        rcopy(dst, dst, z.slot_core[name][s], mate).wait_recv()

    na_act = na.at[:, 0:F]
    gb, gatt, gj, acc, gvl = r["gb"], r["gatt"], r["gj"], r["acc"], r["gvl"]

    def norm_two_back(s):
        y_wait(s, "gn2", yr2)
        let_go()
        gain = vector(3, slice(0, D))

        def step(i, sums):
            lr = rows16(i * 16, 16)
            e = ysend[s, lr, :].astype(F32)
            for dy in range(Y - 1):
                e = e + yr2[s, dy, lr, :].astype(F32)
            hr = rows16(s * HR + i * 16, 16)
            gr = rows16(s * R + c * HR + i * 16, 16)
            h = hid[hr, :]
            mu, inv = stats(h)
            xhat = (h - mu) * inv
            t = e * gain
            m1 = jnp.sum(t, axis=1, keepdims=True) * (1.0 / D)
            m2 = jnp.sum(t * xhat, axis=1, keepdims=True) * (1.0 / D)
            g = feedF[gr, :].astype(F32) + inv * (t - m1 - xhat * m2)
            hid[hr, :] = g
            g = g.astype(BF)
            gb[gr, :] = g
            g = g.astype(F32)
            ex = e * xhat
            fold = lambda m: m[0:8] + m[8:16]
            return (sums[0] + fold(ex), sums[1] + fold(e), sums[2] + fold(g))
        zero = jnp.zeros((8, D), F32)
        sums = lax.fori_loop(0, HR // 16, step, (zero, zero, zero))
        for i in range(3):
            acc[i] = sums[i] if s == 0 else acc[i] + sums[i]
        part = gb.at[own(s)]
        send(rcopy(part, part, z.slot_core["gb"][s], mate))

    def attend_back_start(s):
        part = gb.at[theirs(s)]
        rcopy(part, part, z.slot_core["gb"][s], mate).wait_recv()
        gatt[...] = dot(gb[s * R:s * R + R, :], W[1][...]).astype(BF)

    def attend_back(s, pr):
        cc = lanes(pr * 128, 128)
        rr = slice(s * R, s * R + R)
        kp = k[rr, cc]
        vp = v[rr, cc]
        kt = kp.T
        dk = jnp.zeros((R, 128), F32)
        dv = jnp.zeros((R, 128), F32)
        for (c0, cw) in chunks:
            qp = q[s * R + c0:s * R + c0 + cw, cc]
            go = gatt[c0:c0 + cw, cc]
            parts = []
            for e in range(2):
                qm, gm = half_mask(qp, e), half_mask(go, e)
                sc = mask_keys(dot_nt(kp, qm))
                soft = jnp.exp(sc - lse[(s * z.NP + pr) * 2 + e, :, c0:c0 + cw])
                dv = dv + dot(soft.astype(BF), gm)
                gs = dot_nt(vp, gm)
                delta = jnp.sum(gs * soft, axis=0, keepdims=True)
                ds = (soft * (gs - delta)).astype(BF)
                dk = dk + dot(ds, qm)
                parts.append(dot(kt[e * HD:(e + 1) * HD], ds))
            dq = jnp.concatenate(parts, axis=0) * (HD ** -0.5)
            gj[s * R + c0:s * R + c0 + cw, lanes(pr * 128, 128)] = dq.T.astype(BF)
        gj[rr, lanes(HW + pr * 128, 128)] = dk.astype(BF)
        gj[rr, lanes(2 * HW + pr * 128, 128)] = dv.astype(BF)

    stat, statT, statR = r["stat"], r["statT"], r["statR"]

    def norm_one_sums(s):
        y_wait(s, "gn1", yr3)
        ebuf[s] = own_share(s, gj, W[0], cr3, yr3)
        yc = lanes(y * Dy, Dy)
        gain = vector(0, yc)

        def step(i, sums):
            lr = rows16(i * 16, 16)
            gr = rows16(s * R + c * HR + i * 16, 16)
            mu, inv = stats(tokF[gr, :].astype(F32))
            xhat = (tokF[gr, yc].astype(F32) - mu) * inv
            e = ebuf[s, lr, :]
            t = e * gain
            s1 = jnp.sum(t, axis=1, keepdims=True)
            s2 = jnp.sum(t * xhat, axis=1, keepdims=True)
            lane = lax.broadcasted_iota(jnp.int32, (16, 128), 1)
            stat[lr, :] = jnp.where(lane == 0, s1, jnp.where(lane == 1, s2, 0.0))
            ex = e * xhat
            fold = lambda m: m[0:8] + m[8:16]
            return (sums[0] + fold(ex), sums[1] + fold(e))
        zero = jnp.zeros((8, Dy), F32)
        sums = lax.fori_loop(0, HR // 16, step, (zero, zero))
        for i in range(2):
            row = jnp.sum(sums[i], axis=0, keepdims=True)
            gvl[i:i + 1, yc] = row if s == 0 else gvl[i:i + 1, yc] + row
        statT[s] = stat[...].T[0:8]
        for dy in range(1, Y):
            send(rcopy(statT.at[s], statR.at[s, dy - 1], z.slot_y["st"][s] + dy - 1, y_dev(dy)))

    def norm_one_back(s):
        y_wait(s, "st", statR)
        total = statT[s]
        for dy in range(Y - 1):
            total = total + statR[s, dy]
        total = jnp.concatenate([total, jnp.zeros((120, HR), F32)], axis=0)
        stat[...] = total.T * (1.0 / D)
        yc = lanes(y * Dy, Dy)
        gain = vector(0, yc)

        def step(i):
            lr = rows16(i * 16, 16)
            gr = rows16(s * R + c * HR + i * 16, 16)
            mu, inv = stats(tokF[gr, :].astype(F32))
            xhat = (tokF[gr, yc].astype(F32) - mu) * inv
            t = ebuf[s, lr, :] * gain
            st = stat[lr, :]
            m1, m2 = st[:, 0:1], st[:, 1:2]
            g = hid[rows16(s * HR + i * 16, 16), yc]
            ebuf[s, lr, :] = g + inv * (t - m1 - xhat * m2)
        loop(HR // 16, step, True)
        give_out(s, ebuf, ig, "ig")

    G = [r[f"G{p}"] for p in range(4)]
    RX = [r[f"RX{p}"] for p in range(4)]
    Z = [r[f"Z{p}"] for p in range(4)]
    outs = [r[f"o{p}"] for p in range(4)]

    def weight_grad(p, x, g):
        def step(i):
            rr = pl.ds(pl.multiple_of(i * 256, 256), 256)
            G[p][rr, :] = dot_tn(x[:, lanes(i * 256, 256)], g[...]).astype(BF)
        loop(D // 256, step)

    def gblock(p, blk):
        return rows16(blk * RB, RB)

    def rs_cross(i):
        p, first, width = z.scatters[i]
        cols = pl.ds(first, width)
        for db in range(1, B):
            bd = lax.rem(b + db, B)
            for aa in range(A):
                send(rcopy(
                    G[p].at[gblock(p, aa * B + bd), cols], RX[p].at[db - 1, aa, :, cols],
                    z.rs_x[i] + (db - 1) * A + aa, b_dev(db),
                ))

    def pump():
        while waiting and len(flying) < 2:
            flying.append(waiting.pop(0))
            rs_cross(flying[-1])

    def rs_add(i):
        p, first, width = z.scatters[i]
        cols = pl.ds(first, width)
        for db in range(1, B):
            for aa in range(A):
                dst = RX[p].at[db - 1, aa, :, cols]
                rcopy(dst, dst, z.rs_x[i] + (db - 1) * A + aa, mate).wait_recv()
        flying.remove(i)
        pump()
        if B > 1:
            def step(aa):
                rr = gblock(p, aa * B + b)
                total = G[p][rr, cols].astype(F32)
                for db in range(B - 1):
                    total = total + RX[p][db, aa, :, cols].astype(F32)
                G[p][rr, cols] = total.astype(BF)
            loop(A, step)

        for da in range(1, A):
            rr = gblock(p, lax.rem(a + da, A) * B + b)
            send(rcopy(G[p].at[rr, cols], Z[p].at[da - 1, :, cols], z.rs_z[i] + da, a_dev(da)))

    def rs_done(i):
        p, first, width = z.scatters[i]
        cols = pl.ds(first, width)
        total = G[p][gblock(p, dpi), cols].astype(F32)
        for da in range(1, A):
            dst = Z[p].at[da - 1, :, cols]
            rcopy(dst, dst, z.rs_z[i] + da, mate).wait_recv()
            total = total + Z[p][da - 1, :, cols].astype(F32)
        if p == 0:
            for t in range(first // HW, (first + width - 1) // HW + 1):
                low, high = max(first, t * HW), min(first + width, (t + 1) * HW)
                outs[0][t, :, low - t * HW:high - t * HW] = total[:, low - first:high - first]
        elif p in (1, 3):
            outs[p][cols, :] = total.T
        else:
            outs[p][:, cols] = total

    def rs_groups():
        groups = []
        for i in range(len(z.scatters)):
            group = [functools.partial(rs_add, i)]
            if i:
                group.append(functools.partial(rs_done, i - 1))
            groups.append((i, group))
        return groups + [(None, [functools.partial(rs_done, len(z.scatters) - 1)])]

    def cross_part(part):
        waiting.extend(i for i, piece in enumerate(z.scatters) if piece[0] == part)
        pump()

    first_pieces, second = of_part(0), of_part(1)
    order = first_pieces + second + of_part(2) + of_part(3)
    begun = []

    def ag_next():
        if len(begun) < len(order):
            ag_start(order[len(begun)])
            begun.append(1)

    place_rows(0)
    rows_start(0)
    place_weights(0)
    ag_next()
    ag_next()
    small_in()
    vec_send(0, 0)
    for p in range(1, 4):
        place_weights(p)
    for t in range(1, 2 * NS):
        place_rows(t)
    vec_add(0, 0)
    vec_send(0, 1)
    ag_near(order[0])
    ag_next()
    vec_add(0, 1)
    vec_send(0, 2)
    ag_far(order[0])
    vec_add(0, 2)
    vec_send(0, 3)
    ag_near(order[1])
    ag_next()
    vec_add(0, 3)
    rows_relay(0)
    for t in range(1, NS):
        rows_start(t)
    ag_far(order[1])
    ag_near(order[2])
    ag_next()
    rows_done(0)
    norm_one(0, na)
    ag_far(order[2])
    ag_near(order[3])
    ag_next()
    for t in range(1, NS):
        rows_relay(t)
    for t in range(NS, 2 * NS):
        rows_start(t)
    ag_far(order[3])
    for i in first_pieces:
        ag_done(i)
    for i in order[4:]:
        ticks += [(None, [functools.partial(ag_near, i), ag_next]), (None, [functools.partial(ag_far, i)])]
    for s in range(NS):
        if s > 0:
            rows_done(s)
            norm_one(s, na)
        project(s)
        tick()
        for pr in range(z.NP):
            attend(s, pr)
            if s == 0 or pr == 0:
                tick()
        if s == 0:
            for i in second:
                ag_done(i)
        core_part(s, "branch", att, W[1], cr1)
        if s == 0:
            tick()
        chip_part(s, "branch", att, W[1], cr1, yr1)
    while ticks:
        tick()
    for t in range(NS, 2 * NS):
        rows_relay(t)
    for s in range(NS):
        norm_two(s)
        if s == 0:
            for i in of_part(2):
                ag_done(i)
            for t in range(NS, 2 * NS):
                rows_done(t)
        up(s)
    weight_grad(3, feedF, na_act)
    cross_part(3)
    for i in of_part(3):
        ag_done(i)
    for s in range(NS):
        back_up(s)
        if s > 0:
            chip_part(s - 1, "gn2", gp, W[2], cr2, yr2)
        core_part(s, "gn2", gp, W[2], cr2)
    chip_part(NS - 1, "gn2", gp, W[2], cr2, yr2, True)
    weight_grad(2, n2, gp)
    cross_part(2)
    ticks += rs_groups()
    gvl[...] = jnp.zeros_like(gvl)
    ones_row = jnp.ones((8, z.ROWS), BF)
    gvl[5:6, lanes(mpi * Dm, Dm)] = dot(ones_row, feedF[:, lanes(mpi * Dm, Dm)])[0:1]
    gvl[6:7, 0:F] = dot(ones_row, gp[...])[0:1]
    for s in range(NS):
        core_part(s, "out", na_act, W[3], cr1)
    for s in range(NS):
        free(("n", s))
        norm_one(s, n2)
    tick()
    for s in range(NS):
        norm_two_back(s)
        if s == NS - 1:
            for t in range(NS):
                chip_share(t, "out", na_act, W[3], cr1, yrO, r["ysO"], "o")
        tick()
        attend_back_start(s)
        for pr in range(z.NP):
            attend_back(s, pr)
            if s == 0 and pr == z.NP - 1:
                tick()
        core_part(s, "gn1", gj, W[0], cr3)
        if s < NS - 1:
            chip_share(s, "gn1", gj, W[0], cr3, yr3, ysend, "y", True)
    weight_grad(0, n2, gj)
    cross_part(0)
    chip_share(NS - 1, "gn1", gj, W[0], cr3, yr3, ysend, "y")
    tick()
    weight_grad(1, gb, att)
    cross_part(1)
    for s in range(NS):
        layer_out(s)
    tick()
    gvl[7:8, 0:HW] = dot(ones_row, gj[:, 0:HW])[0:1]
    gvl[7:8, HW:2 * HW] = dot(ones_row, gj[:, 2 * HW:3 * HW])[0:1]
    yc = lanes(y * Dy, Dy)
    for row, i in ((3, 0), (4, 1), (2, 2)):
        gvl[row:row + 1, yc] = jnp.sum(acc[i, :, yc], axis=0, keepdims=True)
    for s in range(NS):
        norm_one_sums(s)
        tick()
    vst[1, 0] = gvl[...]
    vec_send(1, 0)
    for s in range(NS):
        norm_one_back(s)
        vec_add(1, s)
        vec_send(1, s + 1)
        tick()
    for stage in range(NS, 4):
        vec_add(1, stage)
        if stage < 3:
            vec_send(1, stage + 1)
    small_out(vst[1, 4])
    while ticks:
        tick()
    for s in range(NS):
        take_out(s, lo, "lo")
        take_out(s, ig, "ig")
    for key in list(busy):
        free(key)
    for cond, copy in pending:
        when(cond, lambda copy=copy: copy.wait_send())


def body(mesh, tokens, slot_flags, cotangent, attend_gain, attend_shift, input_weight, input_bias,
         output_weight, output_bias, dense_gain, dense_shift, up_weight, up_bias, down_weight, down_bias):
    z = Sizes(mesh, tokens, input_weight, up_weight)
    small = (attend_gain, attend_shift, output_bias, dense_gain, dense_shift, down_bias, up_bias.T, input_bias)
    shapes = [
        jax.ShapeDtypeStruct((z.ROWS, z.Dm), BF),
        jax.ShapeDtypeStruct((z.ROWS, z.Dm), F32),
        jax.ShapeDtypeStruct((3, z.RB, z.HW), F32),
        jax.ShapeDtypeStruct(output_weight.shape, F32),
        jax.ShapeDtypeStruct(up_weight.shape, F32),
        jax.ShapeDtypeStruct(down_weight.shape, F32),
    ] + [jax.ShapeDtypeStruct(x.shape, F32) for x in small]
    vmem = pl.BlockSpec(memory_space=pltpu.VMEM)
    smem = pl.BlockSpec(memory_space=pltpu.SMEM)
    lo, ig, g0, g1, g2, g3, *gs = pl.pallas_call(
        functools.partial(kernel, z),
        out_shape=shapes,
        in_specs=[vmem, vmem, smem] + [vmem] * 12,
        out_specs=[vmem] * 14,
        scratch_shapes=scratch_shapes(z),
        compiler_params=pltpu.CompilerParams(
            collective_id=0, has_side_effects=True, vmem_limit_bytes=VMEM_LIMIT
        ),
        name="layer",
    )(
        tokens, cotangent, slot_flags, input_weight.transpose(1, 0, 2), output_weight, up_weight, down_weight,
        *small,
    )
    filled = slot_flags.astype(F32)[:, None, None]
    layer_rows = (lo.reshape(z.NS, z.R, z.Dm)[:, :z.SEQ].astype(F32) * filled).astype(BF)
    input_grad = ig.reshape(z.NS, z.R, z.Dm)[:, :z.SEQ] * filled
    return (
        layer_rows, input_grad, gs[0], gs[1], g0.transpose(1, 0, 2), gs[7], g1, gs[2], gs[3], gs[4],
        g2, gs[6].T, g3, gs[5],
    )


VMEM_LIMIT = 63 * 2**20


def solution(mesh):
    rows = P("dp", None, "mp")
    vec = P("mp", "dp")
    pair = P(None, "mp", "dp")
    return jax.shard_map(
        functools.partial(body, mesh),
        mesh=mesh,
        in_specs=(rows, P("dp"), rows, vec, vec, rows, pair, vec, vec, vec, vec, P("dp", "mp"), vec, vec, vec),
        out_specs=(rows, rows, vec, vec, rows, pair, vec, vec, vec, vec, P("dp", "mp"), vec, vec, vec),
        check_vma=False,
    )
```

```python
import functools

import jax
import jax.numpy as jnp
from jax import lax
from jax.experimental import pallas as pl
from jax.experimental.pallas import tpu as pltpu
from jax.sharding import PartitionSpec as P

HD = 64
EPS = 1e-06
MESH = pl.DeviceIdType.MESH
BF = jnp.bfloat16
F32 = jnp.float32


def dot(left, right):
    return jnp.dot(left, right, preferred_element_type=F32)


def dot_nt(left, right):
    return lax.dot_general(left, right, (((1,), (1,)), ((), ())), preferred_element_type=F32)


def dot_tn(left, right):
    return lax.dot_general(left, right, (((0,), (0,)), ((), ())), preferred_element_type=F32)


class Ids:
    def __init__(self):
        self.count = 0

    def take(self, number):
        first = self.count
        self.count += number
        return first


class Sizes:
    def __init__(self, mesh, tokens, input_weight, up_weight):
        dp, mp = mesh.shape["dp"], mesh.shape["mp"]
        self.dp, self.mp = dp, mp
        self.A = 4 if dp % 4 == 0 else dp
        self.B = dp // self.A
        self.Y = mp // 2
        self.SEQ, self.NS, self.Dm = tokens.shape
        self.R = -(-self.SEQ // 32) * 32
        self.HR = self.R // 2
        self.ROWS = self.NS * self.R
        self.D = self.Dm * mp
        self.Dy = 2 * self.Dm
        self.RB = input_weight.shape[0]
        self.HW = input_weight.shape[2]
        self.NP = self.HW // 128
        self.F = up_weight.shape[1]
        self.VW = max(self.D, self.F, 2 * self.HW)
        self.wide = HD // dp
        heads = self.D // mp // HD
        self.groups = [heads] * 6 + [self.F // HD, 2 * self.HW // HD]
        self.NR = sum(self.groups)
        self.cols = (3 * self.HW, self.HW, self.F, self.F)
        ids = Ids()
        A, B, Y, NS = self.A, self.B, self.Y, self.NS
        self.gathers = self.cut(((0, 256), (1, 256), (2, 512), (3, 512)))
        self.scatters = self.cut(((3, 256), (2, 256), (1, 256), (0, 256)))
        self.ag_z = [ids.take(6) for _ in self.gathers]
        self.ag_x = [ids.take((B - 1) * A) for _ in self.gathers]
        self.rs_z = [ids.take(A) for _ in self.scatters]
        self.rs_x = [ids.take((B - 1) * A) for _ in self.scatters]
        self.rows_c = [ids.take(1) for _ in range(2 * NS)]
        self.rows_y = [ids.take(Y) for _ in range(2 * NS)]
        self.rows_f = [ids.take(Y) for _ in range(2 * NS)]
        self.vec_ids = [[ids.take(dp), ids.take(mp)] for _ in range(2)]
        self.slot_core = {
            name: [ids.take(1) for _ in range(NS)]
            for name in ("branch", "n2", "out", "lo", "gn2", "gb", "gn1", "ig")
        }
        self.slot_y = {
            name: [ids.take(Y) for _ in range(NS)] for name in ("branch", "out", "gn2", "gn1", "st")
        }
        self.nsem = ids.count

    def cut(self, widths):
        return [
            (p, first, min(width, self.cols[p] - first))
            for p, width in widths
            for first in range(0, self.cols[p], width)
        ]


SCRATCH = (
    "tokF", "feedF", "W0", "W1", "W2", "W3", "na", "q", "k", "v", "att", "csend", "cr1", "ysend", "ysO", "yr1",
    "yrO", "hid", "n2", "gp", "cr2", "yr2", "gb", "gatt", "gj", "cr3", "yr3", "ebuf", "obuf", "stat", "statT",
    "statR", "ubuf", "lse", "G1", "G2", "G3", "RX0", "RX1", "RX2", "RX3", "Z0", "Z1", "Z2", "Z3",
    "acc", "gvl", "prm", "big", "vec", "vall", "vgo", "vgm", "vgc", "vgA", "loP", "igP", "ss", "rs",
)
OPERANDS = (
    "tokens", "cot", "flags", "iw", "ow", "uw", "dw", "p0", "p1", "p2", "p3", "p4", "p5", "pu", "pi",
    "lo", "ig", "o0", "o1", "o2", "o3", "qd", "qu", "qi",
)


def scratch_shapes(z):
    A, B, Y, NS = z.A, z.B, z.Y, z.NS
    V = pltpu.VMEM
    half = (NS, z.HR, z.D)
    shapes = dict(
        tokF=V((z.ROWS, z.D), BF),
        feedF=V((z.ROWS, z.D), BF),
        na=V((z.ROWS, max(z.D, z.F)), BF),
        q=V((z.ROWS, z.HW), BF),
        k=V((z.ROWS, z.HW), BF),
        v=V((z.ROWS, z.HW), BF),
        att=V((z.ROWS, z.HW), BF),
        csend=V(half, BF),
        cr1=V(half, BF),
        ysend=V(half, BF),
        ysO=V(half, BF),
        yr1=V((NS, Y - 1, z.HR, z.D), BF),
        yrO=V((NS, Y - 1, z.HR, z.Dy), BF),
        hid=V((NS * z.HR, z.D), F32),
        n2=V((z.ROWS, z.D), BF),
        gp=V((z.ROWS, z.F), BF),
        cr2=V(half, BF),
        yr2=V((NS, Y - 1, z.HR, z.D), BF),
        gb=V((z.ROWS, z.D), BF),
        gatt=V((z.R, z.HW), BF),
        gj=V((z.ROWS, 3 * z.HW), BF),
        cr3=V(half, BF),
        yr3=V((NS, Y - 1, z.HR, z.Dy), BF),
        ebuf=V((NS, z.HR, z.Dy), F32),
        obuf=V((NS, z.HR, z.Dy), BF),
        stat=V((z.HR, 128), F32),
        statT=V((NS, 8, z.HR), F32),
        statR=V((NS, Y - 1, 8, z.HR), F32),
        ubuf=V((z.R, min(256, z.F)), F32),
        lse=V((NS * 2 * z.NP, 1, z.R), F32),
        vec=V((8, z.VW), F32),
        vall=V((z.mp, z.dp, 8, 128), F32),
        vgo=V((z.dp, 8, 128), F32),
        vgm=V((z.dp, 8, 128), F32),
        vgc=V((z.dp, 8, 128), F32),
        vgA=V((z.dp, 8, 128), F32),
        loP=V((NS, z.HR, z.Dm), BF),
        igP=V((NS, z.HR, z.Dm), F32),
        acc=V((3, 8, z.D), F32),
        gvl=V((8, z.VW), F32),
        prm=V((128, 128), F32),
        big=V((z.NR, z.VW), F32),
        ss=pltpu.SemaphoreType.DMA((z.nsem,)),
        rs=pltpu.SemaphoreType.DMA((z.nsem,)),
    )
    for p, cols in enumerate(z.cols):
        shapes[f"W{p}"] = V((z.D, cols), BF)
        if p > 0:
            shapes[f"G{p}"] = V((z.D, max(cols, z.cols[0]) if p == 3 else cols), BF)
        shapes[f"RX{p}"] = V((max(B - 1, 1), A, z.RB, cols), BF)
        shapes[f"Z{p}"] = V((A - 1, z.RB, cols), BF)
    return [shapes[name] for name in SCRATCH]


def kernel(z, *refs):
    r = dict(zip(OPERANDS + SCRATCH, refs))
    A, B, Y, NS, R, HR, D, Dm, Dy, HW, F, RB = (
        z.A, z.B, z.Y, z.NS, z.R, z.HR, z.D, z.Dm, z.Dy, z.HW, z.F, z.RB,
    )
    ss, rs = r["ss"], r["rs"]
    dpi, mpi = lax.axis_index("dp"), lax.axis_index("mp")
    a, b = dpi // B, dpi % B
    y, c = mpi // 2, mpi % 2

    def dev(a=a, b=b, y=y, c=c):
        return (a * B + b, y * 2 + c)

    def rcopy(src, dst, i, device):
        return pltpu.make_async_remote_copy(
            src_ref=src, dst_ref=dst, send_sem=ss.at[i], recv_sem=rs.at[i],
            device_id=device, device_id_type=MESH,
        )

    def when(cond, f):
        if cond is True:
            f()
        elif cond is not False:
            pl.when(cond)(f)

    pending = []

    def send(copy, cond=True, late=True):
        when(cond, lambda: copy.start())
        if late:
            pending.append((cond, copy))
        return copy

    mate = dev(c=1 - c)

    def y_dev(dy):
        return dev(y=lax.rem(y + dy, Y))

    def b_dev(db):
        return dev(b=lax.rem(b + db, B))

    def a_dev(da):
        return dev(a=lax.rem(a + da, A))

    def rows16(start, size):
        return pl.ds(pl.multiple_of(start, 16), size)

    def lanes(start, size):
        return pl.ds(pl.multiple_of(start, 128), size)

    def loop(n, f, unroll=1):
        def step(i, carry):
            f(i)
            return carry
        lax.fori_loop(0, n, step, 0, unroll=unroll)

    bar = pltpu.get_barrier_semaphore()
    def dp_dev(d):
        return (lax.rem(dpi + d, z.dp), mpi)

    def mp_dev(d):
        return (dpi, lax.rem(mpi + d, z.mp))

    friends = [dp_dev(d) for d in range(1, z.dp)] + [mp_dev(d) for d in range(1, z.mp)]
    for friend in friends:
        pl.semaphore_signal(bar, inc=1, device_id=friend, device_id_type=MESH)
    pl.semaphore_wait(bar, len(friends))

    W = [r[f"W{p}"] for p in range(4)]
    own_w = rows16(dpi * RB, RB)

    def place_weights(p):
        if p == 0:
            for t in range(3):
                W[0][own_w, t * HW:(t + 1) * HW] = r["iw"][t]
        elif p == 2:
            W[2][own_w, :] = r["uw"][...]
        else:
            W[p][own_w, :] = r["ow" if p == 1 else "dw"][...].T

    def wblock(p, blk, first, width):
        return W[p].at[rows16(blk * RB, RB), pl.ds(first, width)]

    def line_dev(step):
        return dev(a=jnp.clip(a + step, 0, A - 1))

    def ag_cross(i, src, blk_a, cond):
        p, first, width = z.gathers[i]
        dst = wblock(p, blk_a * B + b, first, width)
        for db in range(1, B):
            send(rcopy(src, dst, z.ag_x[i] + (db - 1) * A + blk_a, b_dev(db)), cond)

    def ag_start(i):
        p, first, width = z.gathers[i]
        own_block = src = wblock(p, dpi, first, width)
        ag_cross(i, src, a, True)
        send(rcopy(src, own_block, z.ag_z[i], line_dev(1)), a + 1 < A)
        send(rcopy(src, own_block, z.ag_z[i] + 1, line_dev(-1)), a >= 1)
        send(rcopy(src, own_block, z.ag_z[i] + 2, line_dev(2)), a + 2 < A)
        send(rcopy(src, own_block, z.ag_z[i] + 3, line_dev(-2)), a >= 2)

    def ag_take(i, kind, step, relay=None):
        p, first, width = z.gathers[i]
        there = (a + step >= 0) if step < 0 else (a + step < A)
        src_a = jnp.clip(a + step, 0, A - 1)
        blk = wblock(p, src_a * B + b, first, width)
        when(there, lambda: rcopy(blk, blk, z.ag_z[i] + kind, mate).wait_recv())
        if relay is not None:
            go = there & ((a + relay < A) if relay > 0 else (a + relay >= 0))
            send(rcopy(blk, blk, z.ag_z[i] + kind + 2, line_dev(relay)), go)
        ag_cross(i, blk, src_a, there)

    def ag_near(i):
        ag_take(i, 0, -1)
        ag_take(i, 1, 1)
        ag_take(i, 2, -2, 1)
        ag_take(i, 3, 2, -1)

    def ag_far(i):
        ag_take(i, 4, -3)
        ag_take(i, 5, 3)

    def ag_done(i):
        p, first, width = z.gathers[i]
        for db in range(1, B):
            bs = lax.rem(b + B - db, B)
            for aa in range(A):
                blk = wblock(p, aa * B + bs, first, width)
                rcopy(blk, blk, z.ag_x[i] + (db - 1) * A + aa, mate).wait_recv()

    def of_part(p):
        return [i for i, piece in enumerate(z.gathers) if piece[0] == p]

    full = [r["tokF"], r["feedF"]]

    def place_rows(t):
        s = t % NS
        src = r["tokens"] if t < NS else r["cot"]
        keep = 1.0 if t < NS else r["flags"][s].astype(F32)
        cols = lanes(mpi * Dm, Dm)
        head = z.SEQ // 16 * 16
        full[t // NS][s * R:s * R + head, cols] = (src[0:head, s, :].astype(F32) * keep).astype(BF)
        last = jnp.broadcast_to(src[head:z.SEQ, s, :].astype(F32) * keep, (R - head, Dm))
        row = lax.broadcasted_iota(jnp.int32, (R - head, Dm), 0)
        full[t // NS][s * R + head:s * R + R, cols] = jnp.where(row < z.SEQ - head, last, 0.0).astype(BF)

    def mblock(t, m):
        return full[t // NS].at[pl.ds(t % NS * R, R), lanes(m * Dm, Dm)]

    def rows_start(t):
        src = mblock(t, mpi)
        for dy in range(1, Y):
            send(rcopy(src, src, z.rows_y[t] + dy, y_dev(dy)))
        send(rcopy(src, src, z.rows_c[t], mate))

    def rows_relay(t):
        for dy in range(1, Y):
            blk = mblock(t, lax.rem(y + Y - dy, Y) * 2 + c)
            rcopy(blk, blk, z.rows_y[t] + dy, mate).wait_recv()
            send(rcopy(blk, blk, z.rows_f[t] + dy, mate))

    def rows_done(t):
        blk = mblock(t, y * 2 + 1 - c)
        rcopy(blk, blk, z.rows_c[t], mate).wait_recv()
        for dy in range(1, Y):
            blk = mblock(t, lax.rem(y + Y - dy, Y) * 2 + 1 - c)
            rcopy(blk, blk, z.rows_f[t] + dy, mate).wait_recv()

    vall, prm = r["vall"], r["prm"]

    def spread(kind):
        lane = lax.broadcasted_iota(jnp.int32, (z.dp * 8, z.VW), 1)
        row = lax.broadcasted_iota(jnp.int32, (z.dp * 8, z.VW), 0)
        part = row & 7
        hit = ((lane & (HD - 1)) == (row >> 3) * z.wide + part) & (part < z.wide)
        return jnp.where(hit, 1.0, 0.0).astype(kind)

    def heads_mask(m, mine, count):
        row = lax.broadcasted_iota(jnp.int32, (count, z.VW), 0)
        lane = lax.broadcasted_iota(jnp.int32, (count, z.VW), 1)
        first, head = 0, row
        for p, n in enumerate(z.groups):
            this = row - first
            head = jnp.where(row >= first, this + m * n if p < 6 else jnp.where(mine, this, -1), head)
            first += n
        return (lane >> 6) == jnp.where(row < first, head, -1)

    def small_in():
        prm[...] = jnp.zeros_like(prm)
        first = 0
        for p in range(6):
            prm[first:first + z.groups[p], 0:z.wide] = r[f"p{p}"][...].astype(F32)
            first += z.groups[p]
        prm[first:first + z.groups[6], 0:z.wide] = r["pu"][...].astype(F32).T
        first += z.groups[6]
        for t in range(2):
            half = z.groups[7] // 2
            prm[first + t * half:first + (t + 1) * half, 0:z.wide] = r["pi"][t].astype(F32)
        vall[mpi, dpi] = prm[...].T[0:8]

    def small_send(stage):
        blk = vall.at[mpi] if stage else vall.at[mpi, dpi]
        for d in range(1, (z.dp, z.mp)[stage]):
            send(rcopy(blk, blk, z.vec_ids[0][stage] + d, (dp_dev, mp_dev)[stage](d)))

    def small_take(stage):
        for d in range(1, (z.dp, z.mp)[stage]):
            if stage:
                blk = vall.at[lax.rem(mpi + z.mp - d, z.mp)]
            else:
                blk = vall.at[mpi, lax.rem(dpi + z.dp - d, z.dp)]
            rcopy(blk, blk, z.vec_ids[0][stage] + d, mate).wait_recv()

    def small_spread():
        ones = spread(BF)
        total = jnp.zeros((128, z.VW), F32)
        for m in range(z.mp):
            rows = dot_tn(vall[m].reshape(z.dp * 8, 128).astype(BF), ones)
            total = total + jnp.where(heads_mask(m, m == mpi, 128), rows, 0.0)
        p = lax.broadcasted_iota(jnp.int32, (8, 128), 0)
        row = lax.broadcasted_iota(jnp.int32, (8, 128), 1)
        first, group = 0, jnp.zeros_like(row)
        for i, n in enumerate(z.groups):
            group = jnp.where(row >= first, i, group)
            first += n
        r["vec"][...] = dot(jnp.where(group == p, 1.0, 0.0).astype(BF), total.astype(BF))

    vgo, vgm, vgc, vgA = (r[n] for n in ("vgo", "vgm", "vgc", "vgA"))

    def sums_start():
        big = r["big"]
        first = 0
        for p, n in enumerate(z.groups):
            big[first:first + n, :] = jnp.broadcast_to(gvl[p:p + 1, :], (n, z.VW))
            first += n
        ones = spread(F32)
        for m, mine, out in ((mpi, True, vgo), (y * 2 + 1 - c, False, vgm)):
            rows = jnp.where(heads_mask(m, mine, z.NR), big[...], 0.0)
            got = lax.dot_general(
                ones, rows, (((1,), (1,)), ((), ())),
                precision=lax.Precision.HIGHEST, preferred_element_type=F32,
            )
            out[...] = jnp.zeros_like(out)
            out[:, :, 0:z.NR] = got.reshape(z.dp, 8, z.NR)
        send(rcopy(vgm, vgc, z.vec_ids[1][1], mate))

    def sums_cross():
        rcopy(vgc, vgc, z.vec_ids[1][1], mate).wait_recv()
        vgo[...] = vgo[...] + vgc[...]
        for d in range(1, z.dp):
            src = vgo.at[lax.rem(dpi + d, z.dp)]
            send(rcopy(src, vgA.at[d], z.vec_ids[1][0] + d, dp_dev(d)))

    def sums_done():
        total = vgo[dpi]
        for d in range(1, z.dp):
            dst = vgA.at[d]
            rcopy(dst, dst, z.vec_ids[1][0] + d, mate).wait_recv()
            total = total + vgA[d]
        prm[...] = jnp.concatenate([total, jnp.zeros((120, 128), F32)], axis=0).T
        first = 0
        for p in range(6):
            r["qd"][p] = prm[first:first + z.groups[p], 0:z.wide]
            first += z.groups[p]
        r["qu"][...] = prm[first:first + z.groups[6], :].T[0:z.wide]
        first += z.groups[6]
        half = z.groups[7] // 2
        for t in range(2):
            r["qi"][t] = prm[first + t * half:first + (t + 1) * half, 0:z.wide]

    def vector(row, cols=slice(None)):
        return r["vec"][row:row + 1, cols]

    tokF, feedF, na, n2 = r["tokF"], r["feedF"], r["na"], r["n2"]

    def stats(x):
        mu = jnp.sum(x, axis=1, keepdims=True) * (1.0 / D)
        sq = jnp.sum(x * x, axis=1, keepdims=True) * (1.0 / D)
        return mu, lax.rsqrt(sq - mu * mu + EPS)

    def norm_one(s, out):
        gain, shift = vector(0, slice(0, D)), vector(1, slice(0, D))

        def step(i):
            rr = rows16(s * R + i * 32, 32)
            x = tokF[rr, :].astype(F32)
            mu, inv = stats(x)
            out[rr, :D] = ((x - mu) * inv * gain + shift).astype(BF)
        loop(R // 32, step, True)

    ticks, waiting, flying, finished = [], [], [], []

    def tick():
        if ticks and (ticks[0][0] is None or ticks[0][0] in flying):
            for f in ticks.pop(0)[1]:
                f()

    q, k, v, att, lse = r["q"], r["k"], r["v"], r["att"], r["lse"]

    def project(s):
        rr = slice(s * R, s * R + R)
        x = na[rr, :D]
        for third, ref in enumerate((q, k, v)):
            for j in range(0, HW, 256):
                w = min(256, HW - j)
                col = third * HW + j
                out = dot(x, W[0][:, col:col + w])
                if third == 0:
                    out = out + r["vec"][7:8, j:j + w]
                if third == 2:
                    out = out + r["vec"][7:8, HW + j:HW + j + w]
                out = out.astype(BF)
                if third == 0:
                    out = out * BF(HD ** -0.5)
                ref[rr, j:j + w] = out

    chunks = [(i, min(256, R - i)) for i in range(0, R, 256)]
    top = z.SEQ // 16 * 16

    def half_mask(x, e):
        lane = lax.broadcasted_iota(jnp.int32, x.shape, 1)
        return jnp.where((lane < HD) if e == 0 else (lane >= HD), x, jnp.zeros_like(x))

    def mask_keys(scores):
        row = lax.broadcasted_iota(jnp.int32, scores.shape, 0)
        return jnp.where(row < z.SEQ, scores, -1e30)

    def attend(s, pr):
        cc = lanes(pr * 128, 128)
        rr = slice(s * R, s * R + R)
        kp = k[rr, cc]
        vt = v[rr, cc].T
        for (c0, cw) in chunks:
            qp = q[s * R + c0:s * R + c0 + cw, cc]
            parts = []
            for e in range(2):
                sc = mask_keys(dot_nt(kp, half_mask(qp, e)))
                mx = jnp.max(sc, axis=0, keepdims=True)
                ex = jnp.exp(sc - mx)
                tot = jnp.sum(ex, axis=0, keepdims=True)
                soft = (ex * (1.0 / tot)).astype(BF)
                parts.append(dot(vt[e * HD:(e + 1) * HD], soft))
                lse[(s * z.NP + pr) * 2 + e, :, c0:c0 + cw] = mx + jnp.log(tot)
            out = jnp.concatenate(parts, axis=0)
            att[s * R + c0:s * R + c0 + cw, cc] = out.T.astype(BF)

    csend, ysend, ubuf = r["csend"], r["ysend"], r["ubuf"]
    busy = {}
    held = []

    def let_go():
        while held:
            held.pop(0)()

    def free(key):
        for copy in busy.pop(key, []):
            copy.wait_send()

    def own(s):
        return rows16(s * R + c * HR, HR)

    def theirs(s):
        return rows16(s * R + (1 - c) * HR, HR)

    def core_part(s, name, x, w, dst, keep, key):
        free(("c", s))
        free((key, s))
        rows_x = x[s * R:s * R + R, :]

        def step(j):
            cols = lanes(j * 256, 256)
            ubuf[...] = dot_nt(rows_x, w[pl.ds(pl.multiple_of(j * 256, 256), 256), :])
            csend[s, :, cols] = ubuf[rows16((1 - c) * HR, HR), :].astype(BF)
            keep[s, :, cols] = ubuf[rows16(c * HR, HR), :].astype(BF)
        loop(D // 256, step)
        copy = rcopy(csend.at[s], dst.at[s], z.slot_core[name][s], mate)
        busy[("c", s)] = [send(copy, late=False)]

    def core_wait(s, name, dst):
        rcopy(dst.at[s], dst.at[s], z.slot_core[name][s], mate).wait_recv()

    def chip_part(s, name, got, dst, hold=False):
        core_wait(s, name, got)
        ysend[s] = (ysend[s].astype(F32) + got[s].astype(F32)).astype(BF)
        copies = [
            rcopy(ysend.at[s], dst.at[s, dy - 1], z.slot_y[name][s] + dy - 1, y_dev(dy)) for dy in range(1, Y)
        ]
        start_all(("y", s), copies, hold)

    def start_all(key, copies, hold):
        busy[key] = copies

        def go():
            for copy in copies:
                copy.start()
        if hold:
            held.append(go)
        else:
            go()

    def chip_share(s, name, got, dst, buf, key, hold=False):
        core_wait(s, name, got)
        buf[s] = (buf[s].astype(F32) + got[s].astype(F32)).astype(BF)
        copies = [
            rcopy(
                buf.at[s, :, lanes(lax.rem(y + dy, Y) * Dy, Dy)], dst.at[s, dy - 1],
                z.slot_y[name][s] + dy - 1, y_dev(dy),
            )
            for dy in range(1, Y)
        ]
        start_all((key, s), copies, hold)

    def y_wait(s, name, dst):
        for dy in range(1, Y):
            got = dst.at[s, dy - 1]
            rcopy(got, got, z.slot_y[name][s] + dy - 1, mate).wait_recv()

    def own_share(s, buf, dst):
        total = buf[s, :, lanes(y * Dy, Dy)].astype(F32)
        for dy in range(1, Y):
            total = total + dst[s, dy - 1].astype(F32)
        return total

    hid = r["hid"]
    cr1, cr2, cr3, yr1, yr2, yr3, yrO = (r[n] for n in ("cr1", "cr2", "cr3", "yr1", "yr2", "yr3", "yrO"))

    def norm_two(s):
        y_wait(s, "branch", yr1)
        gain, shift, bias = vector(3, slice(0, D)), vector(4, slice(0, D)), vector(2, slice(0, D))

        def step(i):
            lr = rows16(i * 16, 16)
            h = ysend[s, lr, :].astype(F32)
            for dy in range(Y - 1):
                h = h + yr1[s, dy, lr, :].astype(F32)
            gr = rows16(s * R + c * HR + i * 16, 16)
            h = tokF[gr, :].astype(F32) + (h + bias)
            hid[rows16(s * HR + i * 16, 16), :] = h
            mu, inv = stats(h)
            n2[gr, :] = ((h - mu) * inv * gain + shift).astype(BF)
        loop(HR // 16, step, True)
        part = n2.at[own(s)]
        busy[("n", s)] = [send(rcopy(part, part, z.slot_core["n2"][s], mate), late=False)]
        yc = lanes(y * Dy, Dy)
        ebuf[s] = hid[s * HR:s * HR + HR, yc] + r["vec"][5:6, yc]

    gp = r["gp"]
    UC = min(256, F)
    root = 0.5 ** 0.5
    dens = (2.0 * 3.141592653589793) ** -0.5

    def up(s):
        part = n2.at[theirs(s)]
        rcopy(part, part, z.slot_core["n2"][s], mate).wait_recv()
        x = n2[s * R:s * R + R, :]

        def column(j):
            cols = lanes(j * UC, UC)
            ubuf[...] = dot(x, W[2][:, cols]) + r["vec"][6:7, cols]

            def step(i):
                lr = rows16(i * 32, 32)
                gr = rows16(s * R + i * 32, 32)
                u = ubuf[lr, :]
                phi = 0.5 * lax.erf(u * root) + 0.5
                na[gr, cols] = (u * phi).astype(BF)
                gp[gr, cols] = (phi + u * (jnp.exp(-0.5 * u * u) * dens)).astype(BF)
            loop(R // 32, step)
        loop(F // UC, column)

    def back_up(s):
        x = feedF[s * R:s * R + R, :]

        def column(j):
            cols = lanes(j * 256, 256)
            ga = dot(x, W[3][:, cols])
            gp[s * R:s * R + R, cols] = (ga * gp[s * R:s * R + R, cols].astype(F32)).astype(BF)
        loop(F // 256, column)

    obuf, ebuf, lo, ig = r["obuf"], r["ebuf"], r["loP"], r["igP"]

    def layer_out(s):
        y_wait(s, "out", yrO)
        total = own_share(s, r["ysO"], yrO)
        obuf[s] = (total + ebuf[s]).astype(BF)
        swap_out(s, obuf, lo, "lo")

    def put_half(which, write):
        for half in range(2):
            size = min(HR, z.SEQ - half * HR)
            rows = slice(half * HR, half * HR + size)
            pl.when(which == half)(functools.partial(write, rows, size))

    def swap_out(s, buf, got, name):
        send(rcopy(buf.at[s, :, lanes((1 - c) * Dm, Dm)], got.at[s], z.slot_core[name][s], mate))

    def take_out(s, got, name):
        dst = got.at[s]
        rcopy(dst, dst, z.slot_core[name][s], mate).wait_recv()

    def put_layer(which, buf, cols):
        def write(rows, size):
            out = [buf[s, 0:size, cols].astype(F32) * r["flags"][s].astype(F32) for s in range(NS)]
            r["lo"][rows] = jnp.stack([x.astype(BF) for x in out], axis=1)
        put_half(which, write)

    def put_grad(s, which, buf, cols):
        def write(rows, size):
            r["ig"][rows, s, :] = buf[s, 0:size, cols]
        put_half(which, write)

    na_act = na.at[:, 0:F]
    gb, gatt, gj, acc, gvl = r["gb"], r["gatt"], r["gj"], r["acc"], r["gvl"]

    def norm_two_back(s):
        y_wait(s, "gn2", yr2)
        let_go()
        gain = vector(3, slice(0, D))

        def step(i, sums):
            lr = rows16(i * 16, 16)
            e = ysend[s, lr, :].astype(F32)
            for dy in range(Y - 1):
                e = e + yr2[s, dy, lr, :].astype(F32)
            hr = rows16(s * HR + i * 16, 16)
            gr = rows16(s * R + c * HR + i * 16, 16)
            h = hid[hr, :]
            mu, inv = stats(h)
            xhat = (h - mu) * inv
            t = e * gain
            m1 = jnp.sum(t, axis=1, keepdims=True) * (1.0 / D)
            m2 = jnp.sum(t * xhat, axis=1, keepdims=True) * (1.0 / D)
            g = feedF[gr, :].astype(F32) + inv * (t - m1 - xhat * m2)
            hid[hr, :] = g
            g = g.astype(BF)
            gb[gr, :] = g
            g = g.astype(F32)
            ex = e * xhat
            fold = lambda m: m[0:8] + m[8:16]
            return (sums[0] + fold(ex), sums[1] + fold(e), sums[2] + fold(g))
        zero = jnp.zeros((8, D), F32)
        sums = lax.fori_loop(0, HR // 16, step, (zero, zero, zero), unroll=True)
        for i in range(3):
            acc[i] = sums[i] if s == 0 else acc[i] + sums[i]
        part = gb.at[own(s)]
        send(rcopy(part, part, z.slot_core["gb"][s], mate))

    def attend_back_start(s):
        part = gb.at[theirs(s)]
        rcopy(part, part, z.slot_core["gb"][s], mate).wait_recv()
        gatt[...] = dot(gb[s * R:s * R + R, :], W[1][...]).astype(BF)

    def attend_back(s, pr):
        cc = lanes(pr * 128, 128)
        rr = slice(s * R, s * R + R)
        kp = k[rr, cc]
        vp = v[rr, cc]
        kt = kp.T
        dk = jnp.zeros((R, 128), F32)
        dv = jnp.zeros((R, 128), F32)
        for (c0, cw) in chunks:
            qp = q[s * R + c0:s * R + c0 + cw, cc]
            go = gatt[c0:c0 + cw, cc]
            parts = []
            for e in range(2):
                qm, gm = half_mask(qp, e), half_mask(go, e)
                sc = mask_keys(dot_nt(kp, qm))
                soft = jnp.exp(sc - lse[(s * z.NP + pr) * 2 + e, :, c0:c0 + cw])
                dv = dv + dot(soft.astype(BF), gm)
                gs = dot_nt(vp, gm)
                delta = jnp.sum(gs * soft, axis=0, keepdims=True)
                ds = (soft * (gs - delta)).astype(BF)
                dk = dk + dot(ds, qm)
                parts.append(dot(kt[e * HD:(e + 1) * HD], ds))
            dq = jnp.concatenate(parts, axis=0) * (HD ** -0.5)
            gj[s * R + c0:s * R + c0 + cw, lanes(pr * 128, 128)] = dq.T.astype(BF)
        gj[rr, lanes(HW + pr * 128, 128)] = dk.astype(BF)
        gj[rr, lanes(2 * HW + pr * 128, 128)] = dv.astype(BF)

    stat, statT, statR = r["stat"], r["statT"], r["statR"]

    def norm_one_sums(s):
        y_wait(s, "gn1", yr3)
        ebuf[s] = own_share(s, ysend, yr3)
        yc = lanes(y * Dy, Dy)
        gain = vector(0, yc)

        def step(i, sums):
            lr = rows16(i * 16, 16)
            gr = rows16(s * R + c * HR + i * 16, 16)
            mu, inv = stats(tokF[gr, :].astype(F32))
            xhat = (tokF[gr, yc].astype(F32) - mu) * inv
            e = ebuf[s, lr, :]
            t = e * gain
            s1 = jnp.sum(t, axis=1, keepdims=True)
            s2 = jnp.sum(t * xhat, axis=1, keepdims=True)
            lane = lax.broadcasted_iota(jnp.int32, (16, 128), 1)
            stat[lr, :] = jnp.where(lane == 0, s1, jnp.where(lane == 1, s2, 0.0))
            ex = e * xhat
            fold = lambda m: m[0:8] + m[8:16]
            return (sums[0] + fold(ex), sums[1] + fold(e))
        zero = jnp.zeros((8, Dy), F32)
        sums = lax.fori_loop(0, HR // 16, step, (zero, zero), unroll=True)
        for i in range(2):
            row = jnp.sum(sums[i], axis=0, keepdims=True)
            gvl[i:i + 1, yc] = row if s == 0 else gvl[i:i + 1, yc] + row
        statT[s] = stat[...].T[0:8]
        for dy in range(1, Y):
            send(rcopy(statT.at[s], statR.at[s, dy - 1], z.slot_y["st"][s] + dy - 1, y_dev(dy)))

    def norm_one_back(s):
        y_wait(s, "st", statR)
        total = statT[s]
        for dy in range(Y - 1):
            total = total + statR[s, dy]
        total = jnp.concatenate([total, jnp.zeros((120, HR), F32)], axis=0)
        stat[...] = total.T * (1.0 / D)
        yc = lanes(y * Dy, Dy)
        gain = vector(0, yc)

        def step(i):
            lr = rows16(i * 16, 16)
            gr = rows16(s * R + c * HR + i * 16, 16)
            mu, inv = stats(tokF[gr, :].astype(F32))
            xhat = (tokF[gr, yc].astype(F32) - mu) * inv
            t = ebuf[s, lr, :] * gain
            st = stat[lr, :]
            m1, m2 = st[:, 0:1], st[:, 1:2]
            g = hid[rows16(s * HR + i * 16, 16), yc]
            ebuf[s, lr, :] = g + inv * (t - m1 - xhat * m2)
        loop(HR // 16, step, True)
        swap_out(s, ebuf, ig, "ig")
        put_grad(s, c, ebuf, lanes(c * Dm, Dm))

    G = [r["G3"].at[:, 0:3 * HW], r["G1"], r["G2"], r["G3"]]
    RX = [r[f"RX{p}"] for p in range(4)]
    Z = [r[f"Z{p}"] for p in range(4)]
    outs = [r[f"o{p}"] for p in range(4)]

    def weight_grad(p, x, g, s=None):
        rows = slice(None) if s is None else slice(s * R, s * R + R)

        def step(i):
            rr = pl.ds(pl.multiple_of(i * 256, 256), 256)
            part = dot_tn(x[rows, lanes(i * 256, 256)], g[rows, :])
            if s:
                part = part + G[p][rr, :].astype(F32)
            G[p][rr, :] = part.astype(BF)
        loop(D // 256, step)

    def gblock(p, blk):
        return rows16(blk * RB, RB)

    def rs_send(p, copy):
        busy.setdefault(("g", p), []).append(send(copy, late=False))

    def rs_cross(i):
        p, first, width = z.scatters[i]
        cols = pl.ds(first, width)
        for db in range(1, B):
            bd = lax.rem(b + db, B)
            for aa in range(A):
                rs_send(p, rcopy(
                    G[p].at[gblock(p, aa * B + bd), cols], RX[p].at[db - 1, aa, :, cols],
                    z.rs_x[i] + (db - 1) * A + aa, b_dev(db),
                ))

    def pump():
        while waiting and len(flying) < 3:
            flying.append(waiting.pop(0))
            rs_cross(flying[-1])

    def rs_add(i):
        p, first, width = z.scatters[i]
        cols = pl.ds(first, width)
        for db in range(1, B):
            for aa in range(A):
                dst = RX[p].at[db - 1, aa, :, cols]
                rcopy(dst, dst, z.rs_x[i] + (db - 1) * A + aa, mate).wait_recv()
        flying.remove(i)
        pump()
        if B > 1:
            def step(aa):
                rr = gblock(p, aa * B + b)
                total = G[p][rr, cols].astype(F32)
                for db in range(B - 1):
                    total = total + RX[p][db, aa, :, cols].astype(F32)
                G[p][rr, cols] = total.astype(BF)
            loop(A, step)

        for da in range(1, A):
            rr = gblock(p, lax.rem(a + da, A) * B + b)
            rs_send(p, rcopy(G[p].at[rr, cols], Z[p].at[da - 1, :, cols], z.rs_z[i] + da, a_dev(da)))

    def rs_done(i):
        p, first, width = z.scatters[i]
        finished.append(i)
        cols = pl.ds(first, width)
        total = G[p][gblock(p, dpi), cols].astype(F32)
        for da in range(1, A):
            dst = Z[p].at[da - 1, :, cols]
            rcopy(dst, dst, z.rs_z[i] + da, mate).wait_recv()
            total = total + Z[p][da - 1, :, cols].astype(F32)
        if p == 0:
            for t in range(first // HW, (first + width - 1) // HW + 1):
                low, high = max(first, t * HW), min(first + width, (t + 1) * HW)
                outs[0][t, :, low - t * HW:high - t * HW] = total[:, low - first:high - first]
        elif p in (1, 3):
            outs[p][cols, :] = total.T
        else:
            outs[p][:, cols] = total

    def rs_groups():
        count = len(z.scatters)
        groups = []
        for i in range(count):
            group = [functools.partial(rs_add, i)]
            if i >= 2:
                group.append(functools.partial(rs_done, i - 2))
            groups.append((i, group))
        return groups + [(None, [functools.partial(rs_done, i)]) for i in range(max(count - 2, 0), count)]

    def cross_part(part):
        waiting.extend(i for i, piece in enumerate(z.scatters) if piece[0] == part)
        pump()

    first_pieces, second = of_part(0), of_part(1)
    order = first_pieces + second + of_part(2) + of_part(3)
    begun = []

    def ag_next():
        if len(begun) < len(order):
            ag_start(order[len(begun)])
            begun.append(1)

    small_in()
    small_send(0)
    place_weights(0)
    ag_next()
    ag_next()
    place_rows(0)
    small_take(0)
    small_send(1)
    rows_start(0)
    for p in range(1, 4):
        place_weights(p)
    for t in range(1, 2 * NS):
        place_rows(t)
    ag_near(order[0])
    ag_next()
    small_take(1)
    small_spread()
    ag_near(order[1])
    ag_next()
    ag_far(order[0])
    rows_relay(0)
    for t in range(1, NS):
        rows_start(t)
    ag_near(order[2])
    ag_next()
    ag_far(order[1])
    rows_done(0)
    norm_one(0, na)
    ag_near(order[3])
    ag_next()
    ag_far(order[2])
    for t in range(1, NS):
        rows_relay(t)
    for t in range(NS, 2 * NS):
        rows_start(t)
    ag_far(order[3])
    for i in first_pieces:
        ag_done(i)
    for i in order[4:]:
        ticks += [(None, [functools.partial(ag_near, i), ag_next]), (None, [functools.partial(ag_far, i)])]
    for s in range(NS):
        if s > 0:
            rows_done(s)
            norm_one(s, na)
        project(s)
        tick()
        for pr in range(z.NP):
            attend(s, pr)
            if s == 0 or pr == 0:
                tick()
        if s == 0:
            for i in second:
                ag_done(i)
        core_part(s, "branch", att, W[1], cr1, ysend, "y")
        if s == 0:
            tick()
        chip_part(s, "branch", cr1, yr1)
    while ticks:
        tick()
    for t in range(NS, 2 * NS):
        rows_relay(t)
    for s in range(NS):
        norm_two(s)
        if s == 0:
            for i in of_part(2):
                ag_done(i)
            for t in range(NS, 2 * NS):
                rows_done(t)
        up(s)
        weight_grad(3, feedF, na_act, s)
    cross_part(3)
    for i in of_part(3):
        ag_done(i)
    for s in range(NS):
        back_up(s)
        if s > 0:
            chip_part(s - 1, "gn2", cr2, yr2)
        core_part(s, "gn2", gp, W[2], cr2, ysend, "y")
    chip_part(NS - 1, "gn2", cr2, yr2, True)
    ticks += rs_groups()
    weight_grad(2, n2, gp)
    cross_part(2)
    tick()
    gvl[...] = jnp.zeros_like(gvl)
    ones_row = jnp.ones((8, z.ROWS), BF)
    gvl[5:6, lanes(mpi * Dm, Dm)] = dot(ones_row, feedF[:, lanes(mpi * Dm, Dm)])[0:1]
    gvl[6:7, 0:F] = dot(ones_row, gp[...])[0:1]
    for s in range(NS):
        core_part(s, "out", na_act, W[3], cr1, r["ysO"], "o")
    tick()
    for s in range(NS):
        free(("n", s))
        norm_one(s, n2)
    for s in range(NS):
        norm_two_back(s)
        if s == NS - 1:
            for t in range(NS):
                chip_share(t, "out", cr1, yrO, r["ysO"], "o")
        tick()
        attend_back_start(s)
        if s == NS - 1:
            weight_grad(1, gb, att)
            cross_part(1)
        for pr in range(z.NP):
            attend_back(s, pr)
            tick()
        core_part(s, "gn1", gj, W[0], cr3, ysend, "y")
        if s == 0:
            while any(piece[0] == 3 and i not in finished for i, piece in enumerate(z.scatters)):
                tick()
            free(("g", 3))
        weight_grad(0, n2, gj, s)
        if s < NS - 1:
            chip_share(s, "gn1", cr3, yr3, ysend, "y", True)
    cross_part(0)
    chip_share(NS - 1, "gn1", cr3, yr3, ysend, "y")
    tick()
    for s in range(NS):
        layer_out(s)
    put_layer(c, obuf, lanes(c * Dm, Dm))
    tick()
    gvl[7:8, 0:HW] = dot(ones_row, gj[:, 0:HW])[0:1]
    gvl[7:8, HW:2 * HW] = dot(ones_row, gj[:, 2 * HW:3 * HW])[0:1]
    yc = lanes(y * Dy, Dy)
    for row, i in ((3, 0), (4, 1), (2, 2)):
        gvl[row:row + 1, yc] = jnp.sum(acc[i, :, yc], axis=0, keepdims=True)
    for s in range(NS):
        norm_one_sums(s)
        if s == 0:
            for t in range(NS):
                take_out(t, lo, "lo")
            put_layer(1 - c, lo, slice(None))
        tick()
    sums_start()
    for s in range(NS):
        norm_one_back(s)
        if s == 0:
            sums_cross()
        tick()
    sums_done()
    while ticks:
        tick()
    for s in range(NS):
        take_out(s, ig, "ig")
        put_grad(s, 1 - c, ig, slice(None))
    for key in list(busy):
        free(key)
    for cond, copy in pending:
        when(cond, lambda copy=copy: copy.wait_send())


def body(mesh, tokens, slot_flags, cotangent, attend_gain, attend_shift, input_weight, input_bias,
         output_weight, output_bias, dense_gain, dense_shift, up_weight, up_bias, down_weight, down_bias):
    tokens, cotangent = tokens.transpose(1, 0, 2), cotangent.transpose(1, 0, 2)
    z = Sizes(mesh, tokens, input_weight, up_weight)
    small = (attend_gain, attend_shift, output_bias, dense_gain, dense_shift, down_bias, up_bias.T, input_bias)
    shapes = [
        jax.ShapeDtypeStruct(tokens.shape, BF),
        jax.ShapeDtypeStruct(tokens.shape, F32),
        jax.ShapeDtypeStruct((3, z.RB, z.HW), F32),
        jax.ShapeDtypeStruct(output_weight.shape, F32),
        jax.ShapeDtypeStruct(up_weight.shape, F32),
        jax.ShapeDtypeStruct(down_weight.shape, F32),
        jax.ShapeDtypeStruct((6,) + attend_gain.shape, F32),
    ] + [jax.ShapeDtypeStruct(x.shape, F32) for x in small[6:]]
    vmem = pl.BlockSpec(memory_space=pltpu.VMEM)
    smem = pl.BlockSpec(memory_space=pltpu.SMEM)
    lo, ig, g0, g1, g2, g3, gd, gu, gi = pl.pallas_call(
        functools.partial(kernel, z),
        out_shape=shapes,
        in_specs=[vmem, vmem, smem] + [vmem] * 12,
        out_specs=[vmem] * 9,
        scratch_shapes=scratch_shapes(z),
        compiler_params=pltpu.CompilerParams(
            collective_id=0, has_side_effects=True, vmem_limit_bytes=VMEM_LIMIT
        ),
        name="layer",
    )(
        tokens, cotangent, slot_flags, input_weight.transpose(1, 0, 2), output_weight, up_weight, down_weight,
        *small,
    )
    layer_rows = lo.transpose(1, 0, 2)
    input_grad = ig.transpose(1, 0, 2)
    return (
        layer_rows, input_grad, gd[0], gd[1], g0.transpose(1, 0, 2), gi, g1, gd[2], gd[3], gd[4],
        g2, gu.T, g3, gd[5],
    )


VMEM_LIMIT = 63 * 2**20


def solution(mesh):
    rows = P("dp", None, "mp")
    vec = P("mp", "dp")
    pair = P(None, "mp", "dp")
    return jax.shard_map(
        functools.partial(body, mesh),
        mesh=mesh,
        in_specs=(rows, P("dp"), rows, vec, vec, rows, pair, vec, vec, vec, vec, P("dp", "mp"), vec, vec, vec),
        out_specs=(rows, rows, vec, vec, rows, pair, vec, vec, vec, vec, P("dp", "mp"), vec, vec, vec),
        check_vma=False,
    )
```

```python
import functools

import jax
import jax.numpy as jnp
from jax import lax
from jax.experimental import pallas as pl
from jax.experimental.pallas import tpu as pltpu
from jax.sharding import PartitionSpec as P

HD = 64
EPS = 1e-06
MESH = pl.DeviceIdType.MESH
BF = jnp.bfloat16
F32 = jnp.float32


def dot(left, right):
    return jnp.dot(left, right, preferred_element_type=F32)


def dot_nt(left, right):
    return lax.dot_general(left, right, (((1,), (1,)), ((), ())), preferred_element_type=F32)


def dot_tn(left, right):
    return lax.dot_general(left, right, (((0,), (0,)), ((), ())), preferred_element_type=F32)


class Ids:
    def __init__(self):
        self.count = 0

    def take(self, number):
        first = self.count
        self.count += number
        return first


class Sizes:
    def __init__(self, mesh, tokens, input_weight, up_weight):
        dp, mp = mesh.shape["dp"], mesh.shape["mp"]
        self.dp, self.mp = dp, mp
        self.A = 4 if dp % 4 == 0 else dp
        self.B = dp // self.A
        self.Y = mp // 2
        self.SEQ, self.NS, self.Dm = tokens.shape
        self.R = -(-self.SEQ // 32) * 32
        self.HR = self.R // 2
        self.ROWS = self.NS * self.R
        self.D = self.Dm * mp
        self.Dy = 2 * self.Dm
        self.RB = input_weight.shape[0]
        self.HW = input_weight.shape[2]
        self.NP = self.HW // 128
        self.F = up_weight.shape[1]
        self.VW = max(self.D, self.F, 2 * self.HW)
        self.wide = HD // dp
        heads = self.D // mp // HD
        self.groups = [heads] * 6 + [self.F // HD, 2 * self.HW // HD]
        self.NR = sum(self.groups)
        self.cols = (3 * self.HW, self.HW, self.F, self.F)
        ids = Ids()
        A, B, Y, NS = self.A, self.B, self.Y, self.NS
        self.gathers = self.cut(((0, 256), (1, 256), (2, 512), (3, 512)))
        self.scatters = self.cut(((3, 256), (2, 256), (1, 256), (0, 256)))
        self.ag_z = [ids.take(6) for _ in self.gathers]
        self.ag_x = [ids.take((B - 1) * A) for _ in self.gathers]
        self.rs_z = [ids.take(A) for _ in self.scatters]
        self.rs_x = [ids.take((B - 1) * A) for _ in self.scatters]
        self.rows_c = [ids.take(1) for _ in range(2 * NS)]
        self.rows_y = [ids.take(Y) for _ in range(2 * NS)]
        self.rows_f = [ids.take(Y) for _ in range(2 * NS)]
        self.vec_ids = [[ids.take(dp), ids.take(mp)] for _ in range(2)]
        self.slot_core = {
            name: [ids.take(1) for _ in range(NS)]
            for name in ("branch", "n2", "out", "lo", "gn2", "gb", "gn1", "ig")
        }
        self.slot_y = {
            name: [ids.take(Y) for _ in range(NS)] for name in ("branch", "out", "gn2", "gn1", "st")
        }
        self.nsem = ids.count

    def cut(self, widths):
        return [
            (p, first, min(width, self.cols[p] - first))
            for p, width in widths
            for first in range(0, self.cols[p], width)
        ]


SCRATCH = (
    "tokF", "feedF", "W0", "W1", "W2", "W3", "na", "q", "k", "v", "att", "csend", "cr1", "ysend", "ysO", "yr1",
    "yrO", "hid", "n2", "gp", "cr2", "yr2", "gb", "gatt", "gj", "cr3", "yr3", "ebuf", "obuf", "stat", "statT",
    "statR", "ubuf", "lse", "G1", "G2", "G3", "RX0", "RX1", "RX2", "RX3", "Z0", "Z1", "Z2", "Z3",
    "acc", "gvl", "prm", "big", "vec", "vall", "vgo", "vgm", "vgc", "vgA", "igP", "ss", "rs",
)
OPERANDS = (
    "tokens", "cot", "flags", "iw", "ow", "uw", "dw", "p0", "p1", "p2", "p3", "p4", "p5", "pu", "pi",
    "lo", "ig", "o0", "o1", "o2", "o3", "qd", "qu", "qi",
)


def scratch_shapes(z):
    A, B, Y, NS = z.A, z.B, z.Y, z.NS
    V = pltpu.VMEM
    half = (NS, z.HR, z.D)
    shapes = dict(
        tokF=V((z.ROWS, z.D), BF),
        feedF=V((z.ROWS, z.D), BF),
        na=V((z.ROWS, max(z.D, z.F)), BF),
        q=V((z.ROWS, z.HW), BF),
        k=V((z.ROWS, z.HW), BF),
        v=V((z.ROWS, z.HW), BF),
        att=V((z.ROWS, z.HW), BF),
        csend=V(half, BF),
        cr1=V(half, BF),
        ysend=V(half, BF),
        ysO=V(half, BF),
        yr1=V((NS, Y - 1, z.HR, z.D), BF),
        yrO=V((NS, Y - 1, z.HR, z.Dy), BF),
        hid=V((NS * z.HR, z.D), F32),
        n2=V((z.ROWS, z.D), BF),
        gp=V((z.ROWS, z.F), BF),
        cr2=V(half, BF),
        yr2=V((NS, Y - 1, z.HR, z.D), BF),
        gb=V((z.ROWS, z.D), BF),
        gatt=V((z.R, z.HW), BF),
        gj=V((z.ROWS, 3 * z.HW), BF),
        cr3=V(half, BF),
        yr3=V((NS, Y - 1, z.HR, z.Dy), BF),
        ebuf=V((NS, z.HR, z.Dy), F32),
        obuf=V((NS, z.HR, z.Dy), BF),
        stat=V((z.HR, 128), F32),
        statT=V((NS, 8, z.HR), F32),
        statR=V((NS, Y - 1, 8, z.HR), F32),
        ubuf=V((z.R, min(256, z.F)), F32),
        lse=V((NS * 2 * z.NP, 1, z.R), F32),
        vec=V((8, z.VW), F32),
        vall=V((z.mp, z.dp, 8, 128), F32),
        vgo=V((z.dp, 8, 128), F32),
        vgm=V((z.dp, 8, 128), F32),
        vgc=V((z.dp, 8, 128), F32),
        vgA=V((z.dp, 8, 128), F32),
        igP=V((NS, z.HR, z.Dm), F32),
        acc=V((3, 8, z.D), F32),
        gvl=V((8, z.VW), F32),
        prm=V((128, 128), F32),
        big=V((z.NR, z.VW), F32),
        ss=pltpu.SemaphoreType.DMA((z.nsem,)),
        rs=pltpu.SemaphoreType.DMA((z.nsem,)),
    )
    for p, cols in enumerate(z.cols):
        shapes[f"W{p}"] = V((z.D, cols), BF)
        if p > 0:
            shapes[f"G{p}"] = V((z.D, max(cols, z.cols[0]) if p == 3 else cols), BF)
        shapes[f"RX{p}"] = V((max(B - 1, 1), A, z.RB, cols), BF)
        shapes[f"Z{p}"] = V((A - 1, z.RB, cols), BF)
    return [shapes[name] for name in SCRATCH]


def kernel(z, *refs):
    r = dict(zip(OPERANDS + SCRATCH, refs))
    A, B, Y, NS, R, HR, D, Dm, Dy, HW, F, RB = (
        z.A, z.B, z.Y, z.NS, z.R, z.HR, z.D, z.Dm, z.Dy, z.HW, z.F, z.RB,
    )
    ss, rs = r["ss"], r["rs"]
    dpi, mpi = lax.axis_index("dp"), lax.axis_index("mp")
    a, b = dpi // B, dpi % B
    y, c = mpi // 2, mpi % 2

    def dev(a=a, b=b, y=y, c=c):
        return (a * B + b, y * 2 + c)

    def rcopy(src, dst, i, device):
        return pltpu.make_async_remote_copy(
            src_ref=src, dst_ref=dst, send_sem=ss.at[i], recv_sem=rs.at[i],
            device_id=device, device_id_type=MESH,
        )

    def when(cond, f):
        if cond is True:
            f()
        elif cond is not False:
            pl.when(cond)(f)

    pending = []

    def send(copy, cond=True, late=True):
        when(cond, lambda: copy.start())
        if late:
            pending.append((cond, copy))
        return copy

    mate = dev(c=1 - c)

    def y_dev(dy):
        return dev(y=lax.rem(y + dy, Y))

    def b_dev(db):
        return dev(b=lax.rem(b + db, B))

    def a_dev(da):
        return dev(a=lax.rem(a + da, A))

    def rows16(start, size):
        return pl.ds(pl.multiple_of(start, 16), size)

    def lanes(start, size):
        return pl.ds(pl.multiple_of(start, 128), size)

    def loop(n, f, unroll=1):
        def step(i, carry):
            f(i)
            return carry
        lax.fori_loop(0, n, step, 0, unroll=unroll)

    bar = pltpu.get_barrier_semaphore()
    def dp_dev(d):
        return (lax.rem(dpi + d, z.dp), mpi)

    def mp_dev(d):
        return (dpi, lax.rem(mpi + d, z.mp))

    friends = [dp_dev(d) for d in range(1, z.dp)] + [mp_dev(d) for d in range(1, z.mp)]
    for friend in friends:
        pl.semaphore_signal(bar, inc=1, device_id=friend, device_id_type=MESH)
    pl.semaphore_wait(bar, len(friends))

    W = [r[f"W{p}"] for p in range(4)]
    own_w = rows16(dpi * RB, RB)

    def place_weights(p):
        if p == 0:
            for t in range(3):
                W[0][own_w, t * HW:(t + 1) * HW] = r["iw"][t]
        elif p == 2:
            W[2][own_w, :] = r["uw"][...]
        else:
            W[p][own_w, :] = r["ow" if p == 1 else "dw"][...].T

    def wblock(p, blk, first, width):
        return W[p].at[rows16(blk * RB, RB), pl.ds(first, width)]

    def line_dev(step):
        return dev(a=jnp.clip(a + step, 0, A - 1))

    def ag_cross(i, src, blk_a, cond):
        p, first, width = z.gathers[i]
        dst = wblock(p, blk_a * B + b, first, width)
        for db in range(1, B):
            send(rcopy(src, dst, z.ag_x[i] + (db - 1) * A + blk_a, b_dev(db)), cond)

    def ag_start(i):
        p, first, width = z.gathers[i]
        own_block = src = wblock(p, dpi, first, width)
        ag_cross(i, src, a, True)
        send(rcopy(src, own_block, z.ag_z[i], line_dev(1)), a + 1 < A)
        send(rcopy(src, own_block, z.ag_z[i] + 1, line_dev(-1)), a >= 1)
        send(rcopy(src, own_block, z.ag_z[i] + 2, line_dev(2)), a + 2 < A)
        send(rcopy(src, own_block, z.ag_z[i] + 3, line_dev(-2)), a >= 2)

    def ag_take(i, kind, step, relay=None):
        p, first, width = z.gathers[i]
        there = (a + step >= 0) if step < 0 else (a + step < A)
        src_a = jnp.clip(a + step, 0, A - 1)
        blk = wblock(p, src_a * B + b, first, width)
        when(there, lambda: rcopy(blk, blk, z.ag_z[i] + kind, mate).wait_recv())
        if relay is not None:
            go = there & ((a + relay < A) if relay > 0 else (a + relay >= 0))
            send(rcopy(blk, blk, z.ag_z[i] + kind + 2, line_dev(relay)), go)
        ag_cross(i, blk, src_a, there)

    def ag_near(i):
        ag_take(i, 0, -1)
        ag_take(i, 1, 1)
        ag_take(i, 2, -2, 1)
        ag_take(i, 3, 2, -1)

    def ag_far(i):
        ag_take(i, 4, -3)
        ag_take(i, 5, 3)

    def ag_done(i):
        p, first, width = z.gathers[i]
        for db in range(1, B):
            bs = lax.rem(b + B - db, B)
            for aa in range(A):
                blk = wblock(p, aa * B + bs, first, width)
                rcopy(blk, blk, z.ag_x[i] + (db - 1) * A + aa, mate).wait_recv()

    def of_part(p):
        return [i for i, piece in enumerate(z.gathers) if piece[0] == p]

    full = [r["tokF"], r["feedF"]]

    def place_rows(t):
        s = t % NS
        src = r["tokens"] if t < NS else r["cot"]
        keep = 1.0 if t < NS else r["flags"][s].astype(F32)
        cols = lanes(mpi * Dm, Dm)
        head = z.SEQ // 16 * 16
        full[t // NS][s * R:s * R + head, cols] = (src[0:head, s, :].astype(F32) * keep).astype(BF)
        last = jnp.broadcast_to(src[head:z.SEQ, s, :].astype(F32) * keep, (R - head, Dm))
        row = lax.broadcasted_iota(jnp.int32, (R - head, Dm), 0)
        full[t // NS][s * R + head:s * R + R, cols] = jnp.where(row < z.SEQ - head, last, 0.0).astype(BF)

    def mblock(t, m):
        return full[t // NS].at[pl.ds(t % NS * R, R), lanes(m * Dm, Dm)]

    def rows_start(t):
        src = mblock(t, mpi)
        for dy in range(1, Y):
            send(rcopy(src, src, z.rows_y[t] + dy, y_dev(dy)))
        send(rcopy(src, src, z.rows_c[t], mate))

    def rows_relay(t):
        for dy in range(1, Y):
            blk = mblock(t, lax.rem(y + Y - dy, Y) * 2 + c)
            rcopy(blk, blk, z.rows_y[t] + dy, mate).wait_recv()
            send(rcopy(blk, blk, z.rows_f[t] + dy, mate))

    def rows_done(t):
        blk = mblock(t, y * 2 + 1 - c)
        rcopy(blk, blk, z.rows_c[t], mate).wait_recv()
        for dy in range(1, Y):
            blk = mblock(t, lax.rem(y + Y - dy, Y) * 2 + 1 - c)
            rcopy(blk, blk, z.rows_f[t] + dy, mate).wait_recv()

    vall, prm = r["vall"], r["prm"]

    def spread(kind):
        lane = lax.broadcasted_iota(jnp.int32, (z.dp * 8, z.VW), 1)
        row = lax.broadcasted_iota(jnp.int32, (z.dp * 8, z.VW), 0)
        part = row & 7
        hit = ((lane & (HD - 1)) == (row >> 3) * z.wide + part) & (part < z.wide)
        return jnp.where(hit, 1.0, 0.0).astype(kind)

    def heads_mask(m, mine, count):
        row = lax.broadcasted_iota(jnp.int32, (count, z.VW), 0)
        lane = lax.broadcasted_iota(jnp.int32, (count, z.VW), 1)
        first, head = 0, row
        for p, n in enumerate(z.groups):
            this = row - first
            head = jnp.where(row >= first, this + m * n if p < 6 else jnp.where(mine, this, -1), head)
            first += n
        return (lane >> 6) == jnp.where(row < first, head, -1)

    def small_in():
        prm[...] = jnp.zeros_like(prm)
        first = 0
        for p in range(6):
            prm[first:first + z.groups[p], 0:z.wide] = r[f"p{p}"][...].astype(F32)
            first += z.groups[p]
        prm[first:first + z.groups[6], 0:z.wide] = r["pu"][...].astype(F32).T
        first += z.groups[6]
        for t in range(2):
            half = z.groups[7] // 2
            prm[first + t * half:first + (t + 1) * half, 0:z.wide] = r["pi"][t].astype(F32)
        vall[mpi, dpi] = prm[...].T[0:8]

    def small_send(stage):
        blk = vall.at[mpi] if stage else vall.at[mpi, dpi]
        for d in range(1, (z.dp, z.mp)[stage]):
            send(rcopy(blk, blk, z.vec_ids[0][stage] + d, (dp_dev, mp_dev)[stage](d)))

    def small_take(stage):
        for d in range(1, (z.dp, z.mp)[stage]):
            if stage:
                blk = vall.at[lax.rem(mpi + z.mp - d, z.mp)]
            else:
                blk = vall.at[mpi, lax.rem(dpi + z.dp - d, z.dp)]
            rcopy(blk, blk, z.vec_ids[0][stage] + d, mate).wait_recv()

    def small_spread():
        ones = spread(BF)
        total = jnp.zeros((128, z.VW), F32)
        for m in range(z.mp):
            rows = dot_tn(vall[m].reshape(z.dp * 8, 128).astype(BF), ones)
            total = total + jnp.where(heads_mask(m, m == mpi, 128), rows, 0.0)
        p = lax.broadcasted_iota(jnp.int32, (8, 128), 0)
        row = lax.broadcasted_iota(jnp.int32, (8, 128), 1)
        first, group = 0, jnp.zeros_like(row)
        for i, n in enumerate(z.groups):
            group = jnp.where(row >= first, i, group)
            first += n
        r["vec"][...] = dot(jnp.where(group == p, 1.0, 0.0).astype(BF), total.astype(BF))

    vgo, vgm, vgc, vgA = (r[n] for n in ("vgo", "vgm", "vgc", "vgA"))

    def sums_start():
        big = r["big"]
        first = 0
        for p, n in enumerate(z.groups):
            big[first:first + n, :] = jnp.broadcast_to(gvl[p:p + 1, :], (n, z.VW))
            first += n
        ones = spread(F32)
        for m, mine, out in ((mpi, True, vgo), (y * 2 + 1 - c, False, vgm)):
            rows = jnp.where(heads_mask(m, mine, z.NR), big[...], 0.0)
            got = lax.dot_general(
                ones, rows, (((1,), (1,)), ((), ())),
                precision=lax.Precision.HIGHEST, preferred_element_type=F32,
            )
            out[...] = jnp.zeros_like(out)
            out[:, :, 0:z.NR] = got.reshape(z.dp, 8, z.NR)
        send(rcopy(vgm, vgc, z.vec_ids[1][1], mate))

    def sums_cross():
        rcopy(vgc, vgc, z.vec_ids[1][1], mate).wait_recv()
        vgo[...] = vgo[...] + vgc[...]
        for d in range(1, z.dp):
            src = vgo.at[lax.rem(dpi + d, z.dp)]
            send(rcopy(src, vgA.at[d], z.vec_ids[1][0] + d, dp_dev(d)))

    def sums_done():
        total = vgo[dpi]
        for d in range(1, z.dp):
            dst = vgA.at[d]
            rcopy(dst, dst, z.vec_ids[1][0] + d, mate).wait_recv()
            total = total + vgA[d]
        prm[...] = jnp.concatenate([total, jnp.zeros((120, 128), F32)], axis=0).T
        first = 0
        for p in range(6):
            r["qd"][p] = prm[first:first + z.groups[p], 0:z.wide]
            first += z.groups[p]
        r["qu"][...] = prm[first:first + z.groups[6], :].T[0:z.wide]
        first += z.groups[6]
        half = z.groups[7] // 2
        for t in range(2):
            r["qi"][t] = prm[first + t * half:first + (t + 1) * half, 0:z.wide]

    def vector(row, cols=slice(None)):
        return r["vec"][row:row + 1, cols]

    tokF, feedF, na, n2 = r["tokF"], r["feedF"], r["na"], r["n2"]

    def stats(x):
        mu = jnp.sum(x, axis=1, keepdims=True) * (1.0 / D)
        sq = jnp.sum(x * x, axis=1, keepdims=True) * (1.0 / D)
        return mu, lax.rsqrt(sq - mu * mu + EPS)

    def norm_one(s, out):
        gain, shift = vector(0, slice(0, D)), vector(1, slice(0, D))

        def step(i):
            rr = rows16(s * R + i * 32, 32)
            x = tokF[rr, :].astype(F32)
            mu, inv = stats(x)
            out[rr, :D] = ((x - mu) * inv * gain + shift).astype(BF)
        loop(R // 32, step, True)

    ticks, waiting, flying, finished = [], [], [], []

    def tick():
        if ticks and (ticks[0][0] is None or ticks[0][0] in flying):
            for f in ticks.pop(0)[1]:
                f()

    q, k, v, att, lse = r["q"], r["k"], r["v"], r["att"], r["lse"]

    def project(s):
        rr = slice(s * R, s * R + R)
        x = na[rr, :D]
        for third, ref in enumerate((q, k, v)):
            for j in range(0, HW, 256):
                w = min(256, HW - j)
                col = third * HW + j
                out = dot(x, W[0][:, col:col + w])
                if third == 0:
                    out = out + r["vec"][7:8, j:j + w]
                if third == 2:
                    out = out + r["vec"][7:8, HW + j:HW + j + w]
                out = out.astype(BF)
                if third == 0:
                    out = out * BF(HD ** -0.5)
                ref[rr, j:j + w] = out

    chunks = [(i, min(256, R - i)) for i in range(0, R, 256)]
    top = z.SEQ // 16 * 16

    def half_mask(x, e):
        lane = lax.broadcasted_iota(jnp.int32, x.shape, 1)
        return jnp.where((lane < HD) if e == 0 else (lane >= HD), x, jnp.zeros_like(x))

    def mask_keys(scores):
        last = scores[top:]
        row = lax.broadcasted_iota(jnp.int32, last.shape, 0)
        return jnp.concatenate([scores[:top], jnp.where(row < z.SEQ - top, last, -1e30)], axis=0)

    def attend(s, pr):
        cc = lanes(pr * 128, 128)
        rr = slice(s * R, s * R + R)
        kp = k[rr, cc]
        vt = v[rr, cc].T
        for (c0, cw) in chunks:
            qp = q[s * R + c0:s * R + c0 + cw, cc]
            parts = []
            for e in range(2):
                sc = mask_keys(dot_nt(kp, half_mask(qp, e)))
                mx = jnp.max(sc, axis=0, keepdims=True)
                ex = jnp.exp(sc - mx)
                tot = jnp.sum(ex, axis=0, keepdims=True)
                soft = (ex * (1.0 / tot)).astype(BF)
                parts.append(dot(vt[e * HD:(e + 1) * HD], soft))
                lse[(s * z.NP + pr) * 2 + e, :, c0:c0 + cw] = mx + jnp.log(tot)
            out = jnp.concatenate(parts, axis=0)
            att[s * R + c0:s * R + c0 + cw, cc] = out.T.astype(BF)

    csend, ysend, ubuf = r["csend"], r["ysend"], r["ubuf"]
    busy = {}
    held = []

    def let_go():
        while held:
            held.pop(0)()

    def free(key):
        for copy in busy.pop(key, []):
            copy.wait_send()

    def own(s):
        return rows16(s * R + c * HR, HR)

    def theirs(s):
        return rows16(s * R + (1 - c) * HR, HR)

    def core_part(s, name, x, w, dst, keep, key):
        free(("c", s))
        free((key, s))
        rows_x = x[s * R:s * R + R, :]

        def step(j):
            cols = lanes(j * 256, 256)
            ubuf[...] = dot_nt(rows_x, w[pl.ds(pl.multiple_of(j * 256, 256), 256), :])
            csend[s, :, cols] = ubuf[rows16((1 - c) * HR, HR), :].astype(BF)
            keep[s, :, cols] = ubuf[rows16(c * HR, HR), :].astype(BF)
        loop(D // 256, step)
        copy = rcopy(csend.at[s], dst.at[s], z.slot_core[name][s], mate)
        busy[("c", s)] = [send(copy, late=False)]

    def core_wait(s, name, dst):
        rcopy(dst.at[s], dst.at[s], z.slot_core[name][s], mate).wait_recv()

    def chip_part(s, name, got, dst, hold=False):
        core_wait(s, name, got)
        ysend[s] = (ysend[s].astype(F32) + got[s].astype(F32)).astype(BF)
        copies = [
            rcopy(ysend.at[s], dst.at[s, dy - 1], z.slot_y[name][s] + dy - 1, y_dev(dy)) for dy in range(1, Y)
        ]
        start_all(("y", s), copies, hold)

    def start_all(key, copies, hold):
        busy[key] = copies

        def go():
            for copy in copies:
                copy.start()
        if hold:
            held.append(go)
        else:
            go()

    def chip_share(s, name, got, dst, buf, key, hold=False):
        core_wait(s, name, got)
        buf[s] = (buf[s].astype(F32) + got[s].astype(F32)).astype(BF)
        copies = [
            rcopy(
                buf.at[s, :, lanes(lax.rem(y + dy, Y) * Dy, Dy)], dst.at[s, dy - 1],
                z.slot_y[name][s] + dy - 1, y_dev(dy),
            )
            for dy in range(1, Y)
        ]
        start_all((key, s), copies, hold)

    def y_wait(s, name, dst):
        for dy in range(1, Y):
            got = dst.at[s, dy - 1]
            rcopy(got, got, z.slot_y[name][s] + dy - 1, mate).wait_recv()

    def own_share(s, buf, dst):
        total = buf[s, :, lanes(y * Dy, Dy)].astype(F32)
        for dy in range(1, Y):
            total = total + dst[s, dy - 1].astype(F32)
        return total

    hid = r["hid"]
    cr1, cr2, cr3, yr1, yr2, yr3, yrO = (r[n] for n in ("cr1", "cr2", "cr3", "yr1", "yr2", "yr3", "yrO"))

    def norm_two(s):
        y_wait(s, "branch", yr1)
        gain, shift, bias = vector(3, slice(0, D)), vector(4, slice(0, D)), vector(2, slice(0, D))

        def step(i):
            lr = rows16(i * 16, 16)
            h = ysend[s, lr, :].astype(F32)
            for dy in range(Y - 1):
                h = h + yr1[s, dy, lr, :].astype(F32)
            gr = rows16(s * R + c * HR + i * 16, 16)
            h = tokF[gr, :].astype(F32) + (h + bias)
            hid[rows16(s * HR + i * 16, 16), :] = h
            mu, inv = stats(h)
            n2[gr, :] = ((h - mu) * inv * gain + shift).astype(BF)
        loop(HR // 16, step, True)
        part = n2.at[own(s)]
        busy[("n", s)] = [send(rcopy(part, part, z.slot_core["n2"][s], mate), late=False)]
        yc = lanes(y * Dy, Dy)
        ebuf[s] = hid[s * HR:s * HR + HR, yc] + r["vec"][5:6, yc]

    gp = r["gp"]
    UC = min(256, F)
    root = 0.5 ** 0.5
    dens = (2.0 * 3.141592653589793) ** -0.5

    def up(s):
        part = n2.at[theirs(s)]
        rcopy(part, part, z.slot_core["n2"][s], mate).wait_recv()
        x = n2[s * R:s * R + R, :]

        def column(j):
            cols = lanes(j * UC, UC)
            ubuf[...] = dot(x, W[2][:, cols]) + r["vec"][6:7, cols]

            def step(i):
                lr = rows16(i * 32, 32)
                gr = rows16(s * R + i * 32, 32)
                u = ubuf[lr, :]
                phi = 0.5 * lax.erf(u * root) + 0.5
                na[gr, cols] = (u * phi).astype(BF)
                gp[gr, cols] = (phi + u * (jnp.exp(-0.5 * u * u) * dens)).astype(BF)
            loop(R // 32, step)
        loop(F // UC, column)

    def back_up(s):
        x = feedF[s * R:s * R + R, :]

        def column(j):
            cols = lanes(j * 256, 256)
            ga = dot(x, W[3][:, cols])
            gp[s * R:s * R + R, cols] = (ga * gp[s * R:s * R + R, cols].astype(F32)).astype(BF)
        loop(F // 256, column)

    obuf, ebuf, ig = r["obuf"], r["ebuf"], r["igP"]

    def layer_out(s):
        y_wait(s, "out", yrO)
        total = own_share(s, r["ysO"], yrO)
        keep = r["flags"][s].astype(F32)
        obuf[s] = ((total + ebuf[s]) * keep).astype(BF)
        r["lo"][own(s), :] = obuf[s, :, lanes(c * Dm, Dm)]
        send(rcopy(
            obuf.at[s, :, lanes((1 - c) * Dm, Dm)], r["lo"].at[own(s)], z.slot_core["lo"][s], mate
        ))

    def put_half(which, write):
        for half in range(2):
            size = min(HR, z.SEQ - half * HR)
            rows = slice(half * HR, half * HR + size)
            pl.when(which == half)(functools.partial(write, rows, size))

    def swap_out(s, buf, got, name):
        send(rcopy(buf.at[s, :, lanes((1 - c) * Dm, Dm)], got.at[s], z.slot_core[name][s], mate))

    def take_out(s, got, name):
        dst = got.at[s]
        rcopy(dst, dst, z.slot_core[name][s], mate).wait_recv()

    def put_grad(s, which, buf, cols):
        def write(rows, size):
            r["ig"][rows, s, :] = buf[s, 0:size, cols]
        put_half(which, write)

    na_act = na.at[:, 0:F]
    gb, gatt, gj, acc, gvl = r["gb"], r["gatt"], r["gj"], r["acc"], r["gvl"]

    def norm_two_back(s):
        y_wait(s, "gn2", yr2)
        let_go()
        gain = vector(3, slice(0, D))

        def step(i, sums):
            lr = rows16(i * 16, 16)
            e = ysend[s, lr, :].astype(F32)
            for dy in range(Y - 1):
                e = e + yr2[s, dy, lr, :].astype(F32)
            hr = rows16(s * HR + i * 16, 16)
            gr = rows16(s * R + c * HR + i * 16, 16)
            h = hid[hr, :]
            mu, inv = stats(h)
            xhat = (h - mu) * inv
            t = e * gain
            m1 = jnp.sum(t, axis=1, keepdims=True) * (1.0 / D)
            m2 = jnp.sum(t * xhat, axis=1, keepdims=True) * (1.0 / D)
            g = feedF[gr, :].astype(F32) + inv * (t - m1 - xhat * m2)
            hid[hr, :] = g
            g = g.astype(BF)
            gb[gr, :] = g
            g = g.astype(F32)
            ex = e * xhat
            fold = lambda m: m[0:8] + m[8:16]
            return (sums[0] + fold(ex), sums[1] + fold(e), sums[2] + fold(g))
        zero = jnp.zeros((8, D), F32)
        sums = lax.fori_loop(0, HR // 16, step, (zero, zero, zero), unroll=True)
        for i in range(3):
            acc[i] = sums[i] if s == 0 else acc[i] + sums[i]
        part = gb.at[own(s)]
        send(rcopy(part, part, z.slot_core["gb"][s], mate))

    def attend_back_start(s):
        part = gb.at[theirs(s)]
        rcopy(part, part, z.slot_core["gb"][s], mate).wait_recv()
        gatt[...] = dot(gb[s * R:s * R + R, :], W[1][...]).astype(BF)

    def attend_back(s, pr):
        cc = lanes(pr * 128, 128)
        rr = slice(s * R, s * R + R)
        kp = k[rr, cc]
        vp = v[rr, cc]
        kt = kp.T
        dk = jnp.zeros((R, 128), F32)
        dv = jnp.zeros((R, 128), F32)
        for (c0, cw) in chunks:
            qp = q[s * R + c0:s * R + c0 + cw, cc]
            go = gatt[c0:c0 + cw, cc]
            parts = []
            for e in range(2):
                qm, gm = half_mask(qp, e), half_mask(go, e)
                sc = mask_keys(dot_nt(kp, qm))
                soft = jnp.exp(sc - lse[(s * z.NP + pr) * 2 + e, :, c0:c0 + cw])
                dv = dv + dot(soft.astype(BF), gm)
                gs = dot_nt(vp, gm)
                delta = jnp.sum(gs * soft, axis=0, keepdims=True)
                ds = (soft * (gs - delta)).astype(BF)
                dk = dk + dot(ds, qm)
                parts.append(dot(kt[e * HD:(e + 1) * HD], ds))
            dq = jnp.concatenate(parts, axis=0) * (HD ** -0.5)
            gj[s * R + c0:s * R + c0 + cw, lanes(pr * 128, 128)] = dq.T.astype(BF)
        gj[rr, lanes(HW + pr * 128, 128)] = dk.astype(BF)
        gj[rr, lanes(2 * HW + pr * 128, 128)] = dv.astype(BF)

    stat, statT, statR = r["stat"], r["statT"], r["statR"]

    def norm_one_sums(s):
        y_wait(s, "gn1", yr3)
        ebuf[s] = own_share(s, ysend, yr3)
        yc = lanes(y * Dy, Dy)
        gain = vector(0, yc)

        def step(i, sums):
            lr = rows16(i * 16, 16)
            gr = rows16(s * R + c * HR + i * 16, 16)
            mu, inv = stats(tokF[gr, :].astype(F32))
            xhat = (tokF[gr, yc].astype(F32) - mu) * inv
            e = ebuf[s, lr, :]
            t = e * gain
            s1 = jnp.sum(t, axis=1, keepdims=True)
            s2 = jnp.sum(t * xhat, axis=1, keepdims=True)
            lane = lax.broadcasted_iota(jnp.int32, (16, 128), 1)
            stat[lr, :] = jnp.where(lane == 0, s1, jnp.where(lane == 1, s2, 0.0))
            ex = e * xhat
            fold = lambda m: m[0:8] + m[8:16]
            return (sums[0] + fold(ex), sums[1] + fold(e))
        zero = jnp.zeros((8, Dy), F32)
        sums = lax.fori_loop(0, HR // 16, step, (zero, zero), unroll=True)
        for i in range(2):
            row = jnp.sum(sums[i], axis=0, keepdims=True)
            gvl[i:i + 1, yc] = row if s == 0 else gvl[i:i + 1, yc] + row
        statT[s] = stat[...].T[0:8]
        for dy in range(1, Y):
            send(rcopy(statT.at[s], statR.at[s, dy - 1], z.slot_y["st"][s] + dy - 1, y_dev(dy)))

    def norm_one_back(s):
        y_wait(s, "st", statR)
        total = statT[s]
        for dy in range(Y - 1):
            total = total + statR[s, dy]
        total = jnp.concatenate([total, jnp.zeros((120, HR), F32)], axis=0)
        stat[...] = total.T * (1.0 / D)
        yc = lanes(y * Dy, Dy)
        gain = vector(0, yc)

        def step(i):
            lr = rows16(i * 16, 16)
            gr = rows16(s * R + c * HR + i * 16, 16)
            mu, inv = stats(tokF[gr, :].astype(F32))
            xhat = (tokF[gr, yc].astype(F32) - mu) * inv
            t = ebuf[s, lr, :] * gain
            st = stat[lr, :]
            m1, m2 = st[:, 0:1], st[:, 1:2]
            g = hid[rows16(s * HR + i * 16, 16), yc]
            ebuf[s, lr, :] = g + inv * (t - m1 - xhat * m2)
        loop(HR // 16, step, True)
        swap_out(s, ebuf, ig, "ig")
        put_grad(s, c, ebuf, lanes(c * Dm, Dm))

    G = [r["G3"].at[:, 0:3 * HW], r["G1"], r["G2"], r["G3"]]
    RX = [r[f"RX{p}"] for p in range(4)]
    Z = [r[f"Z{p}"] for p in range(4)]
    outs = [r[f"o{p}"] for p in range(4)]

    def weight_grad(p, x, g, s=None):
        rows = slice(None) if s is None else slice(s * R, s * R + R)

        def step(i):
            rr = pl.ds(pl.multiple_of(i * 256, 256), 256)
            part = dot_tn(x[rows, lanes(i * 256, 256)], g[rows, :])
            if s:
                part = part + G[p][rr, :].astype(F32)
            G[p][rr, :] = part.astype(BF)
        loop(D // 256, step)

    def gblock(p, blk):
        return rows16(blk * RB, RB)

    def rs_send(p, copy):
        busy.setdefault(("g", p), []).append(send(copy, late=False))

    def rs_cross(i):
        p, first, width = z.scatters[i]
        cols = pl.ds(first, width)
        for db in range(1, B):
            bd = lax.rem(b + db, B)
            for aa in range(A):
                rs_send(p, rcopy(
                    G[p].at[gblock(p, aa * B + bd), cols], RX[p].at[db - 1, aa, :, cols],
                    z.rs_x[i] + (db - 1) * A + aa, b_dev(db),
                ))

    def pump():
        while waiting and len(flying) < 2:
            flying.append(waiting.pop(0))
            rs_cross(flying[-1])

    def rs_add(i):
        p, first, width = z.scatters[i]
        cols = pl.ds(first, width)
        for db in range(1, B):
            for aa in range(A):
                dst = RX[p].at[db - 1, aa, :, cols]
                rcopy(dst, dst, z.rs_x[i] + (db - 1) * A + aa, mate).wait_recv()
        flying.remove(i)
        pump()
        if B > 1:
            def step(aa):
                rr = gblock(p, aa * B + b)
                total = G[p][rr, cols].astype(F32)
                for db in range(B - 1):
                    total = total + RX[p][db, aa, :, cols].astype(F32)
                G[p][rr, cols] = total.astype(BF)
            loop(A, step)

        for da in range(1, A):
            rr = gblock(p, lax.rem(a + da, A) * B + b)
            rs_send(p, rcopy(G[p].at[rr, cols], Z[p].at[da - 1, :, cols], z.rs_z[i] + da, a_dev(da)))

    def rs_done(i):
        p, first, width = z.scatters[i]
        finished.append(i)
        cols = pl.ds(first, width)
        total = G[p][gblock(p, dpi), cols].astype(F32)
        for da in range(1, A):
            dst = Z[p].at[da - 1, :, cols]
            rcopy(dst, dst, z.rs_z[i] + da, mate).wait_recv()
            total = total + Z[p][da - 1, :, cols].astype(F32)
        if p == 0:
            for t in range(first // HW, (first + width - 1) // HW + 1):
                low, high = max(first, t * HW), min(first + width, (t + 1) * HW)
                outs[0][t, :, low - t * HW:high - t * HW] = total[:, low - first:high - first]
        elif p in (1, 3):
            outs[p][cols, :] = total.T
        else:
            outs[p][:, cols] = total

    def rs_groups():
        count = len(z.scatters)
        groups = []
        for i in range(count):
            group = [functools.partial(rs_add, i)]
            if i >= 2:
                group.append(functools.partial(rs_done, i - 2))
            groups.append((i, group))
        return groups + [(None, [functools.partial(rs_done, i)]) for i in range(max(count - 2, 0), count)]

    def cross_part(part):
        waiting.extend(i for i, piece in enumerate(z.scatters) if piece[0] == part)
        pump()

    first_pieces, second = of_part(0), of_part(1)
    order = first_pieces + second + of_part(2) + of_part(3)
    begun = []

    def ag_next():
        if len(begun) < len(order):
            ag_start(order[len(begun)])
            begun.append(1)

    small_in()
    small_send(0)
    place_weights(0)
    ag_next()
    ag_next()
    place_rows(0)
    small_take(0)
    small_send(1)
    rows_start(0)
    for p in range(1, 4):
        place_weights(p)
    for t in range(1, 2 * NS):
        place_rows(t)
    ag_near(order[0])
    ag_next()
    small_take(1)
    small_spread()
    ag_near(order[1])
    ag_next()
    ag_far(order[0])
    rows_relay(0)
    for t in range(1, NS):
        rows_start(t)
    ag_near(order[2])
    ag_next()
    ag_far(order[1])
    rows_done(0)
    norm_one(0, na)
    ag_near(order[3])
    ag_next()
    ag_far(order[2])
    for t in range(1, NS):
        rows_relay(t)
    for t in range(NS, 2 * NS):
        rows_start(t)
    ag_far(order[3])
    for i in first_pieces:
        ag_done(i)
    for i in order[4:]:
        ticks += [(None, [functools.partial(ag_near, i), ag_next]), (None, [functools.partial(ag_far, i)])]
    for s in range(NS):
        if s > 0:
            rows_done(s)
            norm_one(s, na)
        project(s)
        tick()
        for pr in range(z.NP):
            attend(s, pr)
            if s == 0 or pr == 0:
                tick()
        if s == 0:
            for i in second:
                ag_done(i)
        core_part(s, "branch", att, W[1], cr1, ysend, "y")
        if s == 0:
            tick()
        chip_part(s, "branch", cr1, yr1)
    while ticks:
        tick()
    for t in range(NS, 2 * NS):
        rows_relay(t)
    for s in range(NS):
        norm_two(s)
        if s == 0:
            for i in of_part(2):
                ag_done(i)
            for t in range(NS, 2 * NS):
                rows_done(t)
        up(s)
        weight_grad(3, feedF, na_act, s)
    cross_part(3)
    for i in of_part(3):
        ag_done(i)
    for s in range(NS):
        back_up(s)
        if s > 0:
            chip_part(s - 1, "gn2", cr2, yr2)
        core_part(s, "gn2", gp, W[2], cr2, ysend, "y")
    chip_part(NS - 1, "gn2", cr2, yr2, True)
    ticks += rs_groups()
    weight_grad(2, n2, gp)
    cross_part(2)
    tick()
    gvl[...] = jnp.zeros_like(gvl)
    ones_row = jnp.ones((8, z.ROWS), BF)
    gvl[5:6, lanes(mpi * Dm, Dm)] = dot(ones_row, feedF[:, lanes(mpi * Dm, Dm)])[0:1]
    gvl[6:7, 0:F] = dot(ones_row, gp[...])[0:1]
    for s in range(NS):
        core_part(s, "out", na_act, W[3], cr1, r["ysO"], "o")
    tick()
    for s in range(NS):
        free(("n", s))
        norm_one(s, n2)
    for s in range(NS):
        norm_two_back(s)
        if s == NS - 1:
            for t in range(NS):
                chip_share(t, "out", cr1, yrO, r["ysO"], "o")
        tick()
        attend_back_start(s)
        if s == NS - 1:
            weight_grad(1, gb, att)
            cross_part(1)
        for pr in range(z.NP):
            attend_back(s, pr)
            tick()
        core_part(s, "gn1", gj, W[0], cr3, ysend, "y")
        if s == NS - 1:
            while any(piece[0] == 3 and i not in finished for i, piece in enumerate(z.scatters)):
                tick()
            free(("g", 3))
            weight_grad(0, n2, gj)
        if s < NS - 1:
            chip_share(s, "gn1", cr3, yr3, ysend, "y", True)
    cross_part(0)
    chip_share(NS - 1, "gn1", cr3, yr3, ysend, "y")
    tick()
    for s in range(NS):
        layer_out(s)
    tick()
    gvl[7:8, 0:HW] = dot(ones_row, gj[:, 0:HW])[0:1]
    gvl[7:8, HW:2 * HW] = dot(ones_row, gj[:, 2 * HW:3 * HW])[0:1]
    yc = lanes(y * Dy, Dy)
    for row, i in ((3, 0), (4, 1), (2, 2)):
        gvl[row:row + 1, yc] = jnp.sum(acc[i, :, yc], axis=0, keepdims=True)
    for s in range(NS):
        norm_one_sums(s)
        if s == 0:
            for t in range(NS):
                dst = r["lo"].at[theirs(t)]
                rcopy(dst, dst, z.slot_core["lo"][t], mate).wait_recv()
        tick()
    sums_start()
    for s in range(NS):
        norm_one_back(s)
        if s == 0:
            sums_cross()
        tick()
    sums_done()
    while ticks:
        tick()
    for s in range(NS):
        take_out(s, ig, "ig")
        put_grad(s, 1 - c, ig, slice(None))
    for key in list(busy):
        free(key)
    for cond, copy in pending:
        when(cond, lambda copy=copy: copy.wait_send())


def body(mesh, tokens, slot_flags, cotangent, attend_gain, attend_shift, input_weight, input_bias,
         output_weight, output_bias, dense_gain, dense_shift, up_weight, up_bias, down_weight, down_bias):
    tokens, cotangent = tokens.transpose(1, 0, 2), cotangent.transpose(1, 0, 2)
    z = Sizes(mesh, tokens, input_weight, up_weight)
    small = (attend_gain, attend_shift, output_bias, dense_gain, dense_shift, down_bias, up_bias.T, input_bias)
    shapes = [
        jax.ShapeDtypeStruct((z.ROWS, z.Dm), BF),
        jax.ShapeDtypeStruct(tokens.shape, F32),
        jax.ShapeDtypeStruct((3, z.RB, z.HW), F32),
        jax.ShapeDtypeStruct(output_weight.shape, F32),
        jax.ShapeDtypeStruct(up_weight.shape, F32),
        jax.ShapeDtypeStruct(down_weight.shape, F32),
        jax.ShapeDtypeStruct((6,) + attend_gain.shape, F32),
    ] + [jax.ShapeDtypeStruct(x.shape, F32) for x in small[6:]]
    vmem = pl.BlockSpec(memory_space=pltpu.VMEM)
    smem = pl.BlockSpec(memory_space=pltpu.SMEM)
    lo, ig, g0, g1, g2, g3, gd, gu, gi = pl.pallas_call(
        functools.partial(kernel, z),
        out_shape=shapes,
        in_specs=[vmem, vmem, smem] + [vmem] * 12,
        out_specs=[vmem] * 9,
        scratch_shapes=scratch_shapes(z),
        compiler_params=pltpu.CompilerParams(
            collective_id=0, has_side_effects=True, vmem_limit_bytes=VMEM_LIMIT
        ),
        name="layer",
    )(
        tokens, cotangent, slot_flags, input_weight.transpose(1, 0, 2), output_weight, up_weight, down_weight,
        *small,
    )
    layer_rows = lo.reshape(z.NS, z.R, z.Dm)[:, :z.SEQ]
    input_grad = ig.transpose(1, 0, 2)
    return (
        layer_rows, input_grad, gd[0], gd[1], g0.transpose(1, 0, 2), gi, g1, gd[2], gd[3], gd[4],
        g2, gu.T, g3, gd[5],
    )


VMEM_LIMIT = 63 * 2**20


def solution(mesh):
    rows = P("dp", None, "mp")
    vec = P("mp", "dp")
    pair = P(None, "mp", "dp")
    return jax.shard_map(
        functools.partial(body, mesh),
        mesh=mesh,
        in_specs=(rows, P("dp"), rows, vec, vec, rows, pair, vec, vec, vec, vec, P("dp", "mp"), vec, vec, vec),
        out_specs=(rows, rows, vec, vec, rows, pair, vec, vec, vec, vec, P("dp", "mp"), vec, vec, vec),
        check_vma=False,
    )
```
